128 devices in a mesh: dp: 8 (over z, x_lo), section: 4 (over y), mp: 4 (over x_hi, core).
Axes of the slice: x: 4 (x_hi: 2, x_lo: 2; x = x_hi * 2 + x_lo), y: 4, z: 4, core: 2. Of those that a mesh axis runs over, the one named last changes fastest.
Arguments:
- block_input: bfloat16 [32, 256, 1280], P(('dp', 'section')), may hold values from -6 to 6
- windows: int32 [32, 64], P(('dp', 'section')), may hold values from 0 to 3, never falling along the last dimension, each value on 1 to 32 neighbouring positions
- cell_rows: int32 [4, 2048], P('section', 'dp'), may hold values from -1 to 511, as said below
- text_vectors: bfloat16 [4, 2048, 8192], P('section', 'dp', 'mp'), may hold values from -6 to 6
- sequence_cotangent: bfloat16 [4, 2048, 8192], P('section', 'dp', 'mp'), may hold values from -2.5 to 2.5
- norm_gains: float32 [2, 1280], replicated, may hold values from 0.1 to 1.9
- merge_gain: float32 [1280], replicated, may hold values from 0.1 to 1.9
- triple_weight: bfloat16 [1280, 3, 1280], P('section', None, 'mp'), may hold values from -0.15625 to 0.15625
- output_weight: bfloat16 [1280, 1280], P('section', 'mp'), may hold values from -0.15625 to 0.15625
- gate_up_weight: bfloat16 [1280, 2, 3420], P('section', None, 'mp'), may hold values from -0.15625 to 0.15625
- down_weight: bfloat16 [1280, 3420], P('section', 'mp'), may hold values from -0.109375 to 0.109375
- merge_up: bfloat16 [5120, 5120], P(None, ('section', 'mp')), may hold values from -0.078125 to 0.078125
- merge_down: bfloat16 [5120, 8192], P(('section', 'mp')), may hold values from -0.078125 to 0.078125
Outputs:
- sequence: bfloat16 [4, 2048, 8192], P('section', 'dp', 'mp')
- input_gradient: float32 [32, 256, 1280], P(('dp', 'section'))
- triple_gradient: float32 [1280, 3, 1280], P('section', None, 'mp')
- output_gradient: float32 [1280, 1280], P('section', 'mp')
- gate_up_gradient: float32 [1280, 2, 3420], P('section', None, 'mp')
- down_gradient: float32 [1280, 3420], P('section', 'mp')
- gain_gradient: float32 [2, 1280], replicated
The draws below stay inside these ranges and needn't reach their ends.
Inputs may be any that keep to these rules, and one draw needn't show every extreme that they name: `cell_rows`: in sequence s the rows that are not -1 hold each index d * 64 + c (cell c of pack d * 4 + s) exactly once, rising along the rows; the rows d * 256 to (d + 1) * 256 - 1 hold only indices from d * 64 to (d + 2) * 64 - 1.
All inputs are finite; a program needn't handle non-finite values.
Results may differ from the reference program's by a relative error of at most 0.034.
Values may be sent and summed in bfloat16 or wider, within the bound.
A program may use at most 128 MiB of HBM per device.

```python
import math
import jax
import jax.numpy as jnp
import numpy as np
from jax import lax

D = 1280
FF = 3420
E = 8192
HEAD_DIM = 80
MERGE = 5120
PATCH_DEV = 256
IMAGES = 4
CELLS = 64
IMAGE_CELLS = 32
TEXT_DEV = 256
PACKS = 32
SEQS = 4
LEN = 2048
N_DP = 8


def draw_cell_rows(key, part):
    key = jax.random.fold_in(key, 7)
    first, second = jax.random.split(key)
    shards = LEN // TEXT_DEV
    spill = jax.random.randint(first, (SEQS, shards), 0, CELLS)
    keep = (jnp.arange(shards) < shards - 1).astype(jnp.int32)
    spill = spill * keep[None, :]
    before = jnp.concatenate([jnp.zeros((SEQS, 1), jnp.int32), spill[:, :-1]], axis=1)
    counts = CELLS + spill - before
    starts = jnp.arange(shards, dtype=jnp.int32)[None, :] * CELLS + before
    scores = jax.random.randint(second, (SEQS, shards, TEXT_DEV), 0, 1 << 20) * TEXT_DEV + jnp.arange(TEXT_DEV, dtype=jnp.int32)
    ranks = jnp.argsort(jnp.argsort(scores, axis=-1), axis=-1)
    chosen = ranks < counts[:, :, None]
    order = jnp.cumsum(chosen.astype(jnp.int32), axis=-1) - 1
    values = jnp.where(chosen, starts[:, :, None] + order, -1)
    return values.reshape(SEQS, LEN).astype(jnp.int32)


def level_of(own_key, extent, pieces, smallest, largest):
    level, own = 1.0, jax.random.fold_in(own_key, 6)
    for axis_at, parts in pieces:
        draws = jnp.exp(jax.random.uniform(jax.random.fold_in(own, axis_at), (parts,), jnp.float32, smallest / len(pieces), largest / len(pieces)))
        level = level * jnp.repeat(draws, extent[axis_at] // parts).reshape([-1 if axis == axis_at else 1 for axis in range(len(extent))])
    return level


def length_profile(count, total, reach, slope):
    portions = [(1 << 20) // math.isqrt(standing ** slope) + 1 for standing in range(2, count + 1)]
    spare, holding = total - reach - (count - 1), [1] * (count - 1)
    while spare > 0:
        candidates = [i for i in range(count - 1) if holding[i] < reach]
        mass, remaining = sum([portions[i] for i in candidates]), spare
        for i in candidates:
            extra = min(reach - holding[i], max(1, remaining * portions[i] // mass), spare)
            holding[i] = holding[i] + extra
            spare = spare - extra
    return np.array([reach] + holding)


def uneven(key, amount, total, reach, skew):
    if amount == 2:
        one = jax.random.randint(key, (), max(1, total - reach), min(reach, total - 1) + 1)
        return jnp.stack([one, total - one])
    sizes = jnp.asarray(length_profile(amount, total, reach, skew), jnp.int32)
    pairs = (amount - 1) // 2
    donor, sink = sizes[1:1 + 2 * pairs:2], sizes[2:2 + 2 * pairs:2]
    slack = jnp.minimum(donor - 1, reach - sink)
    shifted = jax.random.randint(jax.random.fold_in(key, 1), (pairs,), 0, 1 << 20) % (slack + 1)
    sizes = sizes.at[1:1 + 2 * pairs:2].set(donor - shifted).at[2:2 + 2 * pairs:2].set(sink + shifted)
    return sizes[jax.random.permutation(jax.random.fold_in(key, 2), amount)]


def normal_values(rng, dims, scale, reach, cuts=(), kind=jnp.bfloat16):
    loudness = level_of(rng, dims, cuts, -0.22, 0.18) if cuts else 1.0
    array = jax.random.normal(rng, dims, jnp.float32) * scale * loudness
    return jnp.minimum(jnp.maximum(array, -reach), reach).astype(kind)


def setup_inputs(seed: int = 0) -> dict:
    arg_keys = jax.random.split(jax.random.key(seed), 14)
    return {
        "block_input": normal_values(arg_keys[0], (PACKS, PATCH_DEV, D), 1.0, 6.0, ((0, 32),)),
        "windows": jax.vmap(lambda own: jnp.searchsorted(jnp.cumsum(uneven(own, IMAGES, CELLS, IMAGE_CELLS, 0)), jnp.arange(CELLS), side="right"))(jax.random.split(arg_keys[1], PACKS)).reshape((PACKS, CELLS)).astype(jnp.int32),
        "cell_rows": draw_cell_rows(jax.random.fold_in(arg_keys[13], 71), 0),
        "text_vectors": normal_values(arg_keys[3], (SEQS, LEN, E), 1.0, 6.0, ((0, 4), (1, 8), (2, 4))),
        "sequence_cotangent": normal_values(arg_keys[4], (SEQS, LEN, E), 0.25, 2.5, ((0, 4), (1, 8), (2, 4))),
        "norm_gains": jnp.clip(1.0 + 0.18 * jax.random.normal(arg_keys[5], (2, D), jnp.float32), 0.1, 1.9),
        "merge_gain": jnp.clip(1.0 + 0.18 * jax.random.normal(arg_keys[6], (D,), jnp.float32), 0.1, 1.9),
        "triple_weight": normal_values(arg_keys[7], (D, 3, D), D ** -0.5, 0.15625, ((0, 4), (2, 4))),
        "output_weight": normal_values(arg_keys[8], (D, D), D ** -0.5, 0.15625, ((0, 4), (1, 4))),
        "gate_up_weight": normal_values(arg_keys[9], (D, 2, FF), D ** -0.5, 0.15625, ((0, 4), (2, 4))),
        "down_weight": normal_values(arg_keys[10], (D, FF), FF ** -0.5, 0.109375, ((0, 4), (1, 4))),
        "merge_up": normal_values(arg_keys[11], (MERGE, MERGE), MERGE ** -0.5, 0.078125, ((1, 16),)),
        "merge_down": normal_values(arg_keys[12], (MERGE, E), MERGE ** -0.5, 0.078125, ((0, 16),)),
    }


epsilon = 1e-06
root_half = 0.7071067811865476
density_scale = 0.3989422804014327

def root_scale(values):
    return lax.rsqrt(lax.optimization_barrier(jnp.mean(values * values, axis=-1, keepdims=True)) + epsilon)

def norm_backward(cotangent, values, scale, gain):
    weighted = cotangent * gain
    return scale * weighted - values * scale ** 3 * lax.optimization_barrier(jnp.mean(weighted * values, axis=-1, keepdims=True))

def gelu_value(values):
    return 0.5 * values * (1.0 + jax.scipy.special.erf(values * root_half))

def gelu_slope(values):
    return 0.5 * (1.0 + jax.scipy.special.erf(values * root_half)) + values * jnp.exp(-0.5 * values * values) * density_scale

def product(left, right):
    return jnp.dot(left, right, preferred_element_type=jnp.float32)

def contract_last(left, right):
    return lax.dot_general(left, right, (((1,), (1,)), ((), ())), preferred_element_type=jnp.float32)

def contract_first(left, right):
    return lax.dot_general(left, right, (((0,), (0,)), ((), ())), preferred_element_type=jnp.float32)

def widen(values):
    return values.astype(jnp.float32)

def attention(queries, keys, values, allowed):
    scale = 1.0 / math.sqrt(queries.shape[-1])
    scores = jnp.einsum('qhd,khd->hqk', widen(queries), widen(keys)) * scale
    scores = jnp.where(allowed[None], scores, -1e+30)
    highest = lax.optimization_barrier(jnp.max(scores, axis=-1, keepdims=True))
    raised = jnp.exp(scores - highest)
    shares = raised / lax.optimization_barrier(jnp.sum(raised, axis=-1, keepdims=True))
    shares_low = shares.astype(jnp.bfloat16)
    mixed = jnp.einsum('hqk,khd->qhd', widen(shares_low), widen(values)).astype(jnp.bfloat16)
    return (shares, shares_low, mixed)

def attention_backward(mixed_back, queries, keys, values, shares, shares_low):
    scale = 1.0 / math.sqrt(queries.shape[-1])
    share_back = jnp.einsum('qhd,khd->hqk', widen(mixed_back), widen(values))
    value_back = jnp.einsum('hqk,qhd->khd', widen(shares_low), widen(mixed_back))
    centre = lax.optimization_barrier(jnp.sum(shares * share_back, axis=-1, keepdims=True))
    score_back = (shares * (share_back - centre) * scale).astype(jnp.bfloat16)
    query_back = jnp.einsum('hqk,khd->qhd', widen(score_back), widen(keys))
    key_back = jnp.einsum('hqk,qhd->khd', widen(score_back), widen(queries))
    return jnp.stack([query_back, key_back, value_back], axis=1).astype(jnp.bfloat16)

def pack_forward(patches, window_row, shared):
    norm_gains, merge_gain, triple_weight, output_weight, gate_up_weight, down_weight, merge_up = shared
    rows, width = patches.shape
    start = patches.astype(jnp.float32)
    scale_one = root_scale(start)
    attend_input = (start * scale_one * norm_gains[0]).astype(jnp.bfloat16)
    projected = product(attend_input, triple_weight.reshape(width, -1)).astype(jnp.bfloat16).reshape(rows, 3, -1, HEAD_DIM)
    patch_windows = jnp.repeat(window_row, 4)
    allowed = patch_windows[:, None] == patch_windows[None, :]
    shares, shares_low, mixed = attention(projected[:, 0], projected[:, 1], projected[:, 2], allowed)
    heads_out = mixed.reshape(rows, -1)
    middle = start + contract_last(heads_out, output_weight)
    scale_two = root_scale(middle)
    feed_input = (middle * scale_two * norm_gains[1]).astype(jnp.bfloat16)
    gate_up = product(feed_input, gate_up_weight.reshape(width, -1)).reshape(rows, 2, -1)
    activated = (jax.nn.silu(gate_up[:, 0]) * gate_up[:, 1]).astype(jnp.bfloat16)
    block_out = middle + contract_last(activated, down_weight)
    scale_three = root_scale(block_out)
    merged = (block_out * scale_three * merge_gain).astype(jnp.bfloat16).reshape(rows // 4, 4 * width)
    pre = product(merged, merge_up)
    return (start, scale_one, attend_input, projected, shares, shares_low, heads_out, middle, scale_two, feed_input, gate_up, activated, block_out, scale_three, pre)

def reference(block_input, windows, cell_rows, text_vectors, sequence_cotangent, norm_gains, merge_gain, triple_weight, output_weight, gate_up_weight, down_weight, merge_up, merge_down):
    shared = (norm_gains, merge_gain, triple_weight, output_weight, gate_up_weight, down_weight, merge_up)
    visual_count = N_DP * CELLS

    def visual_of(item):
        saved = pack_forward(item[0], item[1], shared)
        hidden_cells = gelu_value(saved[-1]).astype(jnp.bfloat16)
        return product(hidden_cells, merge_down).astype(jnp.bfloat16)
    visual = lax.map(visual_of, (block_input, windows))
    by_sequence = visual.reshape(N_DP, SEQS, CELLS, E).transpose(1, 0, 2, 3).reshape(SEQS, visual_count, E)
    is_visual = cell_rows >= 0
    clipped = jnp.clip(cell_rows, 0, visual_count - 1).astype(jnp.int32)
    picks = jax.vmap(lambda table, index: jnp.take(table, index, axis=0))(by_sequence, clipped)
    sequence = jnp.where(is_visual[:, :, None], picks, text_vectors)
    slots = jnp.where(is_visual, cell_rows, visual_count).astype(jnp.int32)

    def collect(cotangent, slot):
        return jnp.zeros((visual_count + 1, E), jnp.bfloat16).at[slot].set(cotangent)[:visual_count]
    by_pack = jax.vmap(collect)(sequence_cotangent, slots)
    visual_back = by_pack.reshape(SEQS, N_DP, CELLS, E).transpose(1, 0, 2, 3).reshape(PACKS, CELLS, E)

    def pack_step(totals, item):
        patches, window_row, cell_back = item
        start, scale_one, attend_input, projected, shares, shares_low, heads_out, middle, scale_two, feed_input, gate_up, activated, block_out, scale_three, pre = pack_forward(patches, window_row, shared)
        rows, width = start.shape
        pre_back = (contract_last(cell_back, merge_down) * gelu_slope(pre)).astype(jnp.bfloat16)
        cells_back = contract_last(pre_back, merge_up).reshape(rows, width)
        out_back = norm_backward(cells_back, block_out, scale_three, merge_gain)
        out_low = out_back.astype(jnp.bfloat16)
        activated_back = product(out_low, down_weight)
        gate = gate_up[:, 0]
        upper = gate_up[:, 1]
        sigmoid_gate = jax.nn.sigmoid(gate)
        gate_part = activated_back * upper * sigmoid_gate * (1.0 + gate * (1.0 - sigmoid_gate))
        up_part = activated_back * gate * sigmoid_gate
        gate_up_back = jnp.stack([gate_part, up_part], axis=1).astype(jnp.bfloat16).reshape(rows, -1)
        feed_back = contract_last(gate_up_back, gate_up_weight.reshape(width, -1))
        middle_back = out_back + norm_backward(feed_back, middle, scale_two, norm_gains[1])
        middle_low = middle_back.astype(jnp.bfloat16)
        heads_back = product(middle_low, output_weight).astype(jnp.bfloat16).reshape(rows, -1, HEAD_DIM)
        triple_back = attention_backward(heads_back, projected[:, 0], projected[:, 1], projected[:, 2], shares, shares_low).reshape(rows, -1)
        attend_back = contract_last(triple_back, triple_weight.reshape(width, -1))
        input_back = middle_back + norm_backward(attend_back, start, scale_one, norm_gains[0])
        terms = (contract_first(attend_input, triple_back).reshape(triple_weight.shape), contract_first(middle_low, heads_out), contract_first(feed_input, gate_up_back).reshape(gate_up_weight.shape), contract_first(out_low, activated))
        rounded = tuple((lax.optimization_barrier(term.astype(jnp.bfloat16)).astype(jnp.float32) for term in terms))
        gain_terms = jnp.stack([lax.optimization_barrier(jnp.sum(attend_back * start * scale_one, axis=0)), lax.optimization_barrier(jnp.sum(feed_back * middle * scale_two, axis=0))])
        updated = tuple((total + term for total, term in zip(totals[:4], rounded))) + (totals[4] + gain_terms,)
        return (updated, input_back)
    start_totals = (jnp.zeros(triple_weight.shape, jnp.float32), jnp.zeros(output_weight.shape, jnp.float32), jnp.zeros(gate_up_weight.shape, jnp.float32), jnp.zeros(down_weight.shape, jnp.float32), jnp.zeros((2, block_input.shape[2]), jnp.float32))
    totals, input_gradient = lax.scan(pack_step, start_totals, (block_input, windows, visual_back))
    return (sequence, input_gradient, totals[0], totals[1], totals[2], totals[3], totals[4])
```

```python
import functools
import math

import jax
import jax.numpy as jnp
from jax import lax
from jax.experimental import pallas as pl
from jax.experimental.pallas import tpu as pltpu
from jax.sharding import PartitionSpec as P

HEAD_DIM = 80


epsilon = 1e-06
root_half = 0.7071067811865476
density_scale = 0.3989422804014327

MESH = pl.DeviceIdType.MESH
VMEM_LIMIT = 60 * 1024 * 1024
VMEM = pl.BlockSpec(memory_space=pltpu.VMEM)
ANY = pl.BlockSpec(memory_space=pl.ANY)


class Place:
    def __init__(self):
        dp, self.y, mp = lax.axis_index("dp"), lax.axis_index("section"), lax.axis_index("mp")
        self.z, self.low = dp // 2, dp % 2
        self.high, self.core = mp // 2, mp % 2

    def at(self, z=None, low=None, y=None, high=None, core=None):
        z = self.z if z is None else z
        low = self.low if low is None else low
        y = self.y if y is None else y
        high = self.high if high is None else high
        core = self.core if core is None else core
        return (z * 2 + low, y, high * 2 + core)

    def along_y(self, k):
        return (self.y + k) % 4

    def along_z(self, k):
        return (self.z + k) % 4


def greet(devices):
    barrier = pltpu.get_barrier_semaphore()
    for device in devices:
        pl.semaphore_signal(barrier, inc=1, device_id=device, device_id_type=MESH)
    pl.semaphore_wait(barrier, len(devices))


def send(source, target, sems, index, device):
    copy = pltpu.make_async_remote_copy(
        src_ref=source,
        dst_ref=target,
        send_sem=sems[0].at[index],
        recv_sem=sems[1].at[index],
        device_id=device,
        device_id_type=MESH,
    )
    copy.start()
    return copy


def sem_pair(*shape):
    return [pltpu.SemaphoreType.DMA(shape), pltpu.SemaphoreType.DMA(shape)]


def wide(values):
    return values.astype(jnp.float32)


def low(values):
    return values.astype(jnp.bfloat16)


def sum_kernel(chunks, part, out, got, half, other, s1, r1, s2, r2, s3, r3):
    me = Place()
    sibling, partner = me.at(core=1 - me.core), me.at(high=1 - me.high)
    rows = part.shape[0] // 2
    step = rows // chunks
    greet((sibling, partner))
    mine, theirs = me.core * rows, (1 - me.core) * rows
    first = [
        send(
            part.at[pl.ds(pl.multiple_of(theirs + k * step, step), step)],
            got.at[pl.ds(k * step, step)],
            (s1, r1),
            k,
            sibling,
        )
        for k in range(chunks)
    ]
    second, third = [], []
    for k in range(chunks):
        here = pl.ds(k * step, step)
        first[k].wait_recv()
        half[here] = low(
            wide(part[pl.ds(pl.multiple_of(mine + k * step, step), step)]) + wide(got[here])
        )
        second.append(send(half.at[here], other.at[here], (s2, r2), k, partner))
    for k in range(chunks):
        here = pl.ds(k * step, step)
        there = pl.ds(pl.multiple_of(mine + k * step, step), step)
        second[k].wait_recv()
        out[there] = low(wide(half[here]) + wide(other[here]))
        third.append(send(out.at[there], out.at[there], (s3, r3), k, sibling))
    for k in range(chunks):
        third[k].wait()
        first[k].wait_send()
        second[k].wait_send()


def sum_mp(part):
    rows, width = part.shape
    chunks = 4
    half = pltpu.VMEM((rows // 2, width), jnp.bfloat16)
    return pl.pallas_call(
        functools.partial(sum_kernel, chunks),
        out_shape=jax.ShapeDtypeStruct((rows, width), jnp.bfloat16),
        in_specs=[VMEM],
        out_specs=VMEM,
        scratch_shapes=[half, half, half]
        + sem_pair(chunks)
        + sem_pair(chunks)
        + sem_pair(chunks),
        compiler_params=pltpu.CompilerParams(
            collective_id=1, has_side_effects=True, vmem_limit_bytes=VMEM_LIMIT
        ),
        name="sum_mp",
    )(part)


Z_ROWS = (48, 32, 32, 48)


def gather_kernel(count, *refs):
    shards, wholes = refs[:count], refs[count : 2 * count]
    own, s1, r1, s2, r2, s3, r3 = refs[2 * count :]
    me = Place()
    others = (1, 2, 3)
    greet(
        [me.at(y=me.along_y(k)) for k in others]
        + [me.at(z=me.along_z(k)) for k in others]
        + [me.at(low=1 - me.low)]
    )
    locals_, first, second = [], [], []
    spans = []
    for t in range(count):
        rows = shards[t].shape[1]
        quarter = Z_ROWS[t]
        side = (rows - 4 * quarter) // 2
        by_z = pl.ds(pl.multiple_of(me.z * quarter, 16), quarter)
        by_low = pl.ds(pl.multiple_of(4 * quarter + me.low * side, 16), side)
        spans.append((by_z, by_low))
    for t in range(count):
        for k in (1, 3, 2):
            for part in range(2):
                span = spans[t][part]
                first.append(
                    send(
                        shards[t].at[:, span],
                        wholes[t].at[:, me.y, span],
                        (s1, r1),
                        (t * 3 + k - 1) * 2 + part,
                        me.at(y=me.along_y(k)),
                    )
                )
        copy = pltpu.make_async_copy(shards[t], wholes[t].at[:, me.y], own.at[t])
        copy.start()
        locals_.append(copy)
    at = 0
    for t in range(count):
        for k in (1, 3, 2):
            source = me.along_y(4 - k)
            for part in range(2):
                first[at].wait_recv()
                at += 1
                block = wholes[t].at[:, source, spans[t][part]]
                if part == 0:
                    for j in (1, 3, 2):
                        second.append(
                            send(
                                block,
                                block,
                                (s2, r2),
                                (t * 3 + k - 1) * 3 + j - 1,
                                me.at(z=me.along_z(j)),
                            )
                        )
                else:
                    second.append(
                        send(block, block, (s3, r3), t * 3 + k - 1, me.at(low=1 - me.low))
                    )
    for copy in second:
        copy.wait_recv()
    for copy in first + second:
        copy.wait_send()
    for copy in locals_:
        copy.wait()


def gather_weights(*shards):
    count = len(shards)
    return pl.pallas_call(
        functools.partial(gather_kernel, count),
        out_shape=[
            jax.ShapeDtypeStruct((s.shape[0], 4) + s.shape[1:], jnp.bfloat16) for s in shards
        ],
        in_specs=[ANY] * count,
        out_specs=[ANY] * count,
        scratch_shapes=[pltpu.SemaphoreType.DMA((count,))]
        + sem_pair(count * 6)
        + sem_pair(count * 9)
        + sem_pair(count * 3),
        compiler_params=pltpu.CompilerParams(
            collective_id=2, has_side_effects=True, vmem_limit_bytes=VMEM_LIMIT
        ),
        name="gather_weights",
    )(*shards)


A_ROWS = 192
A_PART = A_ROWS // 4
B_ROWS = 128
B_PART = B_ROWS // 4
E_ROWS = A_PART + B_PART
TILE = 16


def over_rows(planes, rows, body):
    tiles = rows // TILE

    @pl.loop(0, planes * tiles)
    def _(i):
        body(i // tiles, pl.multiple_of((i % tiles) * TILE, TILE))


def reduce_kernel(count, *refs):
    terms, gain = refs[:count], refs[count]
    outs, gain_out = refs[count + 1 : 2 * count + 1], refs[2 * count + 1]
    scratch = refs[2 * count + 2 :]
    per = 9
    work = [scratch[t * per : (t + 1) * per] for t in range(count)]
    gain_got, gain_sum, *sems = scratch[count * per :]
    ya_s, za_s, zb_s, yb_s, ex_s, fa_s, g_s = [
        (sems[2 * i], sems[2 * i + 1]) for i in range(7)
    ]
    me = Place()
    others = (1, 2, 3)
    y_at = [None] + [me.at(y=me.along_y(k)) for k in others]
    z_at = [None] + [me.at(z=me.along_z(k)) for k in others]
    side = me.at(low=1 - me.low)
    greet(y_at[1:] + z_at[1:] + [side])
    pending = []

    def go(*arguments):
        copy = send(*arguments)
        pending.append(copy)
        return copy

    order = (1, 3, 2)
    first_a, first_b = [], []
    gain_copies = [go(gain, gain_got.at[k - 1], g_s, k - 1, y_at[k]) for k in order]
    for t in range(count):
        ya, sa, za, zb, sb, yb, ee, ex, fa = work[t]
        first_a.append(
            [
                go(terms[t].at[:, me.along_y(k), pl.ds(0, A_ROWS)], ya.at[k - 1], ya_s, t * 3 + k - 1, y_at[k])
                for k in order
            ]
        )
        first_b.append(
            [
                go(
                    terms[t].at[:, :, pl.ds(pl.multiple_of(A_ROWS + me.along_z(k) * B_PART, TILE), B_PART)],
                    zb.at[k - 1],
                    zb_s,
                    t * 3 + k - 1,
                    z_at[k],
                )
                for k in order
            ]
        )
    second_a, second_b, third, fourth = [], [], [], []
    for copy in gain_copies:
        copy.wait_recv()
    gain_sum[0] = gain[...] + gain_got[0] + gain_got[1] + gain_got[2]
    gain_copies = [go(gain_sum.at[0], gain_got.at[2 + k], g_s, 2 + k, z_at[k]) for k in order]
    for t in range(count):
        ya, sa, za, zb, sb, yb, ee, ex, fa = work[t]
        planes = terms[t].shape[0]
        for copy in first_b[t]:
            copy.wait_recv()

        def add_b(i, r):
            p, q = i // 4, i % 4
            here = pl.ds(r, TILE)
            own = terms[t][p, q, pl.ds(pl.multiple_of(A_ROWS + me.z * B_PART + r, TILE), TILE)]
            sb[p, q, here] = low(
                wide(own) + wide(zb[0, p, q, here]) + wide(zb[1, p, q, here]) + wide(zb[2, p, q, here])
            )

        over_rows(planes * 4, B_PART, add_b)
        second_b.append(
            [go(sb.at[:, me.along_y(k)], yb.at[k - 1], yb_s, t * 3 + k - 1, y_at[k]) for k in order]
        )
        for copy in first_a[t]:
            copy.wait_recv()

        def add_a(p, r):
            here = pl.ds(r, TILE)
            sa[p, here] = low(
                wide(terms[t][p, me.y, here]) + wide(ya[0, p, here]) + wide(ya[1, p, here]) + wide(ya[2, p, here])
            )

        over_rows(planes, A_ROWS, add_a)
        second_a.append(
            [
                go(
                    sa.at[:, pl.ds(pl.multiple_of(me.along_z(k) * A_PART, TILE), A_PART)],
                    za.at[k - 1],
                    za_s,
                    t * 3 + k - 1,
                    z_at[k],
                )
                for k in order
            ]
        )
    for copy in gain_copies:
        copy.wait_recv()
    gain_sum[1] = gain_sum[0] + gain_got[3] + gain_got[4] + gain_got[5]
    gain_copies = [go(gain_sum.at[1], gain_got.at[6], g_s, 6, side)]
    for t in range(count):
        ya, sa, za, zb, sb, yb, ee, ex, fa = work[t]
        planes = terms[t].shape[0]
        for copy in second_b[t] + second_a[t]:
            copy.wait_recv()

        def add_a(p, r):
            here = pl.ds(r, TILE)
            own = sa[p, pl.ds(pl.multiple_of(me.z * A_PART + r, TILE), TILE)]
            ee[p, here] = low(wide(own) + wide(za[0, p, here]) + wide(za[1, p, here]) + wide(za[2, p, here]))

        def add_b(p, r):
            here = pl.ds(r, TILE)
            ee[p, pl.ds(pl.multiple_of(A_PART + r, TILE), TILE)] = low(
                wide(sb[p, me.y, here]) + wide(yb[0, p, here]) + wide(yb[1, p, here]) + wide(yb[2, p, here])
            )

        over_rows(planes, A_PART, add_a)
        over_rows(planes, B_PART, add_b)
        third.append(go(ee, ex, ex_s, t, side))
    for copy in gain_copies:
        copy.wait_recv()
    gain_out[...] = gain_sum[1] + gain_got[6]
    for t in range(count):
        ya, sa, za, zb, sb, yb, ee, ex, fa = work[t]
        planes = terms[t].shape[0]
        third[t].wait_recv()

        def add(p, r):
            here = pl.ds(r, TILE)
            fa[0, p, here] = low(wide(ee[p, here]) + wide(ex[p, here]))

        over_rows(planes, E_ROWS, add)
        fourth.append([go(fa.at[0], fa.at[k], fa_s, t * 3 + k - 1, z_at[k]) for k in order])
    for t in range(count):
        ya, sa, za, zb, sb, yb, ee, ex, fa = work[t]
        planes = terms[t].shape[0]
        for k in (0,) + order:
            if k:
                fourth[t][order.index(k)].wait_recv()
            source = (me.z + 4 - k) % 4

            def put_a(p, r):
                outs[t][p, pl.ds(pl.multiple_of(source * A_PART + r, TILE), TILE)] = wide(
                    fa[k, p, pl.ds(r, TILE)]
                )

            def put_b(p, r):
                outs[t][p, pl.ds(pl.multiple_of(A_ROWS + source * B_PART + r, TILE), TILE)] = wide(
                    fa[k, p, pl.ds(pl.multiple_of(A_PART + r, TILE), TILE)]
                )

            over_rows(planes, A_PART, put_a)
            over_rows(planes, B_PART, put_b)
    for copy in pending:
        copy.wait_send()


def reduce_gradients(gain_terms, *terms):
    count = len(terms)
    scratch = []
    for term in terms:
        planes, _, _, width = term.shape

        def buffer(*shape):
            return pltpu.VMEM(shape + (width,), jnp.bfloat16)

        scratch += [
            buffer(3, planes, A_ROWS),
            buffer(planes, A_ROWS),
            buffer(3, planes, A_PART),
            buffer(3, planes, 4, B_PART),
            buffer(planes, 4, B_PART),
            buffer(3, planes, B_PART),
            buffer(planes, E_ROWS),
            buffer(planes, E_ROWS),
            buffer(4, planes, E_ROWS),
        ]
    gain_rows = (8, gain_terms.shape[1])
    scratch += [pltpu.VMEM((7,) + gain_rows, jnp.float32), pltpu.VMEM((2,) + gain_rows, jnp.float32)]
    for size in (3 * count, 3 * count, 3 * count, 3 * count, count, 3 * count, 7):
        scratch += sem_pair(size)
    padded = jnp.concatenate(
        [gain_terms, jnp.zeros((6, gain_terms.shape[1]), jnp.float32)], axis=0
    )
    results = pl.pallas_call(
        functools.partial(reduce_kernel, count),
        out_shape=[
            jax.ShapeDtypeStruct((t.shape[0],) + t.shape[2:], jnp.float32) for t in terms
        ]
        + [jax.ShapeDtypeStruct(gain_rows, jnp.float32)],
        in_specs=[VMEM] * (count + 1),
        out_specs=[VMEM] * (count + 1),
        scratch_shapes=scratch,
        compiler_params=pltpu.CompilerParams(
            collective_id=3, has_side_effects=True, vmem_limit_bytes=VMEM_LIMIT
        ),
        name="reduce_gradients",
    )(*terms, padded)
    return results[:count], results[count][:2]


def passed_along(value, axis, steps):
    count = lax.axis_size(axis)
    initial, last = (max(0, -steps), min(count, count - steps))
    return lax.ppermute(value, axis, [(source, source + steps) for source in range(initial, last)])


def root_scale(values):
    return lax.rsqrt(jnp.mean(values * values, axis=-1, keepdims=True) + epsilon)


def norm_backward(cotangent, values, scale, gain):
    weighted = cotangent * gain
    return scale * weighted - values * scale**3 * jnp.mean(
        weighted * values, axis=-1, keepdims=True
    )


def gelu_value(values):
    return 0.5 * values * (1.0 + jax.scipy.special.erf(values * root_half))


def gelu_slope(values):
    return (
        0.5 * (1.0 + jax.scipy.special.erf(values * root_half))
        + values * jnp.exp(-0.5 * values * values) * density_scale
    )


def product(left, right):
    return jnp.dot(left, right, preferred_element_type=jnp.float32)


def contract_last(left, right):
    return lax.dot_general(
        left, right, (((1,), (1,)), ((), ())), preferred_element_type=jnp.float32
    )


def contract_first(left, right):
    return lax.dot_general(
        left, right, (((0,), (0,)), ((), ())), preferred_element_type=jnp.float32
    )


def local_attention(queries, keys, values, allowed):
    scale = 1.0 / math.sqrt(queries.shape[-1])
    scores = jnp.einsum("qhd,khd->hqk", queries, keys, preferred_element_type=jnp.float32) * scale
    scores = jnp.where(allowed[None], scores, -1e30)
    highest = jnp.max(scores, axis=-1, keepdims=True)
    raised = jnp.exp(scores - highest)
    shares = raised / jnp.sum(raised, axis=-1, keepdims=True)
    shares_low = shares.astype(jnp.bfloat16)
    mixed = jnp.einsum(
        "hqk,khd->qhd", shares_low, values, preferred_element_type=jnp.float32
    ).astype(jnp.bfloat16)
    return (shares, shares_low, mixed)


def local_attention_backward(mixed_back, queries, keys, values, shares, shares_low):
    scale = 1.0 / math.sqrt(queries.shape[-1])
    share_back = jnp.einsum("qhd,khd->hqk", mixed_back, values, preferred_element_type=jnp.float32)
    value_back = jnp.einsum(
        "hqk,qhd->khd", shares_low, mixed_back, preferred_element_type=jnp.float32
    )
    centre = jnp.sum(shares * share_back, axis=-1, keepdims=True)
    score_back = (shares * (share_back - centre) * scale).astype(jnp.bfloat16)
    query_back = jnp.einsum("hqk,khd->qhd", score_back, keys, preferred_element_type=jnp.float32)
    key_back = jnp.einsum("hqk,qhd->khd", score_back, queries, preferred_element_type=jnp.float32)
    return jnp.stack([query_back, key_back, value_back], axis=1).astype(jnp.bfloat16)


def planes_of(weight):
    return jnp.transpose(weight, (1, 0, 2))


def stacked(left, back, planes):
    width = left.shape[1]
    pieces = back.reshape(back.shape[0], planes, -1)
    terms = jnp.einsum("ri,rpj->pij", left, pieces, preferred_element_type=jnp.float32)
    return low(terms).reshape(planes, 4, width // 4, -1)


def local(
    block_input,
    windows,
    cell_rows,
    text_vectors,
    sequence_cotangent,
    norm_gains,
    merge_gain,
    triple_weight,
    output_weight,
    gate_up_weight,
    down_weight,
    merge_up,
    merge_down,
):
    sections = lax.axis_size("section")
    columns = lax.axis_size("mp")
    whole_triple, whole_output, whole_gate_up, whole_down = gather_weights(
        planes_of(triple_weight),
        output_weight[None],
        planes_of(gate_up_weight),
        down_weight[None],
    )
    width = block_input.shape[2]
    whole_triple = planes_of(whole_triple.reshape(3, width, -1))
    whole_gate_up = planes_of(whole_gate_up.reshape(2, width, -1))
    whole_output = whole_output.reshape(width, -1)
    whole_down = whole_down.reshape(width, -1)
    patches = block_input[0]
    rows, width = patches.shape
    cells = rows // 4
    start = patches.astype(jnp.float32)
    scale_one = root_scale(start)
    attend_input = (start * scale_one * norm_gains[0]).astype(jnp.bfloat16)
    projected = (
        product(attend_input, whole_triple.reshape(width, -1))
        .astype(jnp.bfloat16)
        .reshape(rows, 3, -1, HEAD_DIM)
    )
    patch_windows = jnp.repeat(windows[0], 4)
    allowed = patch_windows[:, None] == patch_windows[None, :]
    shares, shares_low, mixed = local_attention(
        projected[:, 0], projected[:, 1], projected[:, 2], allowed
    )
    heads_out = mixed.reshape(rows, -1)
    middle = start + sum_mp(contract_last(heads_out, whole_output).astype(jnp.bfloat16)).astype(jnp.float32)
    scale_two = root_scale(middle)
    feed_input = (middle * scale_two * norm_gains[1]).astype(jnp.bfloat16)
    gate_up = product(feed_input, whole_gate_up.reshape(width, -1)).reshape(rows, 2, -1)
    activated = (jax.nn.silu(gate_up[:, 0]) * gate_up[:, 1]).astype(jnp.bfloat16)
    block_out = middle + sum_mp(contract_last(activated, whole_down).astype(jnp.bfloat16)).astype(jnp.float32)
    scale_three = root_scale(block_out)
    merged = (block_out * scale_three * merge_gain).astype(jnp.bfloat16).reshape(cells, 4 * width)
    pre = product(lax.all_gather(merged, "section", axis=0, tiled=True), merge_up)
    hidden_cells = gelu_value(pre).astype(jnp.bfloat16)
    local_units = merge_up.shape[1]
    llm_width = merge_down.shape[1]
    terms = jnp.einsum(
        "sck,kme->smce",
        hidden_cells.reshape(sections, cells, local_units),
        merge_down.reshape(local_units, columns, llm_width // columns),
        preferred_element_type=jnp.float32,
    )
    visual = (
        lax.psum_scatter(
            terms.reshape(sections * columns, cells, -1).astype(jnp.bfloat16),
            ("section", "mp"),
            scatter_dimension=0,
            tiled=True,
        )
        .astype(jnp.float32)[0]
        .astype(jnp.bfloat16)
    )
    following = passed_along(visual, "dp", -1)
    candidates = jnp.concatenate([visual, following], axis=0)
    offset = lax.axis_index("dp") * cells
    row_cells = cell_rows[0]
    is_visual = row_cells >= 0
    local_cells = jnp.where(is_visual, row_cells - offset, 0)
    picked = jnp.take(candidates, local_cells, axis=0)
    sequence = jnp.where(is_visual[:, None], picked, text_vectors[0])[None]
    slots = jnp.where(is_visual, row_cells - offset, 2 * cells)
    arrived = (
        jnp.zeros((2 * cells + 1, visual.shape[1]), jnp.bfloat16)
        .at[slots]
        .set(sequence_cotangent[0])
    )
    returned = passed_along(arrived[cells : 2 * cells], "dp", 1)
    visual_back = arrived[:cells] + returned
    gathered_back = lax.all_gather(visual_back[None], ("section", "mp"), axis=0, tiled=True)
    hidden_back = jnp.einsum(
        "smce,kme->sck",
        gathered_back.reshape(sections, columns, cells, -1),
        merge_down.reshape(local_units, columns, -1),
        preferred_element_type=jnp.float32,
    )
    pre_back = (hidden_back.reshape(sections * cells, local_units) * gelu_slope(pre)).astype(
        jnp.bfloat16
    )
    pieces = contract_last(pre_back, merge_up).reshape(sections, cells, -1)
    owned = lax.psum_scatter(
        pieces.astype(jnp.bfloat16), "section", scatter_dimension=0, tiled=True
    )
    cells_back = sum_mp(owned.reshape(rows, width)).astype(jnp.float32)
    out_back = norm_backward(cells_back, block_out, scale_three, merge_gain)
    out_low = out_back.astype(jnp.bfloat16)
    activated_back = product(out_low, whole_down)
    gate = gate_up[:, 0]
    upper = gate_up[:, 1]
    sigmoid_gate = jax.nn.sigmoid(gate)
    gate_part = activated_back * upper * sigmoid_gate * (1.0 + gate * (1.0 - sigmoid_gate))
    up_part = activated_back * gate * sigmoid_gate
    gate_up_back = jnp.stack([gate_part, up_part], axis=1).astype(jnp.bfloat16).reshape(rows, -1)
    feed_back = sum_mp(
        contract_last(gate_up_back, whole_gate_up.reshape(width, -1)).astype(jnp.bfloat16)
    ).astype(jnp.float32)
    middle_back = out_back + norm_backward(feed_back, middle, scale_two, norm_gains[1])
    middle_low = middle_back.astype(jnp.bfloat16)
    heads_back = product(middle_low, whole_output).astype(jnp.bfloat16).reshape(rows, -1, HEAD_DIM)
    triple_back = local_attention_backward(
        heads_back, projected[:, 0], projected[:, 1], projected[:, 2], shares, shares_low
    ).reshape(rows, -1)
    attend_back = sum_mp(
        contract_last(triple_back, whole_triple.reshape(width, -1)).astype(jnp.bfloat16)
    ).astype(jnp.float32)
    input_gradient = (middle_back + norm_backward(attend_back, start, scale_one, norm_gains[0]))[
        None
    ]
    gain_terms = jnp.stack(
        [
            jnp.sum(attend_back * start * scale_one, axis=0),
            jnp.sum(feed_back * middle * scale_two, axis=0),
        ]
    )
    gradients, gain_gradient = reduce_gradients(
        gain_terms,
        stacked(attend_input, triple_back, 3),
        stacked(middle_low, heads_out, 1),
        stacked(feed_input, gate_up_back, 2),
        stacked(out_low, activated, 1),
    )
    gradients = (
        planes_of(gradients[0]),
        gradients[1][0],
        planes_of(gradients[2]),
        gradients[3][0],
    )
    return (
        sequence,
        input_gradient,
        gradients[0],
        gradients[1],
        gradients[2],
        gradients[3],
        gain_gradient,
    )


def solution(mesh):
    placed = (
        P(("dp", "section"), None, None),
        P(("dp", "section"), None),
        P("section", "dp"),
        P("section", "dp", "mp"),
        P("section", "dp", "mp"),
        P(),
        P(),
        P("section", None, "mp"),
        P("section", "mp"),
        P("section", None, "mp"),
        P("section", "mp"),
        P(None, ("section", "mp")),
        P(("section", "mp"), None),
    )
    return jax.shard_map(
        local,
        mesh=mesh,
        in_specs=placed,
        out_specs=(
            P("section", "dp", "mp"),
            P(("dp", "section"), None, None),
            P("section", None, "mp"),
            P("section", "mp"),
            P("section", None, "mp"),
            P("section", "mp"),
            P(),
        ),
        check_vma=False,
    )
```

```python
import functools
import math

import jax
import jax.numpy as jnp
from jax import lax
from jax.experimental import pallas as pl
from jax.experimental.pallas import tpu as pltpu
from jax.sharding import PartitionSpec as P

HEAD_DIM = 80


epsilon = 1e-06
root_half = 0.7071067811865476
density_scale = 0.3989422804014327

MESH = pl.DeviceIdType.MESH
VMEM_LIMIT = 60 * 1024 * 1024
VMEM = pl.BlockSpec(memory_space=pltpu.VMEM)
ANY = pl.BlockSpec(memory_space=pl.ANY)


class Place:
    def __init__(self):
        dp, self.y, mp = lax.axis_index("dp"), lax.axis_index("section"), lax.axis_index("mp")
        self.z, self.low = dp // 2, dp % 2
        self.high, self.core = mp // 2, mp % 2

    def at(self, z=None, low=None, y=None, high=None, core=None):
        z = self.z if z is None else z
        low = self.low if low is None else low
        y = self.y if y is None else y
        high = self.high if high is None else high
        core = self.core if core is None else core
        return (z * 2 + low, y, high * 2 + core)

    def along_y(self, k):
        return (self.y + k) % 4

    def along_z(self, k):
        return (self.z + k) % 4


def greet(devices):
    barrier = pltpu.get_barrier_semaphore()
    for device in devices:
        pl.semaphore_signal(barrier, inc=1, device_id=device, device_id_type=MESH)
    pl.semaphore_wait(barrier, len(devices))


def send(source, target, sems, index, device):
    copy = pltpu.make_async_remote_copy(
        src_ref=source,
        dst_ref=target,
        send_sem=sems[0].at[index],
        recv_sem=sems[1].at[index],
        device_id=device,
        device_id_type=MESH,
    )
    copy.start()
    return copy


def sem_pair(*shape):
    return [pltpu.SemaphoreType.DMA(shape), pltpu.SemaphoreType.DMA(shape)]


def wide(values):
    return values.astype(jnp.float32)


def low(values):
    return values.astype(jnp.bfloat16)


def sum_kernel(chunks, part, out, got, half, other, s1, r1, s2, r2, s3, r3):
    me = Place()
    sibling, partner = me.at(core=1 - me.core), me.at(high=1 - me.high)
    rows = part.shape[0] // 2
    step = rows // chunks
    greet((sibling, partner))
    mine, theirs = me.core * rows, (1 - me.core) * rows
    first = [
        send(
            part.at[pl.ds(pl.multiple_of(theirs + k * step, step), step)],
            got.at[pl.ds(k * step, step)],
            (s1, r1),
            k,
            sibling,
        )
        for k in range(chunks)
    ]
    second, third = [], []
    for k in range(chunks):
        here = pl.ds(k * step, step)
        first[k].wait_recv()
        half[here] = low(
            wide(part[pl.ds(pl.multiple_of(mine + k * step, step), step)]) + wide(got[here])
        )
        second.append(send(half.at[here], other.at[here], (s2, r2), k, partner))
    for k in range(chunks):
        here = pl.ds(k * step, step)
        there = pl.ds(pl.multiple_of(mine + k * step, step), step)
        second[k].wait_recv()
        out[there] = low(wide(half[here]) + wide(other[here]))
        third.append(send(out.at[there], out.at[there], (s3, r3), k, sibling))
    for k in range(chunks):
        third[k].wait()
        first[k].wait_send()
        second[k].wait_send()


def sum_mp(part):
    rows, width = part.shape
    chunks = 4
    half = pltpu.VMEM((rows // 2, width), jnp.bfloat16)
    return pl.pallas_call(
        functools.partial(sum_kernel, chunks),
        out_shape=jax.ShapeDtypeStruct((rows, width), jnp.bfloat16),
        in_specs=[VMEM],
        out_specs=VMEM,
        scratch_shapes=[half, half, half]
        + sem_pair(chunks)
        + sem_pair(chunks)
        + sem_pair(chunks),
        compiler_params=pltpu.CompilerParams(
            collective_id=1, has_side_effects=True, vmem_limit_bytes=VMEM_LIMIT
        ),
        name="sum_mp",
    )(part)


Z_ROWS = (48, 32, 32, 48)


def gather_kernel(count, *refs):
    shards, wholes = refs[:count], refs[count : 2 * count]
    own, s1, r1, s2, r2, s3, r3 = refs[2 * count :]
    me = Place()
    others = (1, 2, 3)
    greet(
        [me.at(y=me.along_y(k)) for k in others]
        + [me.at(z=me.along_z(k)) for k in others]
        + [me.at(low=1 - me.low)]
    )
    locals_, first, second = [], [], []
    spans = []
    for t in range(count):
        rows = shards[t].shape[1]
        quarter = Z_ROWS[t]
        side = (rows - 4 * quarter) // 2
        by_z = pl.ds(pl.multiple_of(me.z * quarter, 16), quarter)
        by_low = pl.ds(pl.multiple_of(4 * quarter + me.low * side, 16), side)
        spans.append((by_z, by_low))
    for t in range(count):
        for k in (1, 3, 2):
            for part in range(2):
                span = spans[t][part]
                first.append(
                    send(
                        shards[t].at[:, span],
                        wholes[t].at[:, me.y, span],
                        (s1, r1),
                        (t * 3 + k - 1) * 2 + part,
                        me.at(y=me.along_y(k)),
                    )
                )
        copy = pltpu.make_async_copy(shards[t], wholes[t].at[:, me.y], own.at[t])
        copy.start()
        locals_.append(copy)
    at = 0
    for t in range(count):
        for k in (1, 3, 2):
            source = me.along_y(4 - k)
            for part in range(2):
                first[at].wait_recv()
                at += 1
                block = wholes[t].at[:, source, spans[t][part]]
                if part == 0:
                    for j in (1, 3, 2):
                        second.append(
                            send(
                                block,
                                block,
                                (s2, r2),
                                (t * 3 + k - 1) * 3 + j - 1,
                                me.at(z=me.along_z(j)),
                            )
                        )
                else:
                    second.append(
                        send(block, block, (s3, r3), t * 3 + k - 1, me.at(low=1 - me.low))
                    )
    for copy in second:
        copy.wait_recv()
    for copy in first + second:
        copy.wait_send()
    for copy in locals_:
        copy.wait()


def gather_weights(*shards):
    count = len(shards)
    return pl.pallas_call(
        functools.partial(gather_kernel, count),
        out_shape=[
            jax.ShapeDtypeStruct((s.shape[0], 4) + s.shape[1:], jnp.bfloat16) for s in shards
        ],
        in_specs=[ANY] * count,
        out_specs=[ANY] * count,
        scratch_shapes=[pltpu.SemaphoreType.DMA((count,))]
        + sem_pair(count * 6)
        + sem_pair(count * 9)
        + sem_pair(count * 3),
        compiler_params=pltpu.CompilerParams(
            collective_id=2, has_side_effects=True, vmem_limit_bytes=VMEM_LIMIT
        ),
        name="gather_weights",
    )(*shards)


A_ROWS = 192
A_PART = A_ROWS // 4
B_ROWS = 128
B_PART = B_ROWS // 4
E_ROWS = A_PART + B_PART
TILE = 16


def over_rows(planes, rows, body):
    tiles = rows // TILE

    @pl.loop(0, planes * tiles)
    def _(i):
        body(i // tiles, pl.multiple_of((i % tiles) * TILE, TILE))


def reduce_kernel(count, *refs):
    terms, gain = refs[:count], refs[count]
    outs, gain_out = refs[count + 1 : 2 * count + 1], refs[2 * count + 1]
    scratch = refs[2 * count + 2 :]
    per = 9
    work = [scratch[t * per : (t + 1) * per] for t in range(count)]
    gain_got, gain_sum, *sems = scratch[count * per :]
    ya_s, za_s, zb_s, yb_s, ex_s, fa_s, g_s = [
        (sems[2 * i], sems[2 * i + 1]) for i in range(7)
    ]
    me = Place()
    others = (1, 2, 3)
    y_at = [None] + [me.at(y=me.along_y(k)) for k in others]
    z_at = [None] + [me.at(z=me.along_z(k)) for k in others]
    side = me.at(low=1 - me.low)
    greet(y_at[1:] + z_at[1:] + [side])
    pending = []

    def go(*arguments):
        copy = send(*arguments)
        pending.append(copy)
        return copy

    order = (1, 3, 2)
    first_a, first_b = [], []
    gain_copies = [go(gain, gain_got.at[k - 1], g_s, k - 1, y_at[k]) for k in order]
    for t in range(count):
        ya, sa, za, zb, sb, yb, ee, ex, fa = work[t]
        first_a.append(
            [
                go(terms[t].at[:, me.along_y(k), pl.ds(0, A_ROWS)], ya.at[k - 1], ya_s, t * 3 + k - 1, y_at[k])
                for k in order
            ]
        )
        first_b.append(
            [
                go(
                    terms[t].at[:, :, pl.ds(pl.multiple_of(A_ROWS + me.along_z(k) * B_PART, TILE), B_PART)],
                    zb.at[k - 1],
                    zb_s,
                    t * 3 + k - 1,
                    z_at[k],
                )
                for k in order
            ]
        )
    second_a, second_b, third, fourth = [], [], [], []
    for copy in gain_copies:
        copy.wait_recv()
    gain_sum[0] = gain[...] + gain_got[0] + gain_got[1] + gain_got[2]
    gain_copies = [go(gain_sum.at[0], gain_got.at[2 + k], g_s, 2 + k, z_at[k]) for k in order]
    for t in range(count):
        ya, sa, za, zb, sb, yb, ee, ex, fa = work[t]
        planes = terms[t].shape[0]
        for copy in first_b[t]:
            copy.wait_recv()

        def add_b(i, r):
            p, q = i // 4, i % 4
            here = pl.ds(r, TILE)
            own = terms[t][p, q, pl.ds(pl.multiple_of(A_ROWS + me.z * B_PART + r, TILE), TILE)]
            sb[p, q, here] = low(
                wide(own) + wide(zb[0, p, q, here]) + wide(zb[1, p, q, here]) + wide(zb[2, p, q, here])
            )

        over_rows(planes * 4, B_PART, add_b)
        second_b.append(
            [go(sb.at[:, me.along_y(k)], yb.at[k - 1], yb_s, t * 3 + k - 1, y_at[k]) for k in order]
        )
        for copy in first_a[t]:
            copy.wait_recv()

        def add_a(p, r):
            here = pl.ds(r, TILE)
            sa[p, here] = low(
                wide(terms[t][p, me.y, here]) + wide(ya[0, p, here]) + wide(ya[1, p, here]) + wide(ya[2, p, here])
            )

        over_rows(planes, A_ROWS, add_a)
        second_a.append(
            [
                go(
                    sa.at[:, pl.ds(pl.multiple_of(me.along_z(k) * A_PART, TILE), A_PART)],
                    za.at[k - 1],
                    za_s,
                    t * 3 + k - 1,
                    z_at[k],
                )
                for k in order
            ]
        )
    for copy in gain_copies:
        copy.wait_recv()
    gain_sum[1] = gain_sum[0] + gain_got[3] + gain_got[4] + gain_got[5]
    gain_copies = [go(gain_sum.at[1], gain_got.at[6], g_s, 6, side)]
    for t in range(count):
        ya, sa, za, zb, sb, yb, ee, ex, fa = work[t]
        planes = terms[t].shape[0]
        for copy in second_b[t] + second_a[t]:
            copy.wait_recv()

        def add_a(p, r):
            here = pl.ds(r, TILE)
            own = sa[p, pl.ds(pl.multiple_of(me.z * A_PART + r, TILE), TILE)]
            ee[p, here] = low(wide(own) + wide(za[0, p, here]) + wide(za[1, p, here]) + wide(za[2, p, here]))

        def add_b(p, r):
            here = pl.ds(r, TILE)
            ee[p, pl.ds(pl.multiple_of(A_PART + r, TILE), TILE)] = low(
                wide(sb[p, me.y, here]) + wide(yb[0, p, here]) + wide(yb[1, p, here]) + wide(yb[2, p, here])
            )

        over_rows(planes, A_PART, add_a)
        over_rows(planes, B_PART, add_b)
        third.append(go(ee, ex, ex_s, t, side))
    for copy in gain_copies:
        copy.wait_recv()
    gain_out[...] = gain_sum[1] + gain_got[6]
    for t in range(count):
        ya, sa, za, zb, sb, yb, ee, ex, fa = work[t]
        planes = terms[t].shape[0]
        third[t].wait_recv()

        def add(p, r):
            here = pl.ds(r, TILE)
            fa[0, p, here] = low(wide(ee[p, here]) + wide(ex[p, here]))

        over_rows(planes, E_ROWS, add)
        fourth.append([go(fa.at[0], fa.at[k], fa_s, t * 3 + k - 1, z_at[k]) for k in order])
    for t in range(count):
        ya, sa, za, zb, sb, yb, ee, ex, fa = work[t]
        planes = terms[t].shape[0]
        for k in (0,) + order:
            if k:
                fourth[t][order.index(k)].wait_recv()
            source = (me.z + 4 - k) % 4

            def put_a(p, r):
                outs[t][p, pl.ds(pl.multiple_of(source * A_PART + r, TILE), TILE)] = wide(
                    fa[k, p, pl.ds(r, TILE)]
                )

            def put_b(p, r):
                outs[t][p, pl.ds(pl.multiple_of(A_ROWS + source * B_PART + r, TILE), TILE)] = wide(
                    fa[k, p, pl.ds(pl.multiple_of(A_PART + r, TILE), TILE)]
                )

            over_rows(planes, A_PART, put_a)
            over_rows(planes, B_PART, put_b)
    for copy in pending:
        copy.wait_send()


def reduce_gradients(gain_terms, *terms):
    count = len(terms)
    scratch = []
    for term in terms:
        planes, _, _, width = term.shape

        def buffer(*shape):
            return pltpu.VMEM(shape + (width,), jnp.bfloat16)

        scratch += [
            buffer(3, planes, A_ROWS),
            buffer(planes, A_ROWS),
            buffer(3, planes, A_PART),
            buffer(3, planes, 4, B_PART),
            buffer(planes, 4, B_PART),
            buffer(3, planes, B_PART),
            buffer(planes, E_ROWS),
            buffer(planes, E_ROWS),
            buffer(4, planes, E_ROWS),
        ]
    gain_rows = (8, gain_terms.shape[1])
    scratch += [pltpu.VMEM((7,) + gain_rows, jnp.float32), pltpu.VMEM((2,) + gain_rows, jnp.float32)]
    for size in (3 * count, 3 * count, 3 * count, 3 * count, count, 3 * count, 7):
        scratch += sem_pair(size)
    padded = jnp.concatenate(
        [gain_terms, jnp.zeros((6, gain_terms.shape[1]), jnp.float32)], axis=0
    )
    results = pl.pallas_call(
        functools.partial(reduce_kernel, count),
        out_shape=[
            jax.ShapeDtypeStruct((t.shape[0],) + t.shape[2:], jnp.float32) for t in terms
        ]
        + [jax.ShapeDtypeStruct(gain_rows, jnp.float32)],
        in_specs=[VMEM] * (count + 1),
        out_specs=[VMEM] * (count + 1),
        scratch_shapes=scratch,
        compiler_params=pltpu.CompilerParams(
            collective_id=3, has_side_effects=True, vmem_limit_bytes=VMEM_LIMIT
        ),
        name="reduce_gradients",
    )(*terms, padded)
    return results[:count], results[count][:2]


def root_scale(values):
    return lax.rsqrt(jnp.mean(values * values, axis=-1, keepdims=True) + epsilon)


def norm_backward(cotangent, values, scale, gain):
    weighted = cotangent * gain
    return scale * weighted - values * scale**3 * jnp.mean(
        weighted * values, axis=-1, keepdims=True
    )


def gelu_value(values):
    return 0.5 * values * (1.0 + jax.scipy.special.erf(values * root_half))


def gelu_slope(values):
    return (
        0.5 * (1.0 + jax.scipy.special.erf(values * root_half))
        + values * jnp.exp(-0.5 * values * values) * density_scale
    )


def product(left, right):
    return jnp.dot(left, right, preferred_element_type=jnp.float32)


def contract_last(left, right):
    return lax.dot_general(
        left, right, (((1,), (1,)), ((), ())), preferred_element_type=jnp.float32
    )


def contract_first(left, right):
    return lax.dot_general(
        left, right, (((0,), (0,)), ((), ())), preferred_element_type=jnp.float32
    )


def local_attention(queries, keys, values, allowed):
    scale = 1.0 / math.sqrt(queries.shape[-1])
    scores = jnp.einsum("qhd,khd->hqk", queries, keys, preferred_element_type=jnp.float32) * scale
    scores = jnp.where(allowed[None], scores, -1e30)
    highest = jnp.max(scores, axis=-1, keepdims=True)
    raised = jnp.exp(scores - highest)
    shares = raised / jnp.sum(raised, axis=-1, keepdims=True)
    shares_low = shares.astype(jnp.bfloat16)
    mixed = jnp.einsum(
        "hqk,khd->qhd", shares_low, values, preferred_element_type=jnp.float32
    ).astype(jnp.bfloat16)
    return (shares, shares_low, mixed)


def local_attention_backward(mixed_back, queries, keys, values, shares, shares_low):
    scale = 1.0 / math.sqrt(queries.shape[-1])
    share_back = jnp.einsum("qhd,khd->hqk", mixed_back, values, preferred_element_type=jnp.float32)
    value_back = jnp.einsum(
        "hqk,qhd->khd", shares_low, mixed_back, preferred_element_type=jnp.float32
    )
    centre = jnp.sum(shares * share_back, axis=-1, keepdims=True)
    score_back = (shares * (share_back - centre) * scale).astype(jnp.bfloat16)
    query_back = jnp.einsum("hqk,khd->qhd", score_back, keys, preferred_element_type=jnp.float32)
    key_back = jnp.einsum("hqk,qhd->khd", score_back, queries, preferred_element_type=jnp.float32)
    return jnp.stack([query_back, key_back, value_back], axis=1).astype(jnp.bfloat16)


STEP = 512


def last_with_last(left, right):
    return lax.dot_general(
        left, right, (((1,), (1,)), ((), ())), preferred_element_type=jnp.float32
    )


def merger_kernel(
    rows_across,
    rows_down,
    cotangent,
    text,
    merged,
    up,
    down,
    sequence,
    cells_back,
    spill,
    spill_in,
    backs,
    cells,
    pre,
    hidden,
    hidden_back,
    terms,
    terms_in,
    visual_in,
    visual,
    following,
    pieces,
    pieces_in,
    parts,
    parts_in,
    *sems,
):
    me = Place()
    merged_s, share_s, dp_s, back_s, fore_s, terms_s, visual_s, pieces_s, parts_s, mp_s = [
        (sems[2 * i], sems[2 * i + 1]) for i in range(10)
    ]
    sibling, partner = me.at(core=1 - me.core), me.at(high=1 - me.high)
    turn = 1 - me.low
    after = me.at(z=(me.z + me.low) % 4, low=turn)
    before = me.at(z=(me.z + 3 + me.low) % 4, low=turn)
    pairs = [(j, k) for k in (1, 3, 2) for j in (0, 1)] + [(1, 0)]

    def peer(j, k):
        return me.at(y=me.along_y(k), high=(me.high + j) % 2)

    greet([peer(j, k) for j, k in pairs] + [sibling, after, before])
    pending = []

    def go(*arguments):
        copy = send(*arguments)
        pending.append(copy)
        return copy

    half = pl.ds(pl.multiple_of(me.core * 32, 32), 32)
    merged_copies = {
        k: go(merged.at[half], cells.at[me.y, half], merged_s, k, peer(0, k)) for k in (1, 3, 2)
    }
    cells[me.y] = merged[...]

    slot = lax.broadcasted_iota(jnp.int32, (128, 256), 0)
    offset = (me.z * 2 + me.low) * 64
    taken = jnp.where(rows_across[...] - offset == slot, 1.0, 0.0).astype(jnp.bfloat16)
    for i in range(4):
        span = pl.ds(i * STEP, STEP)
        arrived = low(product(taken, cotangent[:, span]))
        spill[:, span] = arrived[64:]
        backs[me.y, me.high * 2 + me.core, :, span] = arrived[:64]
    spill_copy = go(spill, spill_in, dp_s, 0, after)
    spill_copy.wait_recv()
    own = me.high * 2 + me.core
    for i in range(4):
        span = pl.ds(i * STEP, STEP)
        backs[me.y, own, :, span] = backs[me.y, own, :, span] + spill_in[:, span]
    block = backs.at[me.y, own]
    back_copies = [go(block, block, back_s, j * 4 + k, peer(j, k)) for j, k in pairs]
    fore_copies = [go(block, block, fore_s, 0, sibling)]

    share_copies = []
    for k in (1, 3, 2):
        merged_copies[k].wait_recv()
        region = cells.at[me.along_y(4 - k), half]
        share_copies.append(go(region, region, share_s, k, sibling))
    for copy in share_copies:
        copy.wait_recv()

    pre[...] = jnp.zeros_like(pre)

    @pl.loop(0, 10)
    def _(i):
        span = pl.ds(pl.multiple_of(i * STEP, STEP), STEP)
        pre[...] += last_with_last(cells[:, :, span].reshape(256, STEP), up[:, span])

    hidden[...] = low(gelu_value(pre[...]))

    def term_block(column):
        @pl.loop(0, 4)
        def _(i):
            span = pl.ds(pl.multiple_of(i * STEP, STEP), STEP)
            whole = pl.ds(pl.multiple_of(column * 2048 + i * STEP, STEP), STEP)
            terms[column, :, span] = low(product(hidden[...], down[:, whole]))

    term_copies = []
    for j in (0, 1):
        column = j * 2 + 1 - me.core
        term_block(column)
        term_copies.append(go(terms.at[column], terms_in.at[j], terms_s, j, sibling))
    for j in (0, 1):
        term_block(j * 2 + me.core)

    for (j, k), copy in zip(pairs, back_copies):
        copy.wait_recv()
        region = backs.at[me.along_y((4 - k) % 4), ((me.high + j) % 2) * 2 + me.core]
        fore_copies.append(go(region, region, fore_s, j * 4 + k, sibling))
    for j in (0, 1):
        term_copies[j].wait_recv()
        column = j * 2 + me.core

        @pl.loop(0, 16)
        def _(i):
            here = pl.ds(pl.multiple_of(i * 16, 16), 16)
            terms[column, here] = low(wide(terms[column, here]) + wide(terms_in[j, here]))

    def visual_region(j, k):
        rows = pl.ds(pl.multiple_of(me.along_y(k) * 64, 64), 64)
        return terms.at[((me.high + j) % 2) * 2 + me.core, rows]

    for copy in fore_copies:
        copy.wait_recv()
    hidden_back[...] = jnp.zeros_like(hidden_back)

    @pl.loop(0, 16)
    def _(i):
        inner = pl.ds(pl.multiple_of((i % 4) * STEP, STEP), STEP)
        outer = pl.ds(pl.multiple_of(i * STEP, STEP), STEP)
        left = backs[:, i // 4, :, inner].reshape(256, STEP)
        hidden_back[...] += last_with_last(left, down[:, outer])

    hidden[...] = low(hidden_back[...] * gelu_slope(pre[...]))

    @pl.loop(0, 10)
    def _(i):
        span = pl.ds(pl.multiple_of(i * STEP, STEP), STEP)
        pieces[:, :, :, :, span] = low(product(hidden[...], up[:, span])).reshape(4, 2, 2, 16, STEP)

    pieces_copy = go(pieces.at[:, :, 1 - me.core], pieces_in, pieces_s, 0, sibling)
    pieces_copy.wait_recv()

    @pl.loop(0, 8)
    def _(i):
        a, b = i // 2, i % 2
        for n in range(4):
            span = pl.ds(n * 1280, 1280)
            parts[a, b, :, span] = low(
                wide(pieces[a, b, me.core, :, span]) + wide(pieces_in[a, b, :, span])
            )

    part_copies = [
        go(parts.at[me.along_y(k), (me.high + j) % 2], parts_in.at[j * 4 + k], parts_s, j * 4 + k, peer(j, k))
        for j, k in pairs
    ]
    visual_copies = [
        go(visual_region(j, k), visual_in.at[j * 4 + k], visual_s, j * 4 + k, peer(j, k))
        for j, k in pairs
    ]
    for copy in part_copies:
        copy.wait_recv()
    mine = pl.ds(pl.multiple_of(own * 16, 16), 16)
    for n in range(4):
        span = pl.ds(n * 1280, 1280)
        total = wide(parts[me.y, me.high, :, span])
        for j, k in pairs:
            total = total + wide(parts_in[j * 4 + k, :, span])
        cells_back[mine, span] = low(total)
    mp_copies = [
        go(cells_back.at[mine], cells_back.at[mine], mp_s, 0, partner),
        go(cells_back.at[mine], cells_back.at[mine], mp_s, 1, sibling),
    ]
    mp_copies[0].wait_recv()
    theirs = pl.ds(pl.multiple_of(((1 - me.high) * 2 + me.core) * 16, 16), 16)
    mp_copies.append(go(cells_back.at[theirs], cells_back.at[theirs], mp_s, 2, sibling))

    for copy in visual_copies:
        copy.wait_recv()
    mine_rows = pl.multiple_of(me.y * 64, 64)

    @pl.loop(0, 4)
    def _(i):
        here = pl.ds(pl.multiple_of(i * 16, 16), 16)
        total = wide(terms[own, pl.ds(pl.multiple_of(mine_rows + i * 16, 16), 16)])
        for j, k in pairs:
            total = total + wide(visual_in[j * 4 + k, here])
        visual[here] = low(total)

    visual_copy = go(visual, following, dp_s, 1, before)
    slot = lax.broadcasted_iota(jnp.int32, (256, 64), 1)
    here_cells = jnp.where(rows_down[...] - offset == slot, 1.0, 0.0).astype(jnp.bfloat16)
    next_cells = jnp.where(rows_down[...] - offset - 64 == slot, 1.0, 0.0).astype(jnp.bfloat16)
    visual_copy.wait_recv()
    for i in range(4):
        span = pl.ds(i * STEP, STEP)
        picked = product(here_cells, visual[:, span]) + product(next_cells, following[:, span])
        sequence[:, span] = jnp.where(rows_down[...] >= 0, low(picked), text[:, span])
    mp_copies[1].wait_recv()
    mp_copies[2].wait_recv()
    for copy in pending:
        copy.wait_send()


def merger(cell_rows, cotangent, text, merged, up, down):
    def buffer(*shape):
        return pltpu.VMEM(shape, jnp.bfloat16)

    scratch = [
        buffer(64, 2048),
        buffer(64, 2048),
        buffer(4, 4, 64, 2048),
        buffer(4, 64, 5120),
        pltpu.VMEM((256, 320), jnp.float32),
        buffer(256, 320),
        pltpu.VMEM((256, 320), jnp.float32),
        buffer(4, 256, 2048),
        buffer(2, 256, 2048),
        buffer(8, 64, 2048),
        buffer(64, 2048),
        buffer(64, 2048),
        buffer(4, 2, 2, 16, 5120),
        buffer(4, 2, 16, 5120),
        buffer(4, 2, 16, 5120),
        buffer(8, 16, 5120),
    ]
    for size in (4, 4, 2, 8, 8, 2, 8, 1, 8, 3):
        scratch += sem_pair(size)
    return pl.pallas_call(
        merger_kernel,
        out_shape=[
            jax.ShapeDtypeStruct(text.shape, jnp.bfloat16),
            jax.ShapeDtypeStruct(merged.shape, jnp.bfloat16),
        ],
        in_specs=[VMEM] * 7,
        out_specs=[VMEM] * 2,
        scratch_shapes=scratch,
        compiler_params=pltpu.CompilerParams(
            collective_id=4, has_side_effects=True, vmem_limit_bytes=VMEM_LIMIT
        ),
        name="merger",
    )(cell_rows[None], cell_rows[:, None], cotangent, text, merged, up, down)


def planes_of(weight):
    return jnp.transpose(weight, (1, 0, 2))


def stacked(left, back, planes):
    width = left.shape[1]
    pieces = back.reshape(back.shape[0], planes, -1)
    terms = jnp.einsum("ri,rpj->pij", left, pieces, preferred_element_type=jnp.float32)
    return low(terms).reshape(planes, 4, width // 4, -1)


def local(
    block_input,
    windows,
    cell_rows,
    text_vectors,
    sequence_cotangent,
    norm_gains,
    merge_gain,
    triple_weight,
    output_weight,
    gate_up_weight,
    down_weight,
    merge_up,
    merge_down,
):
    whole_triple, whole_output, whole_gate_up, whole_down = gather_weights(
        planes_of(triple_weight),
        output_weight[None],
        planes_of(gate_up_weight),
        down_weight[None],
    )
    width = block_input.shape[2]
    whole_triple = planes_of(whole_triple.reshape(3, width, -1))
    whole_gate_up = planes_of(whole_gate_up.reshape(2, width, -1))
    whole_output = whole_output.reshape(width, -1)
    whole_down = whole_down.reshape(width, -1)
    patches = block_input[0]
    rows, width = patches.shape
    cells = rows // 4
    start = patches.astype(jnp.float32)
    scale_one = root_scale(start)
    attend_input = (start * scale_one * norm_gains[0]).astype(jnp.bfloat16)
    projected = (
        product(attend_input, whole_triple.reshape(width, -1))
        .astype(jnp.bfloat16)
        .reshape(rows, 3, -1, HEAD_DIM)
    )
    patch_windows = jnp.repeat(windows[0], 4)
    allowed = patch_windows[:, None] == patch_windows[None, :]
    shares, shares_low, mixed = local_attention(
        projected[:, 0], projected[:, 1], projected[:, 2], allowed
    )
    heads_out = mixed.reshape(rows, -1)
    middle = start + sum_mp(contract_last(heads_out, whole_output).astype(jnp.bfloat16)).astype(jnp.float32)
    scale_two = root_scale(middle)
    feed_input = (middle * scale_two * norm_gains[1]).astype(jnp.bfloat16)
    gate_up = product(feed_input, whole_gate_up.reshape(width, -1)).reshape(rows, 2, -1)
    activated = (jax.nn.silu(gate_up[:, 0]) * gate_up[:, 1]).astype(jnp.bfloat16)
    block_out = middle + sum_mp(contract_last(activated, whole_down).astype(jnp.bfloat16)).astype(jnp.float32)
    scale_three = root_scale(block_out)
    merged = (block_out * scale_three * merge_gain).astype(jnp.bfloat16).reshape(cells, 4 * width)
    sequence, cells_back = merger(
        cell_rows[0], sequence_cotangent[0], text_vectors[0], merged, merge_up.T, merge_down
    )
    sequence = sequence[None]
    cells_back = cells_back.reshape(rows, width).astype(jnp.float32)
    out_back = norm_backward(cells_back, block_out, scale_three, merge_gain)
    out_low = out_back.astype(jnp.bfloat16)
    activated_back = product(out_low, whole_down)
    gate = gate_up[:, 0]
    upper = gate_up[:, 1]
    sigmoid_gate = jax.nn.sigmoid(gate)
    gate_part = activated_back * upper * sigmoid_gate * (1.0 + gate * (1.0 - sigmoid_gate))
    up_part = activated_back * gate * sigmoid_gate
    gate_up_back = jnp.stack([gate_part, up_part], axis=1).astype(jnp.bfloat16).reshape(rows, -1)
    feed_back = sum_mp(
        contract_last(gate_up_back, whole_gate_up.reshape(width, -1)).astype(jnp.bfloat16)
    ).astype(jnp.float32)
    middle_back = out_back + norm_backward(feed_back, middle, scale_two, norm_gains[1])
    middle_low = middle_back.astype(jnp.bfloat16)
    heads_back = product(middle_low, whole_output).astype(jnp.bfloat16).reshape(rows, -1, HEAD_DIM)
    triple_back = local_attention_backward(
        heads_back, projected[:, 0], projected[:, 1], projected[:, 2], shares, shares_low
    ).reshape(rows, -1)
    attend_back = sum_mp(
        contract_last(triple_back, whole_triple.reshape(width, -1)).astype(jnp.bfloat16)
    ).astype(jnp.float32)
    input_gradient = (middle_back + norm_backward(attend_back, start, scale_one, norm_gains[0]))[
        None
    ]
    gain_terms = jnp.stack(
        [
            jnp.sum(attend_back * start * scale_one, axis=0),
            jnp.sum(feed_back * middle * scale_two, axis=0),
        ]
    )
    gradients, gain_gradient = reduce_gradients(
        gain_terms,
        stacked(attend_input, triple_back, 3),
        stacked(middle_low, heads_out, 1),
        stacked(feed_input, gate_up_back, 2),
        stacked(out_low, activated, 1),
    )
    gradients = (
        planes_of(gradients[0]),
        gradients[1][0],
        planes_of(gradients[2]),
        gradients[3][0],
    )
    return (
        sequence,
        input_gradient,
        gradients[0],
        gradients[1],
        gradients[2],
        gradients[3],
        gain_gradient,
    )


def solution(mesh):
    placed = (
        P(("dp", "section"), None, None),
        P(("dp", "section"), None),
        P("section", "dp"),
        P("section", "dp", "mp"),
        P("section", "dp", "mp"),
        P(),
        P(),
        P("section", None, "mp"),
        P("section", "mp"),
        P("section", None, "mp"),
        P("section", "mp"),
        P(None, ("section", "mp")),
        P(("section", "mp"), None),
    )
    return jax.shard_map(
        local,
        mesh=mesh,
        in_specs=placed,
        out_specs=(
            P("section", "dp", "mp"),
            P(("dp", "section"), None, None),
            P("section", None, "mp"),
            P("section", "mp"),
            P("section", None, "mp"),
            P("section", "mp"),
            P(),
        ),
        check_vma=False,
    )
```

```python
import functools
import math

import jax
import jax.numpy as jnp
from jax import lax
from jax.experimental import pallas as pl
from jax.experimental.pallas import tpu as pltpu
from jax.sharding import PartitionSpec as P

HEAD_DIM = 80


epsilon = 1e-06
root_half = 0.7071067811865476
density_scale = 0.3989422804014327

MESH = pl.DeviceIdType.MESH
VMEM_LIMIT = 60 * 1024 * 1024
VMEM = pl.BlockSpec(memory_space=pltpu.VMEM)
ANY = pl.BlockSpec(memory_space=pl.ANY)


class Place:
    def __init__(self):
        dp, self.y, mp = lax.axis_index("dp"), lax.axis_index("section"), lax.axis_index("mp")
        self.z, self.low = dp // 2, dp % 2
        self.high, self.core = mp // 2, mp % 2

    def at(self, z=None, low=None, y=None, high=None, core=None):
        z = self.z if z is None else z
        low = self.low if low is None else low
        y = self.y if y is None else y
        high = self.high if high is None else high
        core = self.core if core is None else core
        return (z * 2 + low, y, high * 2 + core)

    def along_y(self, k):
        return (self.y + k) % 4

    def along_z(self, k):
        return (self.z + k) % 4


def greet(devices):
    barrier = pltpu.get_barrier_semaphore()
    for device in devices:
        pl.semaphore_signal(barrier, inc=1, device_id=device, device_id_type=MESH)
    pl.semaphore_wait(barrier, len(devices))


def send(source, target, sems, index, device):
    copy = pltpu.make_async_remote_copy(
        src_ref=source,
        dst_ref=target,
        send_sem=sems[0].at[index],
        recv_sem=sems[1].at[index],
        device_id=device,
        device_id_type=MESH,
    )
    copy.start()
    return copy


def sem_pair(*shape):
    return [pltpu.SemaphoreType.DMA(shape), pltpu.SemaphoreType.DMA(shape)]


def wide(values):
    return values.astype(jnp.float32)


def low(values):
    return values.astype(jnp.bfloat16)


def root_scale(values):
    return lax.rsqrt(jnp.mean(values * values, axis=-1, keepdims=True) + epsilon)


def norm_backward(cotangent, values, scale, gain):
    weighted = cotangent * gain
    return scale * weighted - values * scale**3 * jnp.mean(
        weighted * values, axis=-1, keepdims=True
    )


def gelu_value(values):
    return 0.5 * values * (1.0 + jax.scipy.special.erf(values * root_half))


def gelu_slope(values):
    return (
        0.5 * (1.0 + jax.scipy.special.erf(values * root_half))
        + values * jnp.exp(-0.5 * values * values) * density_scale
    )


def product(left, right):
    return jnp.dot(left, right, preferred_element_type=jnp.float32)


QUARTER, HALF = 48, 48
ALONE = 320 - 4 * QUARTER - 2 * HALF
UNITS = ((0, 0, 3), (1, 0, 1), (2, 0, 1), (2, 1, 1), (3, 0, 1))
PAIRS = [(j, k) for k in (1, 3, 2) for j in (0, 1)] + [(1, 0)]


STEP = 512


def last_with_last(left, right):
    return lax.dot_general(
        left, right, (((1,), (1,)), ((), ())), preferred_element_type=jnp.float32
    )


def merger_kernel(
    rows_down,
    text,
    merged,
    backs,
    up,
    down,
    sequence,
    cells_back,
    cells,
    pre,
    hidden,
    pre_back,
    hidden_back,
    terms,
    terms_in,
    visual_in,
    visual,
    following,
    pieces,
    pieces_in,
    parts,
    parts_in,
    *sems,
):
    me = Place()
    merged_s, share_s, dp_s, terms_s, visual_s, pieces_s, parts_s, mp_s = [
        (sems[2 * i], sems[2 * i + 1]) for i in range(8)
    ]
    sibling, partner = me.at(core=1 - me.core), me.at(high=1 - me.high)
    turn = 1 - me.low
    after = me.at(z=(me.z + me.low) % 4, low=turn)
    before = me.at(z=(me.z + 3 + me.low) % 4, low=turn)

    def peer(j, k):
        return me.at(y=me.along_y(k), high=(me.high + j) % 2)

    greet([peer(j, k) for j, k in PAIRS] + [sibling, after, before])
    pending = []

    def go(*arguments):
        copy = send(*arguments)
        pending.append(copy)
        return copy

    half = pl.ds(pl.multiple_of(me.core * 32, 32), 32)
    merged_copies = {
        k: go(merged.at[half], cells.at[me.y, half], merged_s, k, peer(0, k)) for k in (1, 3, 2)
    }
    cells[me.y] = merged[...]
    own = me.high * 2 + me.core
    hidden_back[...] = jnp.zeros_like(hidden_back)

    @pl.loop(0, 16)
    def _(i):
        inner = pl.ds(pl.multiple_of((i % 4) * STEP, STEP), STEP)
        outer = pl.ds(pl.multiple_of(i * STEP, STEP), STEP)
        left = backs[:, i // 4, :, inner].reshape(256, STEP)
        hidden_back[...] += last_with_last(left, down[:, outer])

    share_copies = []
    for k in (1, 3, 2):
        merged_copies[k].wait_recv()
        region = cells.at[me.along_y(4 - k), half]
        share_copies.append(go(region, region, share_s, k, sibling))
    for copy in share_copies:
        copy.wait_recv()

    pre[...] = jnp.zeros_like(pre)

    @pl.loop(0, 10)
    def _(i):
        span = pl.ds(pl.multiple_of(i * STEP, STEP), STEP)
        pre[...] += last_with_last(cells[:, :, span].reshape(256, STEP), up[:, span])

    pre_back[...] = low(hidden_back[...] * gelu_slope(pre[...]))

    @pl.loop(0, 10)
    def _(i):
        span = pl.ds(pl.multiple_of(i * STEP, STEP), STEP)
        pieces[:, :, :, :, span] = low(product(pre_back[...], up[:, span])).reshape(4, 2, 2, 16, STEP)

    pieces_copy = go(pieces.at[:, :, 1 - me.core], pieces_in, pieces_s, 0, sibling)
    hidden[...] = low(gelu_value(pre[...]))
    pieces_copy.wait_recv()

    @pl.loop(0, 8)
    def _(i):
        a, b = i // 2, i % 2
        for n in range(4):
            span = pl.ds(n * 1280, 1280)
            parts[a, b, :, span] = low(
                wide(pieces[a, b, me.core, :, span]) + wide(pieces_in[a, b, :, span])
            )

    part_copies = [
        go(parts.at[me.along_y(k), (me.high + j) % 2], parts_in.at[j * 4 + k], parts_s, j * 4 + k, peer(j, k))
        for j, k in PAIRS
    ]

    def term_block(column):
        @pl.loop(0, 4)
        def _(i):
            span = pl.ds(pl.multiple_of(i * STEP, STEP), STEP)
            whole = pl.ds(pl.multiple_of(column * 2048 + i * STEP, STEP), STEP)
            terms[column, :, span] = low(product(hidden[...], down[:, whole]))

    term_copies = []
    for j in (0, 1):
        column = j * 2 + 1 - me.core
        term_block(column)
        term_copies.append(go(terms.at[column], terms_in.at[j], terms_s, j, sibling))
    for j in (0, 1):
        column = j * 2 + me.core
        term_block(column)
        term_copies[j].wait_recv()

        @pl.loop(0, 16)
        def _(i):
            here = pl.ds(pl.multiple_of(i * 16, 16), 16)
            terms[column, here] = low(wide(terms[column, here]) + wide(terms_in[j, here]))

    def visual_region(j, k):
        rows = pl.ds(pl.multiple_of(me.along_y(k) * 64, 64), 64)
        return terms.at[((me.high + j) % 2) * 2 + me.core, rows]

    visual_copies = [
        go(visual_region(j, k), visual_in.at[j * 4 + k], visual_s, j * 4 + k, peer(j, k))
        for j, k in PAIRS
    ]
    for copy in part_copies:
        copy.wait_recv()
    mine = pl.ds(pl.multiple_of(own * 16, 16), 16)
    for n in range(4):
        span = pl.ds(n * 1280, 1280)
        total = wide(parts[me.y, me.high, :, span])
        for j, k in PAIRS:
            total = total + wide(parts_in[j * 4 + k, :, span])
        cells_back[mine, span] = low(total)
    mp_copies = [
        go(cells_back.at[mine], cells_back.at[mine], mp_s, 0, partner),
        go(cells_back.at[mine], cells_back.at[mine], mp_s, 1, sibling),
    ]
    mp_copies[0].wait_recv()
    theirs = pl.ds(pl.multiple_of(((1 - me.high) * 2 + me.core) * 16, 16), 16)
    mp_copies.append(go(cells_back.at[theirs], cells_back.at[theirs], mp_s, 2, sibling))

    for copy in visual_copies:
        copy.wait_recv()
    mine_rows = pl.multiple_of(me.y * 64, 64)

    @pl.loop(0, 4)
    def _(i):
        here = pl.ds(pl.multiple_of(i * 16, 16), 16)
        total = wide(terms[own, pl.ds(pl.multiple_of(mine_rows + i * 16, 16), 16)])
        for j, k in PAIRS:
            total = total + wide(visual_in[j * 4 + k, here])
        visual[here] = low(total)

    visual_copy = go(visual, following, dp_s, 0, before)
    slot = lax.broadcasted_iota(jnp.int32, (256, 64), 1)
    offset = (me.z * 2 + me.low) * 64
    here_cells = jnp.where(rows_down[...] - offset == slot, 1.0, 0.0).astype(jnp.bfloat16)
    next_cells = jnp.where(rows_down[...] - offset - 64 == slot, 1.0, 0.0).astype(jnp.bfloat16)
    visual_copy.wait_recv()
    for i in range(4):
        span = pl.ds(i * STEP, STEP)
        picked = product(here_cells, visual[:, span]) + product(next_cells, following[:, span])
        sequence[:, span] = jnp.where(rows_down[...] >= 0, low(picked), text[:, span])
    mp_copies[1].wait_recv()
    mp_copies[2].wait_recv()
    for copy in pending:
        copy.wait_send()


def merger(cell_rows, text, merged, backs, up, down):
    def buffer(*shape):
        return pltpu.VMEM(shape, jnp.bfloat16)

    scratch = [
        buffer(4, 64, 5120),
        pltpu.VMEM((256, 320), jnp.float32),
        buffer(256, 320),
        buffer(256, 320),
        pltpu.VMEM((256, 320), jnp.float32),
        buffer(4, 256, 2048),
        buffer(2, 256, 2048),
        buffer(8, 64, 2048),
        buffer(64, 2048),
        buffer(64, 2048),
        buffer(4, 2, 2, 16, 5120),
        buffer(4, 2, 16, 5120),
        buffer(4, 2, 16, 5120),
        buffer(8, 16, 5120),
    ]
    for size in (4, 4, 1, 2, 8, 1, 8, 3):
        scratch += sem_pair(size)
    return pl.pallas_call(
        merger_kernel,
        out_shape=[
            jax.ShapeDtypeStruct(text.shape, jnp.bfloat16),
            jax.ShapeDtypeStruct(merged.shape, jnp.bfloat16),
        ],
        in_specs=[VMEM] * 6,
        out_specs=[VMEM] * 2,
        scratch_shapes=scratch,
        compiler_params=pltpu.CompilerParams(
            collective_id=4, has_side_effects=True, vmem_limit_bytes=VMEM_LIMIT
        ),
        name="merger",
    )(cell_rows[:, None], text, merged, backs, up, down)


CHUNKS = 4


class SumOverMp:
    def __init__(self, me, go, buffers, sems):
        self.me, self.go = me, go
        self.outgoing, self.got, self.half, self.other, self.total = buffers
        self.sems = sems
        self.sibling, self.partner = me.at(core=1 - me.core), me.at(high=1 - me.high)
        self.mine = pl.multiple_of(me.core * 128, 128)
        self.theirs = pl.multiple_of((1 - me.core) * 128, 128)

    def begin(self, compute):
        step = 128 // CHUNKS
        self.outgoing[...] = low(compute(pl.ds(self.theirs, 128)))
        first = []
        for k in range(CHUNKS):
            here = pl.ds(k * step, step)
            first.append(
                self.go(self.outgoing.at[here], self.got.at[here], self.sems, k, self.sibling)
            )
        self.half[...] = low(compute(pl.ds(self.mine, 128)))
        self.second = []
        for k in range(CHUNKS):
            here = pl.ds(k * step, step)
            first[k].wait_recv()
            self.half[here] = low(wide(self.half[here]) + wide(self.got[here]))
            self.second.append(
                self.go(self.half.at[here], self.other.at[here], self.sems, CHUNKS + k, self.partner)
            )

    def end(self):
        step = 128 // CHUNKS
        third = []
        for k in range(CHUNKS):
            here = pl.ds(k * step, step)
            there = pl.ds(pl.multiple_of(self.mine + k * step, step), step)
            self.second[k].wait_recv()
            self.total[there] = low(wide(self.half[here]) + wide(self.other[here]))
            third.append(
                self.go(
                    self.total.at[there], self.total.at[there], self.sems, 2 * CHUNKS + k, self.sibling
                )
            )
        for copy in third:
            copy.wait_recv()


def sum_buffers():
    half = pltpu.VMEM((128, 1280), jnp.bfloat16)
    return [half, half, half, half, pltpu.VMEM((256, 1280), jnp.bfloat16)]


def head_mask(head):
    lane = lax.broadcasted_iota(jnp.int32, (1, 320), 1)
    inside = (lane >= head * HEAD_DIM) & (lane < (head + 1) * HEAD_DIM)
    return jnp.where(inside, 1.0, 0.0).astype(jnp.bfloat16)


def head_shares(queries, keys, mask, allowed):
    scores = last_with_last(queries * mask, keys) * (1.0 / math.sqrt(HEAD_DIM))
    scores = jnp.where(allowed, scores, -1e30)
    raised = jnp.exp(scores - jnp.max(scores, axis=-1, keepdims=True))
    return raised / jnp.sum(raised, axis=-1, keepdims=True)


def forward_kernel(*refs):
    block_input, across, downwards, gains, merge_gain, rows_across, cotangent = refs[:7]
    shards = refs[7:11]
    wholes = refs[11:15]
    attend, projected, heads_out, middle, feed, gate, upper, activated, block_out, merged = refs[15:25]
    backs, spill, spill_in = refs[25:28]
    sum_one, sum_two = refs[28:33], refs[33:38]
    own, *pairs = refs[38:]
    y_s, z_s, x_s, one_s, two_s, dp_s, back_s, fore_s = [
        (pairs[2 * i], pairs[2 * i + 1]) for i in range(8)
    ]
    me = Place()
    others = (1, 3, 2)
    y_at = {k: me.at(y=me.along_y(k)) for k in others}
    z_at = {k: me.at(z=me.along_z(k)) for k in others}
    side, sibling = me.at(low=1 - me.low), me.at(core=1 - me.core)
    after = me.at(z=(me.z + me.low) % 4, low=1 - me.low)
    far = me.at(z=(me.z + 3 + 2 * me.low) % 4, low=1 - me.low)

    def peer(j, k):
        return me.at(y=me.along_y(k), high=(me.high + j) % 2)

    greet([peer(j, k) for j, k in PAIRS] + [z_at[k] for k in others] + [side, far, sibling])
    pending = []

    def go(*arguments):
        copy = send(*arguments)
        pending.append(copy)
        return copy

    spans = (
        pl.ds(pl.multiple_of(me.z * QUARTER, 16), QUARTER),
        pl.ds(pl.multiple_of(4 * QUARTER + me.low * HALF, 16), HALF),
        pl.ds(320 - ALONE, ALONE),
    )
    local_copies, first, second = [], {}, {}

    def begin(u):
        t, p, n = UNITS[u]
        for k in others:
            for part in range(3):
                first[u, k, part] = go(
                    shards[t].at[pl.ds(p, n), spans[part]],
                    wholes[t].at[pl.ds(p, n), me.y, spans[part]],
                    y_s,
                    (u * 3 + k - 1) * 3 + part,
                    y_at[k],
                )

    def forward(u):
        t, p, n = UNITS[u]
        copies = []
        for k in others:
            source = me.along_y(4 - k)
            first[u, k, 0].wait_recv()
            block = wholes[t].at[pl.ds(p, n), source, spans[0]]
            for j in others:
                copies.append(go(block, block, z_s, (u * 3 + k - 1) * 3 + j - 1, z_at[j]))
            first[u, k, 1].wait_recv()
            block = wholes[t].at[pl.ds(p, n), source, spans[1]]
            copies.append(go(block, block, x_s, u * 3 + k - 1, side))
            copies.append(first[u, k, 2])
        second[u] = copies

    def complete(u):
        for copy in second[u]:
            copy.wait_recv()

    def whole(t, p):
        return wholes[t][p].reshape(1280, -1)

    begin(0)
    begin(1)
    for t in range(4):
        copy = pltpu.make_async_copy(shards[t], wholes[t].at[:, me.y], own.at[t])
        copy.start()
        local_copies.append(copy)
    slot = lax.broadcasted_iota(jnp.int32, (128, 256), 0)
    offset = (me.z * 2 + me.low) * 64
    taken = jnp.where(rows_across[...] - offset == slot, 1.0, 0.0).astype(jnp.bfloat16)
    column = me.high * 2 + me.core
    for i in range(4):
        span = pl.ds(i * STEP, STEP)
        arrived = low(product(taken, cotangent[:, span]))
        spill[:, span] = arrived[64:]
        backs[me.y, column, :, span] = arrived[:64]
    spill_copy = go(spill, spill_in, dp_s, 0, after)
    start = wide(block_input[...])
    attend[...] = low(start * root_scale(start) * gains[0:1])
    forward(0)
    begin(2)
    forward(1)
    begin(3)
    complete(0)
    for copy in local_copies:
        copy.wait()
    for p in range(3):
        projected[p] = low(product(attend[...], whole(0, p)))
    forward(2)
    begin(4)
    allowed = downwards[...] == across[...]
    mixed = jnp.zeros((256, 320), jnp.float32)
    for head in range(4):
        mask = head_mask(head)
        shares = head_shares(projected[0], projected[1], mask, allowed)
        mixed = mixed + product(low(shares), projected[2] * mask)
    heads_out[...] = low(mixed)
    complete(1)
    forward(3)
    total = SumOverMp(me, go, sum_one, one_s)
    total.begin(lambda rows: last_with_last(heads_out[rows], whole(1, 0)))
    spill_copy.wait_recv()
    for i in range(4):
        span = pl.ds(i * STEP, STEP)
        backs[me.y, column, :, span] = backs[me.y, column, :, span] + spill_in[:, span]
    forward(4)
    total.end()
    block = backs.at[me.y, column]
    back_copies = [go(block, block, back_s, j * 4 + k, peer(j, k)) for j, k in PAIRS]
    fore_copies = [go(block, block, fore_s, 0, sibling)]
    middle[...] = wide(block_input[...]) + wide(sum_one[4][...])
    feed[...] = low(middle[...] * root_scale(middle[...]) * gains[1:2])
    complete(2)
    gate[...] = product(feed[...], whole(2, 0))
    complete(3)
    upper[...] = product(feed[...], whole(2, 1))
    activated[...] = low(gate[...] * jax.nn.sigmoid(gate[...]) * upper[...])
    complete(4)
    total = SumOverMp(me, go, sum_two, two_s)
    total.begin(lambda rows: last_with_last(activated[rows], whole(3, 0)))
    for (j, k), copy in zip(PAIRS, back_copies):
        copy.wait_recv()
        region = backs.at[me.along_y((4 - k) % 4), ((me.high + j) % 2) * 2 + me.core]
        fore_copies.append(go(region, region, fore_s, j * 4 + k, sibling))
    total.end()
    block_out[...] = middle[...] + wide(sum_two[4][...])
    merged[...] = low(block_out[...] * root_scale(block_out[...]) * merge_gain[...])
    for copy in fore_copies:
        copy.wait_recv()
    for copy in pending:
        copy.wait_send()


def block_forward(block_input, patch_windows, gains, merge_gain, cell_rows, cotangent, shards):
    rows, width = block_input.shape
    units = shards[2].shape[2]

    def shape(kind, *dims):
        return jax.ShapeDtypeStruct(dims, kind)

    low_, wide_ = jnp.bfloat16, jnp.float32
    outs = [shape(low_, s.shape[0], 4, *s.shape[1:]) for s in shards] + [
        shape(low_, rows, width),
        shape(low_, 3, rows, 320),
        shape(low_, rows, 320),
        shape(wide_, rows, width),
        shape(low_, rows, width),
        shape(wide_, rows, units),
        shape(wide_, rows, units),
        shape(low_, rows, units),
        shape(wide_, rows, width),
        shape(low_, rows, width),
        shape(low_, 4, 4, 64, cotangent.shape[1]),
    ]
    spill = pltpu.VMEM((64, cotangent.shape[1]), jnp.bfloat16)
    scratch = [spill, spill] + sum_buffers() + sum_buffers() + [pltpu.SemaphoreType.DMA((4,))]
    for size in (45, 45, 15, 3 * CHUNKS, 3 * CHUNKS, 1, 8, 8):
        scratch += sem_pair(size)
    results = pl.pallas_call(
        forward_kernel,
        out_shape=outs,
        in_specs=[VMEM] * 11,
        out_specs=[VMEM] * len(outs),
        scratch_shapes=scratch,
        compiler_params=pltpu.CompilerParams(
            collective_id=1, has_side_effects=True, vmem_limit_bytes=VMEM_LIMIT
        ),
        name="block_forward",
    )(
        block_input,
        patch_windows[None],
        patch_windows[:, None],
        gains,
        merge_gain[None],
        cell_rows[None],
        cotangent,
        *shards,
    )
    return results[:4], results[4:14], results[14]


A_ROWS = 192
A_PART = A_ROWS // 4
B_PART = (320 - A_ROWS) // 4
E_ROWS = A_PART + B_PART
TILE = 16
ORDER = (1, 3, 2)


def over_rows(planes, rows, body):
    tiles = rows // TILE

    @pl.loop(0, planes * tiles)
    def _(i):
        body(i // tiles, pl.multiple_of((i % tiles) * TILE, TILE))


class Reduction:
    def __init__(self, me, go, term, out, buffers, sems, index, y_at, z_at, side):
        self.me, self.go, self.term, self.out = me, go, term, out
        self.ya, self.sa, self.za, self.zb, self.sb, self.yb, self.ee, self.ex = buffers
        self.sems, self.index, self.y_at, self.z_at, self.side = sems, index, y_at, z_at, side
        self.planes = term.shape[0]

    def stage_one(self):
        me = self.me
        self.first_a = [
            self.go(
                self.term.at[:, me.along_y(k), pl.ds(0, A_ROWS)],
                self.ya.at[k - 1],
                self.sems[0],
                self.index * 3 + k - 1,
                self.y_at[k],
            )
            for k in ORDER
        ]
        self.first_b = [
            self.go(
                self.term.at[
                    :, :, pl.ds(pl.multiple_of(A_ROWS + me.along_z(k) * B_PART, TILE), B_PART)
                ],
                self.zb.at[k - 1],
                self.sems[1],
                self.index * 3 + k - 1,
                self.z_at[k],
            )
            for k in ORDER
        ]

    def stage_two(self):
        me, term, ya, sa, zb, sb = self.me, self.term, self.ya, self.sa, self.zb, self.sb
        for copy in self.first_b:
            copy.wait_recv()

        def add_b(i, r):
            p, q = i // 4, i % 4
            here = pl.ds(r, TILE)
            there = pl.ds(pl.multiple_of(A_ROWS + me.z * B_PART + r, TILE), TILE)
            sb[p, q, here] = low(
                wide(term[p, q, there])
                + wide(zb[0, p, q, here])
                + wide(zb[1, p, q, here])
                + wide(zb[2, p, q, here])
            )

        over_rows(self.planes * 4, B_PART, add_b)
        self.second = [
            self.go(
                sb.at[:, me.along_y(k)],
                self.yb.at[k - 1],
                self.sems[2],
                self.index * 3 + k - 1,
                self.y_at[k],
            )
            for k in ORDER
        ]
        for copy in self.first_a:
            copy.wait_recv()

        def add_a(p, r):
            here = pl.ds(r, TILE)
            sa[p, here] = low(
                wide(term[p, me.y, here])
                + wide(ya[0, p, here])
                + wide(ya[1, p, here])
                + wide(ya[2, p, here])
            )

        over_rows(self.planes, A_ROWS, add_a)
        self.second += [
            self.go(
                sa.at[:, pl.ds(pl.multiple_of(me.along_z(k) * A_PART, TILE), A_PART)],
                self.za.at[k - 1],
                self.sems[3],
                self.index * 3 + k - 1,
                self.z_at[k],
            )
            for k in ORDER
        ]

    def stage_three(self):
        me, sa, za, sb, yb, ee = self.me, self.sa, self.za, self.sb, self.yb, self.ee
        for copy in self.second:
            copy.wait_recv()

        def add_a(p, r):
            here = pl.ds(r, TILE)
            there = pl.ds(pl.multiple_of(me.z * A_PART + r, TILE), TILE)
            ee[p, here] = low(
                wide(sa[p, there]) + wide(za[0, p, here]) + wide(za[1, p, here]) + wide(za[2, p, here])
            )

        def add_b(p, r):
            here = pl.ds(r, TILE)
            there = pl.ds(pl.multiple_of(A_PART + r, TILE), TILE)
            ee[p, there] = low(
                wide(sb[p, me.y, here])
                + wide(yb[0, p, here])
                + wide(yb[1, p, here])
                + wide(yb[2, p, here])
            )

        over_rows(self.planes, A_PART, add_a)
        over_rows(self.planes, B_PART, add_b)
        self.third = self.go(ee, self.ex, self.sems[4], self.index, self.side)

    def stage_four(self):
        me, out, ee, ex = self.me, self.out, self.ee, self.ex
        self.third.wait_recv()

        def add(p, r):
            here = pl.ds(r, TILE)
            out[me.z, p, here] = low(wide(ee[p, here]) + wide(ex[p, here]))

        over_rows(self.planes, E_ROWS, add)
        self.fourth = [
            self.go(
                out.at[me.z], out.at[me.z], self.sems[5], self.index * 3 + k - 1, self.z_at[k]
            )
            for k in ORDER
        ]

    def finish(self):
        for copy in self.fourth:
            copy.wait_recv()


def first_with_first(left, right):
    return lax.dot_general(
        left, right, (((0,), (0,)), ((), ())), preferred_element_type=jnp.float32
    )


def backward_kernel(*refs):
    (
        block_input,
        across,
        downwards,
        gains,
        merge_gain,
        cells_back,
        triple,
        output,
        gate_up,
        down,
        attend,
        projected,
        heads_out,
        middle,
        feed,
        gate,
        upper,
        activated,
        block_out,
    ) = refs[:19]
    input_gradient = refs[19]
    outs = refs[20:25]
    gain_out = refs[25]
    refs = refs[26:]
    sum_one, sum_two = refs[:5], refs[5:10]
    terms = refs[10:15]
    buffers = [refs[15 + 8 * t : 23 + 8 * t] for t in range(5)]
    middle_back, middle_low, out_low, gate_up_back, triple_back, gain, gain_in, gain_sum = refs[55:63]
    sems = refs[63:]
    pair = [(sems[2 * i], sems[2 * i + 1]) for i in range(9)]
    me = Place()
    y_at = {k: me.at(y=me.along_y(k)) for k in ORDER}
    z_at = {k: me.at(z=me.along_z(k)) for k in ORDER}
    side = me.at(low=1 - me.low)
    greet(
        [y_at[k] for k in ORDER]
        + [z_at[k] for k in ORDER]
        + [side, me.at(core=1 - me.core), me.at(high=1 - me.high)]
    )
    pending = []

    def go(*arguments):
        copy = send(*arguments)
        pending.append(copy)
        return copy

    reductions = [
        Reduction(me, go, terms[t], outs[t], buffers[t], pair[:6], t, y_at, z_at, side)
        for t in range(5)
    ]
    of_triple, of_output, of_gate, of_upper, of_down = reductions

    def form(t, p, left, right):
        for i in range(2):
            block = first_with_first(left[:, i * 640 : (i + 1) * 640], right)
            terms[t][p, 2 * i : 2 * i + 2] = low(block).reshape(2, 320, right.shape[1])

    def whole(weight, p):
        return weight[p].reshape(1280, -1)

    scale_three = root_scale(block_out[...])
    out_back = norm_backward(wide(cells_back[...]), block_out[...], scale_three, merge_gain[...])
    middle_back[...] = out_back
    out_low[...] = low(out_back)
    form(4, 0, out_low, activated[...])
    of_down.stage_one()
    activated_back = product(out_low[...], whole(down, 0))
    slope = jax.nn.sigmoid(gate[...])
    gate_up_back[1] = low(activated_back * gate[...] * slope)
    gate_up_back[0] = low(activated_back * upper[...] * slope * (1.0 + gate[...] * (1.0 - slope)))
    total = SumOverMp(me, go, sum_one, pair[6])
    total.begin(
        lambda rows: last_with_last(gate_up_back[0, rows], whole(gate_up, 0))
        + last_with_last(gate_up_back[1, rows], whole(gate_up, 1))
    )
    form(2, 0, feed, gate_up_back[0])
    of_gate.stage_one()
    total.end()
    feed_back = wide(sum_one[4][...])
    scale_two = root_scale(middle[...])
    middle_back[...] = middle_back[...] + norm_backward(
        feed_back, middle[...], scale_two, gains[1:2]
    )
    middle_low[...] = low(middle_back[...])
    gain[...] = jnp.zeros_like(gain)
    gain[1:2] = jnp.sum(feed_back * middle[...] * scale_two, axis=0, keepdims=True)
    form(3, 0, feed, gate_up_back[1])
    of_upper.stage_one()
    heads_back = low(product(middle_low[...], whole(output, 0)))
    of_down.stage_two()
    form(1, 0, middle_low, heads_out[...])
    of_output.stage_one()
    allowed = downwards[...] == across[...]
    query_back = jnp.zeros((256, 320), jnp.float32)
    key_back = jnp.zeros((256, 320), jnp.float32)
    value_back = jnp.zeros((256, 320), jnp.float32)
    for head in range(4):
        mask = head_mask(head)
        shares = head_shares(projected[0], projected[1], mask, allowed)
        share_back = last_with_last(heads_back * mask, projected[2])
        centre = jnp.sum(shares * share_back, axis=-1, keepdims=True)
        score_back = low(shares * (share_back - centre) * (1.0 / math.sqrt(HEAD_DIM)))
        query_back = query_back + product(score_back, projected[1] * mask)
        key_back = key_back + first_with_first(score_back, projected[0] * mask)
        value_back = value_back + first_with_first(low(shares), heads_back * mask)
    triple_back[0] = low(query_back)
    triple_back[1] = low(key_back)
    triple_back[2] = low(value_back)
    of_gate.stage_two()
    total = SumOverMp(me, go, sum_two, pair[7])
    total.begin(
        lambda rows: last_with_last(triple_back[0, rows], whole(triple, 0))
        + last_with_last(triple_back[1, rows], whole(triple, 1))
        + last_with_last(triple_back[2, rows], whole(triple, 2))
    )
    for p in range(3):
        form(0, p, attend, triple_back[p])
    of_triple.stage_one()
    of_down.stage_three()
    total.end()
    attend_back = wide(sum_two[4][...])
    start = wide(block_input[...])
    scale_one = root_scale(start)
    input_gradient[...] = middle_back[...] + norm_backward(attend_back, start, scale_one, gains[0:1])
    gain[0:1] = jnp.sum(attend_back * start * scale_one, axis=0, keepdims=True)
    gain_copies = [go(gain, gain_in.at[k - 1], pair[8], k - 1, y_at[k]) for k in ORDER]
    of_upper.stage_two()
    of_gate.stage_three()
    of_down.stage_four()
    of_output.stage_two()
    for copy in gain_copies:
        copy.wait_recv()
    gain_sum[0] = gain[...] + gain_in[0] + gain_in[1] + gain_in[2]
    gain_copies = [go(gain_sum.at[0], gain_in.at[2 + k], pair[8], 2 + k, z_at[k]) for k in ORDER]
    of_triple.stage_two()
    of_upper.stage_three()
    of_gate.stage_four()
    for copy in gain_copies:
        copy.wait_recv()
    gain_sum[1] = gain_sum[0] + gain_in[3] + gain_in[4] + gain_in[5]
    gain_copies = [go(gain_sum.at[1], gain_in.at[6], pair[8], 6, side)]
    of_output.stage_three()
    of_triple.stage_three()
    of_upper.stage_four()
    for copy in gain_copies:
        copy.wait_recv()
    gain_out[...] = gain_sum[1] + gain_in[6]
    of_output.stage_four()
    of_triple.stage_four()
    for reduction in reductions:
        reduction.finish()
    for copy in pending:
        copy.wait_send()


def block_backward(block_input, patch_windows, gains, merge_gain, cells_back, wholes, saved):
    rows, width = block_input.shape
    units = saved[5].shape[1]

    def low_buffer(*shape):
        return pltpu.VMEM(shape, jnp.bfloat16)

    def wide_buffer(*shape):
        return pltpu.VMEM(shape, jnp.float32)

    sizes = ((3, 320), (1, 320), (1, units), (1, units), (1, units))
    scratch = sum_buffers() + sum_buffers()
    scratch += [low_buffer(planes, 4, 320, columns) for planes, columns in sizes]
    for planes, columns in sizes:
        scratch += [
            low_buffer(3, planes, A_ROWS, columns),
            low_buffer(planes, A_ROWS, columns),
            low_buffer(3, planes, A_PART, columns),
            low_buffer(3, planes, 4, B_PART, columns),
            low_buffer(planes, 4, B_PART, columns),
            low_buffer(3, planes, B_PART, columns),
            low_buffer(planes, E_ROWS, columns),
            low_buffer(planes, E_ROWS, columns),
        ]
    scratch += [
        wide_buffer(rows, width),
        low_buffer(rows, width),
        low_buffer(rows, width),
        low_buffer(2, rows, units),
        low_buffer(3, rows, 320),
        wide_buffer(8, width),
        wide_buffer(7, 8, width),
        wide_buffer(2, 8, width),
    ]
    for size in (15, 15, 15, 15, 5, 15, 3 * CHUNKS, 3 * CHUNKS, 7):
        scratch += sem_pair(size)
    operands = [
        block_input,
        patch_windows[None],
        patch_windows[:, None],
        gains,
        merge_gain[None],
        cells_back,
        *wholes,
        *saved,
    ]
    outs = (
        [jax.ShapeDtypeStruct((rows, width), jnp.float32)]
        + [
            jax.ShapeDtypeStruct((4, planes, E_ROWS, columns), jnp.bfloat16)
            for planes, columns in sizes
        ]
        + [jax.ShapeDtypeStruct((8, width), jnp.float32)]
    )
    results = pl.pallas_call(
        backward_kernel,
        out_shape=outs,
        in_specs=[VMEM] * len(operands),
        out_specs=[VMEM] * len(outs),
        scratch_shapes=scratch,
        compiler_params=pltpu.CompilerParams(
            collective_id=3, has_side_effects=True, vmem_limit_bytes=VMEM_LIMIT
        ),
        name="block_backward",
    )(*operands)

    def assembled(owned):
        planes, columns = owned.shape[1], owned.shape[3]
        owned = jnp.transpose(owned, (1, 0, 2, 3))
        return wide(
            jnp.concatenate(
                [
                    owned[:, :, :A_PART].reshape(planes, -1, columns),
                    owned[:, :, A_PART:].reshape(planes, -1, columns),
                ],
                axis=1,
            )
        )

    gradients = [assembled(owned) for owned in results[1:6]]
    return results[0], gradients, results[6][:2]


def planes_of(weight):
    return jnp.transpose(weight, (1, 0, 2))


def local(
    block_input,
    windows,
    cell_rows,
    text_vectors,
    sequence_cotangent,
    norm_gains,
    merge_gain,
    triple_weight,
    output_weight,
    gate_up_weight,
    down_weight,
    merge_up,
    merge_down,
):
    patches = block_input[0]
    rows, width = patches.shape
    patch_windows = jnp.repeat(windows[0], 4)
    shards = (
        planes_of(triple_weight),
        output_weight[None],
        planes_of(gate_up_weight),
        down_weight[None],
    )
    wholes, saved, backs = block_forward(
        patches,
        patch_windows,
        norm_gains,
        merge_gain,
        cell_rows[0],
        sequence_cotangent[0],
        shards,
    )
    sequence, cells_back = merger(
        cell_rows[0],
        text_vectors[0],
        saved[-1].reshape(rows // 4, 4 * width),
        backs,
        merge_up.T,
        merge_down,
    )
    input_gradient, gradients, gain_gradient = block_backward(
        patches,
        patch_windows,
        norm_gains,
        merge_gain,
        cells_back.reshape(rows, width),
        wholes,
        saved[:-1],
    )
    return (
        sequence[None],
        input_gradient[None],
        planes_of(gradients[0]),
        gradients[1][0],
        jnp.stack([gradients[2][0], gradients[3][0]], axis=1),
        gradients[4][0],
        gain_gradient,
    )


def solution(mesh):
    placed = (
        P(("dp", "section"), None, None),
        P(("dp", "section"), None),
        P("section", "dp"),
        P("section", "dp", "mp"),
        P("section", "dp", "mp"),
        P(),
        P(),
        P("section", None, "mp"),
        P("section", "mp"),
        P("section", None, "mp"),
        P("section", "mp"),
        P(None, ("section", "mp")),
        P(("section", "mp"), None),
    )
    return jax.shard_map(
        local,
        mesh=mesh,
        in_specs=placed,
        out_specs=(
            P("section", "dp", "mp"),
            P(("dp", "section"), None, None),
            P("section", None, "mp"),
            P("section", "mp"),
            P("section", None, "mp"),
            P("section", "mp"),
            P(),
        ),
        check_vma=False,
    )
```

```python
import functools
import math

import jax
import jax.numpy as jnp
from jax import lax
from jax.experimental import pallas as pl
from jax.experimental.pallas import tpu as pltpu
from jax.sharding import PartitionSpec as P

HEAD_DIM = 80


epsilon = 1e-06
root_half = 0.7071067811865476
density_scale = 0.3989422804014327

MESH = pl.DeviceIdType.MESH
VMEM_LIMIT = 62 * 1024 * 1024
VMEM = pl.BlockSpec(memory_space=pltpu.VMEM)
ANY = pl.BlockSpec(memory_space=pl.ANY)


def upright(row):
    count = row.shape[1]
    across = lax.broadcasted_iota(jnp.int32, (count, count), 1)
    down = lax.broadcasted_iota(jnp.int32, (count, count), 0)
    return jnp.sum(jnp.where(across == down, row, 0), axis=1, keepdims=True)


def same_image(windows):
    across = lax.broadcasted_iota(jnp.int32, (64, 256), 1) // 4
    down = lax.broadcasted_iota(jnp.int32, (64, 256), 0)
    column = upright(windows)
    of_patch = jnp.sum(jnp.where(across == down, column, 0), axis=0, keepdims=True)
    return upright(of_patch) == of_patch


def local_copy(source, target, sem):
    copy = pltpu.make_async_copy(source, target, sem)
    copy.start()
    return copy


class Place:
    def __init__(self):
        dp, self.y, mp = lax.axis_index("dp"), lax.axis_index("section"), lax.axis_index("mp")
        self.z, self.low = dp // 2, dp % 2
        self.high, self.core = mp // 2, mp % 2

    def at(self, z=None, low=None, y=None, high=None, core=None):
        z = self.z if z is None else z
        low = self.low if low is None else low
        y = self.y if y is None else y
        high = self.high if high is None else high
        core = self.core if core is None else core
        return (z * 2 + low, y, high * 2 + core)

    def along_y(self, k):
        return (self.y + k) % 4

    def along_z(self, k):
        return (self.z + k) % 4


def greet(devices):
    barrier = pltpu.get_barrier_semaphore()
    for device in devices:
        pl.semaphore_signal(barrier, inc=1, device_id=device, device_id_type=MESH)
    pl.semaphore_wait(barrier, len(devices))


def send(source, target, sems, index, device):
    copy = pltpu.make_async_remote_copy(
        src_ref=source,
        dst_ref=target,
        send_sem=sems[0].at[index],
        recv_sem=sems[1].at[index],
        device_id=device,
        device_id_type=MESH,
    )
    copy.start()
    return copy


def sem_pair(*shape):
    return [pltpu.SemaphoreType.DMA(shape), pltpu.SemaphoreType.DMA(shape)]


def wide(values):
    return values.astype(jnp.float32)


def low(values):
    return values.astype(jnp.bfloat16)


def root_scale(values):
    return lax.rsqrt(jnp.mean(values * values, axis=-1, keepdims=True) + epsilon)


def norm_backward(cotangent, values, scale, gain):
    weighted = cotangent * gain
    return scale * weighted - values * scale**3 * jnp.mean(
        weighted * values, axis=-1, keepdims=True
    )


def gelu_value(values):
    return 0.5 * values * (1.0 + jax.scipy.special.erf(values * root_half))


def gelu_slope(values):
    return (
        0.5 * (1.0 + jax.scipy.special.erf(values * root_half))
        + values * jnp.exp(-0.5 * values * values) * density_scale
    )


def product(left, right):
    return jnp.dot(left, right, preferred_element_type=jnp.float32)


QUARTER, HALF = 48, 48
ALONE = 320 - 4 * QUARTER - 2 * HALF
UNITS = ((0, 0, 3), (1, 0, 1), (2, 0, 1), (2, 1, 1), (3, 0, 1))
PAIRS = [(j, k) for k in (1, 3, 2) for j in (0, 1)] + [(1, 0)]


STEP = 512


def last_with_last(left, right):
    return lax.dot_general(
        left, right, (((1,), (1,)), ((), ())), preferred_element_type=jnp.float32
    )


def merger_kernel(
    rows_across,
    text,
    merged,
    backs_kept,
    up_kept,
    down_kept,
    sequence,
    gradient,
    backs,
    up,
    down,
    cells_back,
    apart,
    cells,
    pre,
    hidden,
    pre_back,
    hidden_back,
    terms,
    terms_in,
    visual_in,
    visual,
    following,
    pieces,
    pieces_in,
    parts,
    parts_in,
    *sems,
):
    me = Place()
    load, *sems = sems
    merged_s, share_s, dp_s, terms_s, visual_s, pieces_s, parts_s, mp_s = [
        (sems[2 * i], sems[2 * i + 1]) for i in range(8)
    ]
    loads = [
        local_copy(source, target, load.at[i])
        for i, (source, target) in enumerate(
            ((down_kept, down), (backs_kept, backs), (up_kept, up))
        )
    ]
    sibling, partner = me.at(core=1 - me.core), me.at(high=1 - me.high)
    turn = 1 - me.low
    after = me.at(z=(me.z + me.low) % 4, low=turn)
    before = me.at(z=(me.z + 3 + me.low) % 4, low=turn)

    def peer(j, k):
        return me.at(y=me.along_y(k), high=(me.high + j) % 2)

    greet([peer(j, k) for j, k in PAIRS] + [sibling, after, before])
    pending = []

    def go(*arguments):
        copy = send(*arguments)
        pending.append(copy)
        return copy

    half = pl.ds(pl.multiple_of(me.core * 32, 32), 32)
    merged_copies = {
        k: go(merged.at[half], cells.at[me.y, half], merged_s, k, peer(0, k)) for k in (1, 3, 2)
    }
    cells[me.y] = merged[...]
    own = me.high * 2 + me.core
    hidden_back[...] = jnp.zeros_like(hidden_back)
    for copy in loads:
        copy.wait()

    @pl.loop(0, 16)
    def _(i):
        inner = pl.ds(pl.multiple_of((i % 4) * STEP, STEP), STEP)
        outer = pl.ds(pl.multiple_of(i * STEP, STEP), STEP)
        left = backs[:, i // 4, :, inner].reshape(256, STEP)
        hidden_back[...] += last_with_last(left, down[:, outer])

    share_copies = []
    for k in (1, 3, 2):
        merged_copies[k].wait_recv()
        region = cells.at[me.along_y(4 - k), half]
        share_copies.append(go(region, region, share_s, k, sibling))
    for copy in share_copies:
        copy.wait_recv()

    pre[...] = jnp.zeros_like(pre)

    @pl.loop(0, 10)
    def _(i):
        span = pl.ds(pl.multiple_of(i * STEP, STEP), STEP)
        pre[...] += last_with_last(cells[:, :, span].reshape(256, STEP), up[:, span])

    pre_back[...] = low(hidden_back[...] * gelu_slope(pre[...]))

    @pl.loop(0, 10)
    def _(i):
        span = pl.ds(pl.multiple_of(i * STEP, STEP), STEP)
        pieces[:, :, :, :, span] = low(product(pre_back[...], up[:, span])).reshape(4, 2, 2, 16, STEP)

    pieces_copy = go(pieces.at[:, :, 1 - me.core], pieces_in, pieces_s, 0, sibling)
    hidden[...] = low(gelu_value(pre[...]))
    pieces_copy.wait_recv()

    @pl.loop(0, 8)
    def _(i):
        a, b = i // 2, i % 2
        for n in range(4):
            span = pl.ds(n * 1280, 1280)
            parts[a, b, :, span] = low(
                wide(pieces[a, b, me.core, :, span]) + wide(pieces_in[a, b, :, span])
            )

    part_copies = [
        go(parts.at[me.along_y(k), (me.high + j) % 2], parts_in.at[j * 4 + k], parts_s, j * 4 + k, peer(j, k))
        for j, k in PAIRS
    ]

    def term_block(column):
        @pl.loop(0, 4)
        def _(i):
            span = pl.ds(pl.multiple_of(i * STEP, STEP), STEP)
            whole = pl.ds(pl.multiple_of(column * 2048 + i * STEP, STEP), STEP)
            terms[column, :, span] = low(product(hidden[...], down[:, whole]))

    term_copies = []
    for j in (0, 1):
        column = j * 2 + 1 - me.core
        term_block(column)
        term_copies.append(go(terms.at[column], terms_in.at[j], terms_s, j, sibling))
    for j in (0, 1):
        column = j * 2 + me.core
        term_block(column)
        term_copies[j].wait_recv()

        @pl.loop(0, 16)
        def _(i):
            here = pl.ds(pl.multiple_of(i * 16, 16), 16)
            terms[column, here] = low(wide(terms[column, here]) + wide(terms_in[j, here]))

    def visual_region(j, k):
        rows = pl.ds(pl.multiple_of(me.along_y(k) * 64, 64), 64)
        return terms.at[((me.high + j) % 2) * 2 + me.core, rows]

    visual_copies = [
        go(visual_region(j, k), visual_in.at[j * 4 + k], visual_s, j * 4 + k, peer(j, k))
        for j, k in PAIRS
    ]
    for copy in part_copies:
        copy.wait_recv()
    mine = pl.ds(pl.multiple_of(own * 16, 16), 16)
    for n in range(4):
        span = pl.ds(n * 1280, 1280)
        total = wide(parts[me.y, me.high, :, span])
        for j, k in PAIRS:
            total = total + wide(parts_in[j * 4 + k, :, span])
        cells_back[mine, span] = low(total)
    mp_copies = [
        go(cells_back.at[mine], cells_back.at[mine], mp_s, 0, partner),
        go(cells_back.at[mine], cells_back.at[mine], mp_s, 1, sibling),
    ]
    mp_copies[0].wait_recv()
    theirs = pl.ds(pl.multiple_of(((1 - me.high) * 2 + me.core) * 16, 16), 16)
    mp_copies.append(go(cells_back.at[theirs], cells_back.at[theirs], mp_s, 2, sibling))

    for copy in visual_copies:
        copy.wait_recv()
    mine_rows = pl.multiple_of(me.y * 64, 64)

    @pl.loop(0, 4)
    def _(i):
        here = pl.ds(pl.multiple_of(i * 16, 16), 16)
        total = wide(terms[own, pl.ds(pl.multiple_of(mine_rows + i * 16, 16), 16)])
        for j, k in PAIRS:
            total = total + wide(visual_in[j * 4 + k, here])
        visual[here] = low(total)

    visual_copy = go(visual, following, dp_s, 0, before)
    mp_copies[1].wait_recv()
    mp_copies[2].wait_recv()
    for i in range(10):
        for j in range(4):
            there = pl.ds(j * 1280 + i * 128, 128)
            apart[i, pl.ds(j, 64, stride=4), :] = wide(cells_back[:, there])
        gradient[:, i * 128 : (i + 1) * 128] = apart[i]
    slot = lax.broadcasted_iota(jnp.int32, (256, 64), 1)
    rows_down = upright(rows_across[...])
    offset = (me.z * 2 + me.low) * 64
    here_cells = jnp.where(rows_down - offset == slot, 1.0, 0.0).astype(jnp.bfloat16)
    next_cells = jnp.where(rows_down - offset - 64 == slot, 1.0, 0.0).astype(jnp.bfloat16)
    visual_copy.wait_recv()
    for i in range(4):
        span = pl.ds(i * STEP, STEP)
        picked = product(here_cells, visual[:, span]) + product(next_cells, following[:, span])
        sequence[:, span] = jnp.where(rows_down >= 0, low(picked), text[:, span])
    for copy in pending:
        copy.wait_send()


def merger(cell_rows, text, merged, backs, up, down):
    def buffer(*shape):
        return pltpu.VMEM(shape, jnp.bfloat16)

    scratch = [
        buffer(*backs.shape),
        buffer(*up.shape),
        buffer(*down.shape),
        buffer(*merged.shape),
        pltpu.VMEM((10, 256, 128), jnp.float32),
        buffer(4, 64, 5120),
        pltpu.VMEM((256, 320), jnp.float32),
        buffer(256, 320),
        buffer(256, 320),
        pltpu.VMEM((256, 320), jnp.float32),
        buffer(4, 256, 2048),
        buffer(2, 256, 2048),
        buffer(8, 64, 2048),
        buffer(64, 2048),
        buffer(64, 2048),
        buffer(4, 2, 2, 16, 5120),
        buffer(4, 2, 16, 5120),
        buffer(4, 2, 16, 5120),
        buffer(8, 16, 5120),
    ]
    scratch += [pltpu.SemaphoreType.DMA((3,))]
    for size in (4, 4, 1, 2, 8, 1, 8, 3):
        scratch += sem_pair(size)
    return pl.pallas_call(
        merger_kernel,
        out_shape=[
            jax.ShapeDtypeStruct(text.shape, jnp.bfloat16),
            jax.ShapeDtypeStruct((256, 1280), jnp.float32),
        ],
        in_specs=[VMEM] * 3 + [ANY] * 3,
        out_specs=[VMEM] * 2,
        scratch_shapes=scratch,
        compiler_params=pltpu.CompilerParams(
            collective_id=4, has_side_effects=True, vmem_limit_bytes=VMEM_LIMIT
        ),
        name="merger",
    )(cell_rows, text, merged, backs, up, down)


CHUNKS = 4


class SumOverMp:
    def __init__(self, me, go, buffers, sems):
        self.me, self.go = me, go
        self.outgoing, self.got, self.half, self.other, self.total = buffers
        self.sems = sems
        self.sibling, self.partner = me.at(core=1 - me.core), me.at(high=1 - me.high)
        self.mine = pl.multiple_of(me.core * 128, 128)
        self.theirs = pl.multiple_of((1 - me.core) * 128, 128)

    def begin(self, compute):
        step = 128 // CHUNKS
        self.outgoing[...] = low(compute(pl.ds(self.theirs, 128)))
        first = []
        for k in range(CHUNKS):
            here = pl.ds(k * step, step)
            first.append(
                self.go(self.outgoing.at[here], self.got.at[here], self.sems, k, self.sibling)
            )
        self.half[...] = low(compute(pl.ds(self.mine, 128)))
        self.second = []
        for k in range(CHUNKS):
            here = pl.ds(k * step, step)
            first[k].wait_recv()
            self.half[here] = low(wide(self.half[here]) + wide(self.got[here]))
            self.second.append(
                self.go(self.half.at[here], self.other.at[here], self.sems, CHUNKS + k, self.partner)
            )

    def end(self):
        step = 128 // CHUNKS
        third = []
        for k in range(CHUNKS):
            here = pl.ds(k * step, step)
            there = pl.ds(pl.multiple_of(self.mine + k * step, step), step)
            self.second[k].wait_recv()
            self.total[there] = low(wide(self.half[here]) + wide(self.other[here]))
            third.append(
                self.go(
                    self.total.at[there], self.total.at[there], self.sems, 2 * CHUNKS + k, self.sibling
                )
            )
        for copy in third:
            copy.wait_recv()


def sum_buffers():
    half = pltpu.VMEM((128, 1280), jnp.bfloat16)
    return [half, half, half, half, pltpu.VMEM((256, 1280), jnp.bfloat16)]


def head_mask(head):
    lane = lax.broadcasted_iota(jnp.int32, (1, 320), 1)
    inside = (lane >= head * HEAD_DIM) & (lane < (head + 1) * HEAD_DIM)
    return jnp.where(inside, 1.0, 0.0).astype(jnp.bfloat16)


def head_shares(queries, keys, mask, allowed):
    scores = last_with_last(queries * mask, keys) * (1.0 / math.sqrt(HEAD_DIM))
    scores = jnp.where(allowed, scores, -1e30)
    raised = jnp.exp(scores - jnp.max(scores, axis=-1, keepdims=True))
    return raised / jnp.sum(raised, axis=-1, keepdims=True)


def forward_kernel(*refs):
    block_input, windows, gains, merge_gain, rows_across, cotangent = refs[:6]
    shards = refs[6:10]
    kept = refs[10:14]
    attend, projected, heads_out, middle, feed, gate, upper, activated, block_out, merged = refs[14:24]
    backs = refs[24]
    wholes = refs[25:29]
    spill, spill_in, merged_wide = refs[29:32]
    sum_one, sum_two = refs[32:37], refs[37:42]
    own, keep, *pairs = refs[42:]
    y_s, z_s, x_s, one_s, two_s, dp_s, back_s, fore_s = [
        (pairs[2 * i], pairs[2 * i + 1]) for i in range(8)
    ]
    me = Place()
    others = (1, 3, 2)
    y_at = {k: me.at(y=me.along_y(k)) for k in others}
    z_at = {k: me.at(z=me.along_z(k)) for k in others}
    side, sibling = me.at(low=1 - me.low), me.at(core=1 - me.core)
    after = me.at(z=(me.z + me.low) % 4, low=1 - me.low)
    far = me.at(z=(me.z + 3 + 2 * me.low) % 4, low=1 - me.low)

    def peer(j, k):
        return me.at(y=me.along_y(k), high=(me.high + j) % 2)

    greet([peer(j, k) for j, k in PAIRS] + [z_at[k] for k in others] + [side, far, sibling])
    pending = []

    def go(*arguments):
        copy = send(*arguments)
        pending.append(copy)
        return copy

    spans = (
        pl.ds(pl.multiple_of(me.z * QUARTER, 16), QUARTER),
        pl.ds(pl.multiple_of(4 * QUARTER + me.low * HALF, 16), HALF),
        pl.ds(320 - ALONE, ALONE),
    )
    local_copies, first, second = [], {}, {}

    def begin(u):
        t, p, n = UNITS[u]
        for k in others:
            for part in range(3):
                first[u, k, part] = go(
                    shards[t].at[pl.ds(p, n), spans[part]],
                    wholes[t].at[pl.ds(p, n), me.y, spans[part]],
                    y_s,
                    (u * 3 + k - 1) * 3 + part,
                    y_at[k],
                )

    def forward(u):
        t, p, n = UNITS[u]
        copies = []
        for k in others:
            source = me.along_y(4 - k)
            first[u, k, 0].wait_recv()
            block = wholes[t].at[pl.ds(p, n), source, spans[0]]
            for j in others:
                copies.append(go(block, block, z_s, (u * 3 + k - 1) * 3 + j - 1, z_at[j]))
            first[u, k, 1].wait_recv()
            block = wholes[t].at[pl.ds(p, n), source, spans[1]]
            copies.append(go(block, block, x_s, u * 3 + k - 1, side))
            copies.append(first[u, k, 2])
        second[u] = copies

    keeps = []

    def complete(u):
        t, p, n = UNITS[u]
        for copy in second[u]:
            copy.wait_recv()
        planes = pl.ds(p, n)
        keeps.append(local_copy(wholes[t].at[planes], kept[t].at[planes], keep.at[u]))

    def whole(t, p):
        return wholes[t][p].reshape(1280, -1)

    begin(0)
    begin(1)
    for t in range(4):
        local_copies.append(local_copy(shards[t], wholes[t].at[:, me.y], own.at[t]))
    slot = lax.broadcasted_iota(jnp.int32, (128, 256), 0)
    offset = (me.z * 2 + me.low) * 64
    taken = jnp.where(rows_across[...] - offset == slot, 1.0, 0.0).astype(jnp.bfloat16)
    column = me.high * 2 + me.core
    for i in range(4):
        span = pl.ds(i * STEP, STEP)
        arrived = low(product(taken, cotangent[:, span]))
        spill[:, span] = arrived[64:]
        backs[me.y, column, :, span] = arrived[:64]
    spill_copy = go(spill, spill_in, dp_s, 0, after)
    start = wide(block_input[...])
    attend[...] = low(start * root_scale(start) * gains[0:1])
    forward(0)
    begin(2)
    forward(1)
    begin(3)
    for copy in local_copies:
        copy.wait()
    complete(0)
    for p in range(3):
        projected[p] = low(product(attend[...], whole(0, p)))
    forward(2)
    begin(4)
    allowed = same_image(windows[...])
    mixed = jnp.zeros((256, 320), jnp.float32)
    for head in range(4):
        mask = head_mask(head)
        shares = head_shares(projected[0], projected[1], mask, allowed)
        mixed = mixed + product(low(shares), projected[2] * mask)
    heads_out[...] = low(mixed)
    complete(1)
    forward(3)
    total = SumOverMp(me, go, sum_one, one_s)
    total.begin(lambda rows: last_with_last(heads_out[rows], whole(1, 0)))
    spill_copy.wait_recv()
    for i in range(4):
        span = pl.ds(i * STEP, STEP)
        backs[me.y, column, :, span] = backs[me.y, column, :, span] + spill_in[:, span]
    forward(4)
    total.end()
    block = backs.at[me.y, column]
    back_copies = [go(block, block, back_s, j * 4 + k, peer(j, k)) for j, k in PAIRS]
    fore_copies = [go(block, block, fore_s, 0, sibling)]
    middle[...] = wide(block_input[...]) + wide(sum_one[4][...])
    feed[...] = low(middle[...] * root_scale(middle[...]) * gains[1:2])
    complete(2)
    gate[...] = product(feed[...], whole(2, 0))
    complete(3)
    upper[...] = product(feed[...], whole(2, 1))
    activated[...] = low(gate[...] * jax.nn.sigmoid(gate[...]) * upper[...])
    complete(4)
    total = SumOverMp(me, go, sum_two, two_s)
    total.begin(lambda rows: last_with_last(activated[rows], whole(3, 0)))
    for (j, k), copy in zip(PAIRS, back_copies):
        copy.wait_recv()
        region = backs.at[me.along_y((4 - k) % 4), ((me.high + j) % 2) * 2 + me.core]
        fore_copies.append(go(region, region, fore_s, j * 4 + k, sibling))
    total.end()
    block_out[...] = middle[...] + wide(sum_two[4][...])
    scale_three = root_scale(block_out[...])
    for i in range(10):
        span = slice(i * 128, (i + 1) * 128)
        merged_wide[i] = block_out[:, span] * scale_three * merge_gain[:, span]
        for j in range(4):
            there = pl.ds(j * 1280 + i * 128, 128)
            merged[:, there] = low(merged_wide[i, pl.ds(j, 64, stride=4), :])
    for copy in fore_copies:
        copy.wait_recv()
    for copy in keeps:
        copy.wait()
    for copy in pending:
        copy.wait_send()


def block_forward(block_input, windows, gains, merge_gain, cell_rows, cotangent, shards):
    rows, width = block_input.shape
    units = shards[2].shape[2]

    def shape(kind, *dims):
        return jax.ShapeDtypeStruct(dims, kind)

    low_, wide_ = jnp.bfloat16, jnp.float32
    outs = [shape(low_, s.shape[0], 4, *s.shape[1:]) for s in shards] + [
        shape(low_, rows, width),
        shape(low_, 3, rows, 320),
        shape(low_, rows, 320),
        shape(wide_, rows, width),
        shape(low_, rows, width),
        shape(wide_, rows, units),
        shape(wide_, rows, units),
        shape(low_, rows, units),
        shape(wide_, rows, width),
        shape(low_, rows // 4, 4 * width),
        shape(low_, 4, 4, 64, cotangent.shape[1]),
    ]
    spill = pltpu.VMEM((64, cotangent.shape[1]), jnp.bfloat16)
    scratch = [pltpu.VMEM(out.shape, jnp.bfloat16) for out in outs[:4]]
    scratch += [spill, spill, pltpu.VMEM((10, rows, 128), jnp.float32)]
    scratch += sum_buffers() + sum_buffers()
    scratch += [pltpu.SemaphoreType.DMA((4,)), pltpu.SemaphoreType.DMA((len(UNITS),))]
    for size in (45, 45, 15, 3 * CHUNKS, 3 * CHUNKS, 1, 8, 8):
        scratch += sem_pair(size)
    results = pl.pallas_call(
        forward_kernel,
        out_shape=outs,
        in_specs=[VMEM] * 10,
        out_specs=[ANY] * 4 + [VMEM] * (len(outs) - 4),
        scratch_shapes=scratch,
        compiler_params=pltpu.CompilerParams(
            collective_id=1, has_side_effects=True, vmem_limit_bytes=VMEM_LIMIT
        ),
        name="block_forward",
    )(
        block_input,
        windows,
        gains,
        merge_gain[None],
        cell_rows,
        cotangent,
        *shards,
    )
    return results[:4], results[4:14], results[14]


A_ROWS = 192
A_PART = A_ROWS // 4
B_PART = (320 - A_ROWS) // 4
E_ROWS = A_PART + B_PART
A_HALF, B_HALF = A_ROWS // 2, B_PART // 2
E_TOP = 48
TILE = 16
ORDER = (1, 3, 2)


def over_rows(planes, rows, body):
    tiles = rows // TILE

    @pl.loop(0, planes * tiles)
    def _(i):
        body(i // tiles, pl.multiple_of((i % tiles) * TILE, TILE))


class Reduction:
    def __init__(self, me, go, term, final, buffers, sems, index, y_at, z_at, side):
        self.me, self.go, self.term, self.final = me, go, term, final
        self.ya, self.fy, self.sa, self.za, self.zb, self.fz, self.sb, self.yb, self.ee, self.ex = buffers
        self.sems, self.index, self.y_at, self.z_at, self.side = sems, index, y_at, z_at, side
        self.planes = term.shape[0]
        self.relayed = index >= 2

    def stage_one(self):
        me, term, go, ya, zb = self.me, self.term, self.go, self.ya, self.zb
        top, bottom = pl.ds(0, A_HALF), pl.ds(A_HALF, A_HALF)
        at = self.index * 6

        def a_rows(k, span):
            return term.at[:, me.along_y(k), span]

        def b_rows(k, half):
            first = A_ROWS + me.along_z(k) * B_PART + half * B_HALF
            return term.at[:, :, pl.ds(pl.multiple_of(first, TILE), B_HALF)]

        up, down = self.y_at[1], self.y_at[3]
        sems = self.sems[0]
        self.far_a = [
            go(a_rows(2, top), self.fy.at[0], sems, at, up),
            go(a_rows(2, bottom), self.fy.at[1], sems, at + 1, down),
        ]
        up_z, down_z = self.z_at[1], self.z_at[3]
        sems_z = self.sems[1]
        self.far_b = [
            go(b_rows(2, 0), self.fz.at[0], sems_z, at, up_z),
            go(b_rows(2, 1), self.fz.at[1], sems_z, at + 1, down_z),
        ]
        self.first_a = [
            go(a_rows(1, bottom), ya.at[0, :, bottom], sems, at + 2, up),
            go(a_rows(3, top), ya.at[1, :, top], sems, at + 3, down),
        ]
        b_top, b_bottom = pl.ds(0, B_HALF), pl.ds(B_HALF, B_HALF)
        self.first_b = [
            go(b_rows(1, 1), zb.at[0, :, :, b_bottom], sems_z, at + 2, up_z),
            go(b_rows(3, 0), zb.at[1, :, :, b_top], sems_z, at + 3, down_z),
        ]

    def stage_half(self):
        me, term, go, fy, fz = self.me, self.term, self.go, self.fy, self.fz
        at = self.index * 6
        for copy in self.far_b + self.far_a:
            copy.wait_recv()

        def add_b(i, r):
            p, q = i // 4, i % 4
            here = pl.ds(r, TILE)
            first = pl.multiple_of(A_ROWS + me.along_z(1) * B_PART + r, TILE)
            fz[0, p, q, here] = low(wide(fz[0, p, q, here]) + wide(term[p, q, pl.ds(first, TILE)]))
            first = pl.multiple_of(A_ROWS + me.along_z(3) * B_PART + B_HALF + r, TILE)
            fz[1, p, q, here] = low(wide(fz[1, p, q, here]) + wide(term[p, q, pl.ds(first, TILE)]))

        def add_a(p, r):
            here = pl.ds(r, TILE)
            there = pl.ds(pl.multiple_of(A_HALF + r, TILE), TILE)
            fy[0, p, here] = low(wide(fy[0, p, here]) + wide(term[p, me.along_y(1), here]))
            fy[1, p, here] = low(wide(fy[1, p, here]) + wide(term[p, me.along_y(3), there]))

        over_rows(self.planes * 4, B_HALF, add_b)
        over_rows(self.planes, A_HALF, add_a)
        top, bottom = pl.ds(0, A_HALF), pl.ds(A_HALF, A_HALF)
        b_top, b_bottom = pl.ds(0, B_HALF), pl.ds(B_HALF, B_HALF)
        ya, zb = self.ya, self.zb
        self.first_b += [
            go(fz.at[0], zb.at[0, :, :, b_top], self.sems[1], at + 4, self.z_at[1]),
            go(fz.at[1], zb.at[1, :, :, b_bottom], self.sems[1], at + 5, self.z_at[3]),
        ]
        self.first_a += [
            go(fy.at[0], ya.at[0, :, top], self.sems[0], at + 4, self.y_at[1]),
            go(fy.at[1], ya.at[1, :, bottom], self.sems[0], at + 5, self.y_at[3]),
        ]

    def stage_two(self):
        me, term, ya, sa, zb, sb = self.me, self.term, self.ya, self.sa, self.zb, self.sb
        for copy in self.first_b:
            copy.wait_recv()

        def add_b(i, r):
            p, q = i // 4, i % 4
            here = pl.ds(r, TILE)
            there = pl.ds(pl.multiple_of(A_ROWS + me.z * B_PART + r, TILE), TILE)
            sb[p, q, here] = low(
                wide(term[p, q, there]) + wide(zb[0, p, q, here]) + wide(zb[1, p, q, here])
            )

        over_rows(self.planes * 4, B_PART, add_b)
        self.second = [
            self.go(
                sb.at[:, me.along_y(k)],
                self.yb.at[k - 1],
                self.sems[2],
                self.index * 3 + k - 1,
                self.y_at[k],
            )
            for k in ORDER
        ]
        for copy in self.first_a:
            copy.wait_recv()

        def add_a(p, r):
            here = pl.ds(r, TILE)
            sa[p, here] = low(
                wide(term[p, me.y, here]) + wide(ya[0, p, here]) + wide(ya[1, p, here])
            )

        over_rows(self.planes, A_ROWS, add_a)
        self.second += [
            self.go(
                sa.at[:, pl.ds(pl.multiple_of(me.along_z(k) * A_PART, TILE), A_PART)],
                self.za.at[k - 1],
                self.sems[3],
                self.index * 3 + k - 1,
                self.z_at[k],
            )
            for k in ORDER
        ]

    def stage_three(self):
        me, sa, za, sb, yb, ee = self.me, self.sa, self.za, self.sb, self.yb, self.ee
        for copy in self.second:
            copy.wait_recv()

        def add_a(p, r):
            here = pl.ds(r, TILE)
            there = pl.ds(pl.multiple_of(me.z * A_PART + r, TILE), TILE)
            ee[p, here] = low(
                wide(sa[p, there]) + wide(za[0, p, here]) + wide(za[1, p, here]) + wide(za[2, p, here])
            )

        def add_b(p, r):
            here = pl.ds(r, TILE)
            there = pl.ds(pl.multiple_of(A_PART + r, TILE), TILE)
            ee[p, there] = low(
                wide(sb[p, me.y, here])
                + wide(yb[0, p, here])
                + wide(yb[1, p, here])
                + wide(yb[2, p, here])
            )

        over_rows(self.planes, A_PART, add_a)
        over_rows(self.planes, B_PART, add_b)
        self.third = self.go(ee, self.ex, self.sems[4], self.index, self.side)

    def owned(self, source):
        return source % 2, (source // 2) * (A_ROWS // 2)

    def stage_four(self):
        me, ya, ee, ex = self.me, self.ya, self.ee, self.ex
        self.third.wait_recv()
        slot, base = self.owned(me.z)

        def add(p, r):
            there = pl.ds(pl.multiple_of(base + r, TILE), TILE)
            here = pl.ds(r, TILE)
            ya[slot, p, there] = low(wide(ee[p, here]) + wide(ex[p, here]))

        over_rows(self.planes, E_ROWS, add)
        mine = self.piece(0, 0, E_ROWS)
        at = self.index * 4
        near = (1, 3) if self.relayed else ORDER
        self.fourth = {k: self.go(mine, mine, self.sems[5], at + k - 1, self.z_at[k]) for k in near}

    def piece(self, k, start, rows):
        slot, base = self.owned(self.me.along_z(k))
        return self.ya.at[slot, :, pl.ds(pl.multiple_of(base + start, TILE), rows)]

    def relay(self):
        if not self.relayed:
            return
        at = self.index * 4
        self.fourth[1].wait_recv()
        piece = self.piece(3, 0, E_TOP)
        self.fourth[2] = self.go(piece, piece, self.sems[5], at + 1, self.z_at[1])
        self.fourth[3].wait_recv()
        piece = self.piece(1, E_TOP, E_ROWS - E_TOP)
        self.fourth[4] = self.go(piece, piece, self.sems[5], at + 3, self.z_at[3])

    def finish(self):
        me, ya, final = self.me, self.ya, self.final
        for k in (0,) + ORDER:
            if k == 2 and self.relayed:
                self.fourth[2].wait_recv()
                self.fourth[4].wait_recv()
            elif k and not self.relayed:
                self.fourth[k].wait_recv()
            source = me.along_z((4 - k) % 4)
            slot, base = self.owned(source)

            def put_a(p, r):
                there = pl.ds(pl.multiple_of(source * A_PART + r, TILE), TILE)
                here = pl.ds(pl.multiple_of(base + r, TILE), TILE)
                final[p, there] = wide(ya[slot, p, here])

            def put_b(p, r):
                there = pl.ds(pl.multiple_of(A_ROWS + source * B_PART + r, TILE), TILE)
                here = pl.ds(pl.multiple_of(base + A_PART + r, TILE), TILE)
                final[p, there] = wide(ya[slot, p, here])

            over_rows(self.planes, A_PART, put_a)
            over_rows(self.planes, B_PART, put_b)


def first_with_first(left, right):
    return lax.dot_general(
        left, right, (((0,), (0,)), ((), ())), preferred_element_type=jnp.float32
    )


def backward_kernel(*refs):
    (
        block_input,
        windows,
        gains,
        merge_gain,
        cells_back,
        triple_kept,
        output_kept,
        gate_up_kept,
        down_kept,
        attend,
        projected,
        heads_out,
        middle,
        feed,
        gate,
        upper,
        activated,
        block_out,
    ) = refs[:18]
    input_gradient = refs[18]
    outs = refs[19:24]
    gain_out = refs[24]
    refs = refs[25:]
    triple, output, gate_up, down, load = refs[:5]
    refs = refs[5:]
    sum_one, sum_two = refs[:5], refs[5:10]
    terms = refs[10:15]
    buffers = [refs[15 + 10 * t : 25 + 10 * t] for t in range(5)]
    middle_back, middle_low, out_low, gate_up_back, triple_back, gain, gain_in, gain_sum = refs[65:73]
    sems = refs[73:]
    pair = [(sems[2 * i], sems[2 * i + 1]) for i in range(9)]
    loads = [
        local_copy(source, target, load.at[i])
        for i, (source, target) in enumerate(
            ((down_kept, down), (gate_up_kept, gate_up), (output_kept, output), (triple_kept, triple))
        )
    ]
    me = Place()
    y_at = {k: me.at(y=me.along_y(k)) for k in ORDER}
    z_at = {k: me.at(z=me.along_z(k)) for k in ORDER}
    side = me.at(low=1 - me.low)
    greet(
        [y_at[k] for k in ORDER]
        + [z_at[k] for k in ORDER]
        + [side, me.at(core=1 - me.core), me.at(high=1 - me.high)]
    )
    pending = []

    def go(*arguments):
        copy = send(*arguments)
        pending.append(copy)
        return copy

    reductions = [
        Reduction(me, go, terms[t], outs[t], buffers[t], pair[:6], t, y_at, z_at, side)
        for t in range(5)
    ]
    of_triple, of_output, of_gate, of_upper, of_down = reductions

    def form(t, p, left, right):
        for i in range(2):
            block = first_with_first(left[:, i * 640 : (i + 1) * 640], right)
            terms[t][p, 2 * i : 2 * i + 2] = low(block).reshape(2, 320, right.shape[1])

    def whole(weight, p):
        return weight[p].reshape(1280, -1)

    scale_three = root_scale(block_out[...])
    out_back = norm_backward(cells_back[...], block_out[...], scale_three, merge_gain[...])
    middle_back[...] = out_back
    out_low[...] = low(out_back)
    form(4, 0, out_low, activated[...])
    of_down.stage_one()
    for copy in loads:
        copy.wait()
    activated_back = product(out_low[...], whole(down, 0))
    slope = jax.nn.sigmoid(gate[...])
    gate_up_back[1] = low(activated_back * gate[...] * slope)
    gate_up_back[0] = low(activated_back * upper[...] * slope * (1.0 + gate[...] * (1.0 - slope)))
    total = SumOverMp(me, go, sum_one, pair[6])
    total.begin(
        lambda rows: last_with_last(gate_up_back[0, rows], whole(gate_up, 0))
        + last_with_last(gate_up_back[1, rows], whole(gate_up, 1))
    )
    form(2, 0, feed, gate_up_back[0])
    of_gate.stage_one()
    of_down.stage_half()
    total.end()
    feed_back = wide(sum_one[4][...])
    scale_two = root_scale(middle[...])
    middle_back[...] = middle_back[...] + norm_backward(
        feed_back, middle[...], scale_two, gains[1:2]
    )
    middle_low[...] = low(middle_back[...])
    gain[...] = jnp.zeros_like(gain)
    gain[1:2] = jnp.sum(feed_back * middle[...] * scale_two, axis=0, keepdims=True)
    form(3, 0, feed, gate_up_back[1])
    of_upper.stage_one()
    of_gate.stage_half()
    heads_back = low(product(middle_low[...], whole(output, 0)))
    allowed = same_image(windows[...])
    query_back = jnp.zeros((256, 320), jnp.float32)
    key_back = jnp.zeros((256, 320), jnp.float32)
    value_back = jnp.zeros((256, 320), jnp.float32)
    for head in range(4):
        mask = head_mask(head)
        shares = head_shares(projected[0], projected[1], mask, allowed)
        share_back = last_with_last(heads_back * mask, projected[2])
        centre = jnp.sum(shares * share_back, axis=-1, keepdims=True)
        score_back = low(shares * (share_back - centre) * (1.0 / math.sqrt(HEAD_DIM)))
        query_back = query_back + product(score_back, projected[1] * mask)
        key_back = key_back + first_with_first(score_back, projected[0] * mask)
        value_back = value_back + first_with_first(low(shares), heads_back * mask)
    triple_back[0] = low(query_back)
    triple_back[1] = low(key_back)
    triple_back[2] = low(value_back)
    for p in range(3):
        form(0, p, attend, triple_back[p])
    of_triple.stage_one()
    form(1, 0, middle_low, heads_out[...])
    of_output.stage_one()
    of_upper.stage_half()
    of_down.stage_two()
    total = SumOverMp(me, go, sum_two, pair[7])
    total.begin(
        lambda rows: last_with_last(triple_back[0, rows], whole(triple, 0))
        + last_with_last(triple_back[1, rows], whole(triple, 1))
        + last_with_last(triple_back[2, rows], whole(triple, 2))
    )
    of_triple.stage_half()
    of_gate.stage_two()
    total.end()
    attend_back = wide(sum_two[4][...])
    start = wide(block_input[...])
    scale_one = root_scale(start)
    input_gradient[...] = middle_back[...] + norm_backward(attend_back, start, scale_one, gains[0:1])
    gain[0:1] = jnp.sum(attend_back * start * scale_one, axis=0, keepdims=True)
    gain_copies = [go(gain, gain_in.at[k - 1], pair[8], k - 1, y_at[k]) for k in ORDER]
    of_down.stage_three()
    of_output.stage_half()
    of_upper.stage_two()
    of_gate.stage_three()
    of_down.stage_four()
    for copy in gain_copies:
        copy.wait_recv()
    gain_sum[0] = gain[...] + gain_in[0] + gain_in[1] + gain_in[2]
    gain_copies = [go(gain_sum.at[0], gain_in.at[2 + k], pair[8], 2 + k, z_at[k]) for k in ORDER]
    of_triple.stage_two()
    of_upper.stage_three()
    of_gate.stage_four()
    of_down.relay()
    of_output.stage_two()
    for copy in gain_copies:
        copy.wait_recv()
    gain_sum[1] = gain_sum[0] + gain_in[3] + gain_in[4] + gain_in[5]
    gain_copies = [go(gain_sum.at[1], gain_in.at[6], pair[8], 6, side)]
    of_triple.stage_three()
    of_upper.stage_four()
    of_gate.relay()
    of_output.stage_three()
    for copy in gain_copies:
        copy.wait_recv()
    gain_out[...] = gain_sum[1] + gain_in[6]
    of_triple.stage_four()
    of_upper.relay()
    of_output.stage_four()
    for reduction in (of_down, of_gate, of_upper, of_triple, of_output):
        reduction.finish()
    for copy in pending:
        copy.wait_send()


def block_backward(block_input, windows, gains, merge_gain, cells_back, wholes, saved):
    rows, width = block_input.shape
    units = saved[5].shape[1]

    def low_buffer(*shape):
        return pltpu.VMEM(shape, jnp.bfloat16)

    def wide_buffer(*shape):
        return pltpu.VMEM(shape, jnp.float32)

    sizes = ((3, 320), (1, 320), (1, units), (1, units), (1, units))
    scratch = [low_buffer(*whole.shape) for whole in wholes]
    scratch += [pltpu.SemaphoreType.DMA((4,))]
    scratch += sum_buffers() + sum_buffers()
    scratch += [low_buffer(planes, 4, 320, columns) for planes, columns in sizes]
    for planes, columns in sizes:
        scratch += [
            low_buffer(2, planes, A_ROWS, columns),
            low_buffer(2, planes, A_HALF, columns),
            low_buffer(planes, A_ROWS, columns),
            low_buffer(3, planes, A_PART, columns),
            low_buffer(2, planes, 4, B_PART, columns),
            low_buffer(2, planes, 4, B_HALF, columns),
            low_buffer(planes, 4, B_PART, columns),
            low_buffer(3, planes, B_PART, columns),
            low_buffer(planes, E_ROWS, columns),
            low_buffer(planes, E_ROWS, columns),
        ]
    scratch += [
        wide_buffer(rows, width),
        low_buffer(rows, width),
        low_buffer(rows, width),
        low_buffer(2, rows, units),
        low_buffer(3, rows, 320),
        wide_buffer(8, width),
        wide_buffer(7, 8, width),
        wide_buffer(2, 8, width),
    ]
    for size in (30, 30, 15, 15, 5, 20, 3 * CHUNKS, 3 * CHUNKS, 7):
        scratch += sem_pair(size)
    operands = [
        block_input,
        windows,
        gains,
        merge_gain[None],
        cells_back,
        *wholes,
        *saved,
    ]
    outs = (
        [jax.ShapeDtypeStruct((rows, width), jnp.float32)]
        + [
            jax.ShapeDtypeStruct((planes, 320, columns), jnp.float32) for planes, columns in sizes
        ]
        + [jax.ShapeDtypeStruct((8, width), jnp.float32)]
    )
    results = pl.pallas_call(
        backward_kernel,
        out_shape=outs,
        in_specs=[VMEM] * 5 + [ANY] * 4 + [VMEM] * (len(operands) - 9),
        out_specs=[VMEM] * len(outs),
        scratch_shapes=scratch,
        compiler_params=pltpu.CompilerParams(
            collective_id=3, has_side_effects=True, vmem_limit_bytes=VMEM_LIMIT
        ),
        name="block_backward",
    )(*operands)

    gradients = results[1:6]
    return results[0], gradients, results[6][:2]


def planes_of(weight):
    return jnp.transpose(weight, (1, 0, 2))


def local(
    block_input,
    windows,
    cell_rows,
    text_vectors,
    sequence_cotangent,
    norm_gains,
    merge_gain,
    triple_weight,
    output_weight,
    gate_up_weight,
    down_weight,
    merge_up,
    merge_down,
):
    patches = block_input[0]
    shards = (
        planes_of(triple_weight),
        output_weight[None],
        planes_of(gate_up_weight),
        down_weight[None],
    )
    wholes, saved, backs = block_forward(
        patches,
        windows,
        norm_gains,
        merge_gain,
        cell_rows,
        sequence_cotangent[0],
        shards,
    )
    sequence, cells_back = merger(
        cell_rows,
        text_vectors[0],
        saved[-1],
        backs,
        merge_up.T,
        merge_down,
    )
    input_gradient, gradients, gain_gradient = block_backward(
        patches,
        windows,
        norm_gains,
        merge_gain,
        cells_back,
        wholes,
        saved[:-1],
    )
    return (
        sequence[None],
        input_gradient[None],
        planes_of(gradients[0]),
        gradients[1][0],
        jnp.stack([gradients[2][0], gradients[3][0]], axis=1),
        gradients[4][0],
        gain_gradient,
    )


def solution(mesh):
    placed = (
        P(("dp", "section"), None, None),
        P(("dp", "section"), None),
        P("section", "dp"),
        P("section", "dp", "mp"),
        P("section", "dp", "mp"),
        P(),
        P(),
        P("section", None, "mp"),
        P("section", "mp"),
        P("section", None, "mp"),
        P("section", "mp"),
        P(None, ("section", "mp")),
        P(("section", "mp"), None),
    )
    return jax.shard_map(
        local,
        mesh=mesh,
        in_specs=placed,
        out_specs=(
            P("section", "dp", "mp"),
            P(("dp", "section"), None, None),
            P("section", None, "mp"),
            P("section", "mp"),
            P("section", None, "mp"),
            P("section", "mp"),
            P(),
        ),
        check_vma=False,
    )
```

```python
import functools
import math

import jax
import jax.numpy as jnp
from jax import lax
from jax.experimental import pallas as pl
from jax.experimental.pallas import tpu as pltpu
from jax.sharding import PartitionSpec as P

HEAD_DIM = 80


epsilon = 1e-06
root_half = 0.7071067811865476
density_scale = 0.3989422804014327

MESH = pl.DeviceIdType.MESH
VMEM_LIMIT = 62 * 1024 * 1024
VMEM = pl.BlockSpec(memory_space=pltpu.VMEM)
ANY = pl.BlockSpec(memory_space=pl.ANY)


def upright(row):
    count = row.shape[1]
    across = lax.broadcasted_iota(jnp.int32, (count, count), 1)
    down = lax.broadcasted_iota(jnp.int32, (count, count), 0)
    return jnp.sum(jnp.where(across == down, row, 0), axis=1, keepdims=True)


def same_image(windows):
    across = lax.broadcasted_iota(jnp.int32, (64, 256), 1) // 4
    down = lax.broadcasted_iota(jnp.int32, (64, 256), 0)
    column = upright(windows)
    of_patch = jnp.sum(jnp.where(across == down, column, 0), axis=0, keepdims=True)
    return upright(of_patch) == of_patch


def local_copy(source, target, sem):
    copy = pltpu.make_async_copy(source, target, sem)
    copy.start()
    return copy


class Place:
    def __init__(self):
        dp, self.y, mp = lax.axis_index("dp"), lax.axis_index("section"), lax.axis_index("mp")
        self.z, self.low = dp // 2, dp % 2
        self.high, self.core = mp // 2, mp % 2

    def at(self, z=None, low=None, y=None, high=None, core=None):
        z = self.z if z is None else z
        low = self.low if low is None else low
        y = self.y if y is None else y
        high = self.high if high is None else high
        core = self.core if core is None else core
        return (z * 2 + low, y, high * 2 + core)

    def along_y(self, k):
        return (self.y + k) % 4

    def along_z(self, k):
        return (self.z + k) % 4


def greet(devices):
    barrier = pltpu.get_barrier_semaphore()
    for device in devices:
        pl.semaphore_signal(barrier, inc=1, device_id=device, device_id_type=MESH)
    pl.semaphore_wait(barrier, len(devices))


def send(source, target, sems, index, device):
    copy = pltpu.make_async_remote_copy(
        src_ref=source,
        dst_ref=target,
        send_sem=sems[0].at[index],
        recv_sem=sems[1].at[index],
        device_id=device,
        device_id_type=MESH,
    )
    copy.start()
    return copy


def sem_pair(*shape):
    return [pltpu.SemaphoreType.DMA(shape), pltpu.SemaphoreType.DMA(shape)]


def wide(values):
    return values.astype(jnp.float32)


def low(values):
    return values.astype(jnp.bfloat16)


def root_scale(values):
    return lax.rsqrt(jnp.mean(values * values, axis=-1, keepdims=True) + epsilon)


def norm_backward(cotangent, values, scale, gain):
    weighted = cotangent * gain
    return scale * weighted - values * scale**3 * jnp.mean(
        weighted * values, axis=-1, keepdims=True
    )


def gelu_value(values):
    return 0.5 * values * (1.0 + jax.scipy.special.erf(values * root_half))


def gelu_slope(values):
    return (
        0.5 * (1.0 + jax.scipy.special.erf(values * root_half))
        + values * jnp.exp(-0.5 * values * values) * density_scale
    )


def product(left, right):
    return jnp.dot(left, right, preferred_element_type=jnp.float32)


QUARTER, HALF = 48, 48
ALONE = 320 - 4 * QUARTER - 2 * HALF
UNITS = ((0, 0, 3), (1, 0, 1), (2, 0, 1), (2, 1, 1), (3, 0, 1))
SHARE_Z = ({1: (0, 16), 3: (16, 32)}, {1: (0, 32), 3: (32, 16)})
SHARE = ({1: (0, 32), 3: (32, 16)}, {1: (0, 16), 3: (16, 32)}, {1: (0, 16), 3: (16, 16)})
PAIRS = [(j, k) for k in (1, 3, 2) for j in (0, 1)] + [(1, 0)]


STEP = 512


def last_with_last(left, right):
    return lax.dot_general(
        left, right, (((1,), (1,)), ((), ())), preferred_element_type=jnp.float32
    )


def merger_kernel(
    rows_across,
    text,
    merged,
    backs_kept,
    up_kept,
    down_kept,
    sequence,
    gradient,
    backs,
    up,
    down,
    cells_back,
    apart,
    cells,
    pre,
    hidden,
    pre_back,
    hidden_back,
    terms,
    terms_in,
    visual_in,
    visual,
    following,
    pieces,
    pieces_in,
    parts,
    parts_in,
    *sems,
):
    me = Place()
    load, *sems = sems
    merged_s, share_s, dp_s, terms_s, visual_s, pieces_s, parts_s, mp_s = [
        (sems[2 * i], sems[2 * i + 1]) for i in range(8)
    ]
    loads = [
        local_copy(source, target, load.at[i])
        for i, (source, target) in enumerate(
            ((down_kept, down), (backs_kept, backs), (up_kept, up))
        )
    ]
    sibling, partner = me.at(core=1 - me.core), me.at(high=1 - me.high)
    turn = 1 - me.low
    after = me.at(z=(me.z + me.low) % 4, low=turn)
    before = me.at(z=(me.z + 3 + me.low) % 4, low=turn)

    def peer(j, k):
        return me.at(y=me.along_y(k), high=(me.high + j) % 2)

    greet([peer(j, k) for j, k in PAIRS] + [sibling, after, before])
    pending = []

    def go(*arguments):
        copy = send(*arguments)
        pending.append(copy)
        return copy

    half = pl.ds(pl.multiple_of(me.core * 32, 32), 32)
    merged_copies = {
        k: go(merged.at[half], cells.at[me.y, half], merged_s, k, peer(0, k)) for k in (1, 3, 2)
    }
    cells[me.y] = merged[...]
    own = me.high * 2 + me.core
    hidden_back[...] = jnp.zeros_like(hidden_back)
    for copy in loads:
        copy.wait()

    @pl.loop(0, 16)
    def _(i):
        inner = pl.ds(pl.multiple_of((i % 4) * STEP, STEP), STEP)
        outer = pl.ds(pl.multiple_of(i * STEP, STEP), STEP)
        left = backs[:, i // 4, :, inner].reshape(256, STEP)
        hidden_back[...] += last_with_last(left, down[:, outer])

    share_copies = []
    for k in (1, 3, 2):
        merged_copies[k].wait_recv()
        region = cells.at[me.along_y(4 - k), half]
        share_copies.append(go(region, region, share_s, k, sibling))
    for copy in share_copies:
        copy.wait_recv()

    pre[...] = jnp.zeros_like(pre)

    @pl.loop(0, 10)
    def _(i):
        span = pl.ds(pl.multiple_of(i * STEP, STEP), STEP)
        pre[...] += last_with_last(cells[:, :, span].reshape(256, STEP), up[:, span])

    pre_back[...] = low(hidden_back[...] * gelu_slope(pre[...]))

    @pl.loop(0, 10)
    def _(i):
        span = pl.ds(pl.multiple_of(i * STEP, STEP), STEP)
        pieces[:, :, :, :, span] = low(product(pre_back[...], up[:, span])).reshape(4, 2, 2, 16, STEP)

    pieces_copy = go(pieces.at[:, :, 1 - me.core], pieces_in, pieces_s, 0, sibling)
    hidden[...] = low(gelu_value(pre[...]))
    pieces_copy.wait_recv()

    @pl.loop(0, 8)
    def _(i):
        a, b = i // 2, i % 2
        for n in range(4):
            span = pl.ds(n * 1280, 1280)
            parts[a, b, :, span] = low(
                wide(pieces[a, b, me.core, :, span]) + wide(pieces_in[a, b, :, span])
            )

    part_copies = [
        go(parts.at[me.along_y(k), (me.high + j) % 2], parts_in.at[j * 4 + k], parts_s, j * 4 + k, peer(j, k))
        for j, k in PAIRS
    ]

    def term_block(column):
        @pl.loop(0, 4)
        def _(i):
            span = pl.ds(pl.multiple_of(i * STEP, STEP), STEP)
            whole = pl.ds(pl.multiple_of(column * 2048 + i * STEP, STEP), STEP)
            terms[column, :, span] = low(product(hidden[...], down[:, whole]))

    term_copies = []
    for j in (0, 1):
        column = j * 2 + 1 - me.core
        term_block(column)
        term_copies.append(go(terms.at[column], terms_in.at[j], terms_s, j, sibling))
    for j in (0, 1):
        column = j * 2 + me.core
        term_block(column)
        term_copies[j].wait_recv()

        @pl.loop(0, 16)
        def _(i):
            here = pl.ds(pl.multiple_of(i * 16, 16), 16)
            terms[column, here] = low(wide(terms[column, here]) + wide(terms_in[j, here]))

    def visual_region(j, k):
        rows = pl.ds(pl.multiple_of(me.along_y(k) * 64, 64), 64)
        return terms.at[((me.high + j) % 2) * 2 + me.core, rows]

    visual_copies = [
        go(visual_region(j, k), visual_in.at[j * 4 + k], visual_s, j * 4 + k, peer(j, k))
        for j, k in PAIRS
    ]
    for copy in part_copies:
        copy.wait_recv()
    mine = pl.ds(pl.multiple_of(own * 16, 16), 16)
    for n in range(4):
        span = pl.ds(n * 1280, 1280)
        total = wide(parts[me.y, me.high, :, span])
        for j, k in PAIRS:
            total = total + wide(parts_in[j * 4 + k, :, span])
        cells_back[mine, span] = low(total)
    mp_copies = [
        go(cells_back.at[mine], cells_back.at[mine], mp_s, 0, partner),
        go(cells_back.at[mine], cells_back.at[mine], mp_s, 1, sibling),
    ]
    mp_copies[0].wait_recv()
    theirs = pl.ds(pl.multiple_of(((1 - me.high) * 2 + me.core) * 16, 16), 16)
    mp_copies.append(go(cells_back.at[theirs], cells_back.at[theirs], mp_s, 2, sibling))

    for copy in visual_copies:
        copy.wait_recv()
    mine_rows = pl.multiple_of(me.y * 64, 64)

    @pl.loop(0, 4)
    def _(i):
        here = pl.ds(pl.multiple_of(i * 16, 16), 16)
        total = wide(terms[own, pl.ds(pl.multiple_of(mine_rows + i * 16, 16), 16)])
        for j, k in PAIRS:
            total = total + wide(visual_in[j * 4 + k, here])
        visual[here] = low(total)

    visual_copy = go(visual, following, dp_s, 0, before)
    mp_copies[1].wait_recv()
    mp_copies[2].wait_recv()
    for i in range(10):
        for j in range(4):
            there = pl.ds(j * 1280 + i * 128, 128)
            apart[i, pl.ds(j, 64, stride=4), :] = wide(cells_back[:, there])
        gradient[:, i * 128 : (i + 1) * 128] = apart[i]
    slot = lax.broadcasted_iota(jnp.int32, (256, 64), 1)
    rows_down = upright(rows_across[...])
    offset = (me.z * 2 + me.low) * 64
    here_cells = jnp.where(rows_down - offset == slot, 1.0, 0.0).astype(jnp.bfloat16)
    next_cells = jnp.where(rows_down - offset - 64 == slot, 1.0, 0.0).astype(jnp.bfloat16)
    visual_copy.wait_recv()
    for i in range(4):
        span = pl.ds(i * STEP, STEP)
        picked = product(here_cells, visual[:, span]) + product(next_cells, following[:, span])
        sequence[:, span] = jnp.where(rows_down >= 0, low(picked), text[:, span])
    for copy in pending:
        copy.wait_send()


def merger(cell_rows, text, merged, backs, up, down):
    def buffer(*shape):
        return pltpu.VMEM(shape, jnp.bfloat16)

    scratch = [
        buffer(*backs.shape),
        buffer(*up.shape),
        buffer(*down.shape),
        buffer(*merged.shape),
        pltpu.VMEM((10, 256, 128), jnp.float32),
        buffer(4, 64, 5120),
        pltpu.VMEM((256, 320), jnp.float32),
        buffer(256, 320),
        buffer(256, 320),
        pltpu.VMEM((256, 320), jnp.float32),
        buffer(4, 256, 2048),
        buffer(2, 256, 2048),
        buffer(8, 64, 2048),
        buffer(64, 2048),
        buffer(64, 2048),
        buffer(4, 2, 2, 16, 5120),
        buffer(4, 2, 16, 5120),
        buffer(4, 2, 16, 5120),
        buffer(8, 16, 5120),
    ]
    scratch += [pltpu.SemaphoreType.DMA((3,))]
    for size in (4, 4, 1, 2, 8, 1, 8, 3):
        scratch += sem_pair(size)
    return pl.pallas_call(
        merger_kernel,
        out_shape=[
            jax.ShapeDtypeStruct(text.shape, jnp.bfloat16),
            jax.ShapeDtypeStruct((256, 1280), jnp.float32),
        ],
        in_specs=[VMEM] * 3 + [ANY] * 3,
        out_specs=[VMEM] * 2,
        scratch_shapes=scratch,
        compiler_params=pltpu.CompilerParams(
            collective_id=4, has_side_effects=True, vmem_limit_bytes=VMEM_LIMIT
        ),
        name="merger",
    )(cell_rows, text, merged, backs, up, down)


CHUNKS = 4


class SumOverMp:
    def __init__(self, me, go, buffers, sems):
        self.me, self.go = me, go
        self.outgoing, self.got, self.half, self.other, self.total = buffers
        self.sems = sems
        self.sibling, self.partner = me.at(core=1 - me.core), me.at(high=1 - me.high)
        self.mine = pl.multiple_of(me.core * 128, 128)
        self.theirs = pl.multiple_of((1 - me.core) * 128, 128)

    def begin(self, compute):
        step = 128 // CHUNKS
        self.outgoing[...] = low(compute(pl.ds(self.theirs, 128)))
        first = []
        for k in range(CHUNKS):
            here = pl.ds(k * step, step)
            first.append(
                self.go(self.outgoing.at[here], self.got.at[here], self.sems, k, self.sibling)
            )
        self.half[...] = low(compute(pl.ds(self.mine, 128)))
        self.second = []
        for k in range(CHUNKS):
            here = pl.ds(k * step, step)
            first[k].wait_recv()
            self.half[here] = low(wide(self.half[here]) + wide(self.got[here]))
            self.second.append(
                self.go(self.half.at[here], self.other.at[here], self.sems, CHUNKS + k, self.partner)
            )

    def end(self):
        step = 128 // CHUNKS
        third = []
        for k in range(CHUNKS):
            here = pl.ds(k * step, step)
            there = pl.ds(pl.multiple_of(self.mine + k * step, step), step)
            self.second[k].wait_recv()
            self.total[there] = low(wide(self.half[here]) + wide(self.other[here]))
            third.append(
                self.go(
                    self.total.at[there], self.total.at[there], self.sems, 2 * CHUNKS + k, self.sibling
                )
            )
        for copy in third:
            copy.wait_recv()


def sum_buffers():
    half = pltpu.VMEM((128, 1280), jnp.bfloat16)
    return [half, half, half, half, pltpu.VMEM((256, 1280), jnp.bfloat16)]


def head_mask(head):
    lane = lax.broadcasted_iota(jnp.int32, (1, 320), 1)
    inside = (lane >= head * HEAD_DIM) & (lane < (head + 1) * HEAD_DIM)
    return jnp.where(inside, 1.0, 0.0).astype(jnp.bfloat16)


def head_shares(queries, keys, mask, allowed):
    scores = last_with_last(queries * mask, keys) * (1.0 / math.sqrt(HEAD_DIM))
    scores = jnp.where(allowed, scores, -1e30)
    raised = jnp.exp(scores - jnp.max(scores, axis=-1, keepdims=True))
    return raised / jnp.sum(raised, axis=-1, keepdims=True)


def forward_kernel(*refs):
    block_input, windows, gains, merge_gain, rows_across, cotangent = refs[:6]
    shards = refs[6:10]
    kept = refs[10:14]
    attend, projected, heads_out, middle, feed, gate, upper, activated, block_out, merged = refs[14:24]
    backs = refs[24]
    wholes = refs[25:29]
    spill, spill_in, merged_wide = refs[29:32]
    sum_one, sum_two = refs[32:37], refs[37:42]
    own, keep, *pairs = refs[42:]
    y_s, z_s, x_s, one_s, two_s, dp_s, back_s, fore_s = [
        (pairs[2 * i], pairs[2 * i + 1]) for i in range(8)
    ]
    me = Place()
    others = (1, 3, 2)
    y_at = {k: me.at(y=me.along_y(k)) for k in others}
    z_at = {k: me.at(z=me.along_z(k)) for k in others}
    side, sibling = me.at(low=1 - me.low), me.at(core=1 - me.core)
    after = me.at(z=(me.z + me.low) % 4, low=1 - me.low)
    far = me.at(z=(me.z + 3 + 2 * me.low) % 4, low=1 - me.low)

    greet(
        [y_at[1], y_at[3], z_at[1], z_at[3], side, far, sibling, me.at(high=1 - me.high)]
    )
    pending = []

    def go(*arguments):
        copy = send(*arguments)
        pending.append(copy)
        return copy

    starts = (me.z * QUARTER, 4 * QUARTER + me.low * HALF, 320 - ALONE)
    sizes = (QUARTER, HALF, ALONE)
    local_copies, near, far_copies, along, onwards, relays = [], {}, {}, {}, {}, {}

    def rows_of(u, source, start, size):
        t, p, n = UNITS[u]
        return wholes[t].at[pl.ds(p, n), source, pl.ds(pl.multiple_of(start, 16), size)]

    def begin(u):
        t, p, n = UNITS[u]
        for d in (1, 3):
            for part in range(3):
                span = pl.ds(pl.multiple_of(starts[part], 16), sizes[part])
                near[u, d, part] = go(
                    shards[t].at[pl.ds(p, n), span],
                    wholes[t].at[pl.ds(p, n), me.y, span],
                    y_s,
                    u * 12 + (d // 2) * 3 + part,
                    y_at[d],
                )

    def onward(u, k):
        source = me.along_y(k)
        block = rows_of(u, source, starts[0], sizes[0])
        for e in (1, 3):
            along[u, k, e] = go(block, block, z_s, u * 12 + (k - 1) * 2 + e // 2, z_at[e])
        block = rows_of(u, source, starts[1], sizes[1])
        onwards[u, k] = go(block, block, x_s, u * 3 + k - 1, side)

    def relay_y(u):
        for d in (1, 3):
            for part in range(3):
                near[u, d, part].wait_recv()
                first, size = SHARE[part][d]
                block = rows_of(u, me.along_y(4 - d), starts[part] + first, size)
                far_copies[u, d, part] = go(
                    block, block, y_s, u * 12 + 6 + (d // 2) * 3 + part, y_at[d]
                )
        onward(u, 3)
        onward(u, 1)

    def distant(u):
        for d in (1, 3):
            for part in range(3):
                far_copies[u, d, part].wait_recv()
        onward(u, 2)

    def relay_z(u):
        for k in (3, 1, 2):
            for e in (1, 3):
                along[u, k, e].wait_recv()
                first, size = SHARE_Z[k % 2][e]
                block = rows_of(u, me.along_y(k), me.along_z(4 - e) * QUARTER + first, size)
                relays[u, k, e] = go(
                    block, block, z_s, u * 12 + 6 + (k - 1) * 2 + e // 2, z_at[e]
                )

    keeps = []

    def complete(u):
        t, p, n = UNITS[u]
        for k in (3, 1, 2):
            onwards[u, k].wait_recv()
            relays[u, k, 1].wait_recv()
            relays[u, k, 3].wait_recv()
        planes = pl.ds(p, n)
        keeps.append(local_copy(wholes[t].at[planes], kept[t].at[planes], keep.at[u]))

    def whole(t, p):
        return wholes[t][p].reshape(1280, -1)

    begin(0)
    begin(1)
    for t in range(4):
        local_copies.append(local_copy(shards[t], wholes[t].at[:, me.y], own.at[t]))
    slot = lax.broadcasted_iota(jnp.int32, (128, 256), 0)
    offset = (me.z * 2 + me.low) * 64
    taken = jnp.where(rows_across[...] - offset == slot, 1.0, 0.0).astype(jnp.bfloat16)
    column = me.high * 2 + me.core
    for i in range(4):
        span = pl.ds(i * STEP, STEP)
        arrived = low(product(taken, cotangent[:, span]))
        spill[:, span] = arrived[64:]
        backs[me.y, column, :, span] = arrived[:64]
    spill_copy = go(spill, spill_in, dp_s, 0, after)
    start = wide(block_input[...])
    attend[...] = low(start * root_scale(start) * gains[0:1])
    relay_y(0)
    begin(2)
    distant(0)
    relay_y(1)
    distant(1)
    begin(3)
    relay_z(0)
    spill_copy.wait_recv()
    for i in range(4):
        span = pl.ds(i * STEP, STEP)
        backs[me.y, column, :, span] = backs[me.y, column, :, span] + spill_in[:, span]
    block = backs.at[me.y, column]
    across = go(block, block, back_s, 0, me.at(high=1 - me.high))
    relay_z(1)
    for copy in local_copies:
        copy.wait()
    complete(0)
    for p in range(3):
        projected[p] = low(product(attend[...], whole(0, p)))
    relay_y(2)
    begin(4)
    distant(2)
    allowed = same_image(windows[...])
    mixed = jnp.zeros((256, 320), jnp.float32)
    for head in range(4):
        mask = head_mask(head)
        shares = head_shares(projected[0], projected[1], mask, allowed)
        mixed = mixed + product(low(shares), projected[2] * mask)
    heads_out[...] = low(mixed)
    complete(1)
    relay_y(3)
    distant(3)
    relay_z(2)
    total = SumOverMp(me, go, sum_one, one_s)
    total.begin(lambda rows: last_with_last(heads_out[rows], whole(1, 0)))
    relay_y(4)
    across.wait_recv()
    columns = (column, (1 - me.high) * 2 + me.core)
    back_copies, back_relays, fore_copies = {}, [], []
    for j in (0, 1):
        block = backs.at[me.y, columns[j]]
        for d in (1, 3):
            back_copies[j, d] = go(block, block, back_s, 1 + j * 2 + d // 2, y_at[d])
        fore_copies.append(go(block, block, fore_s, j * 4, sibling))
    distant(4)
    total.end()
    middle[...] = wide(block_input[...]) + wide(sum_one[4][...])
    feed[...] = low(middle[...] * root_scale(middle[...]) * gains[1:2])
    relay_z(3)
    complete(2)
    gate[...] = product(feed[...], whole(2, 0))
    relay_z(4)
    for (j, d), copy in back_copies.items():
        copy.wait_recv()
        source = me.along_y(4 - d)
        block = backs.at[source, columns[j], pl.ds(16 * (d - 1), 32)]
        back_relays.append(go(block, block, back_s, 5 + j * 2 + d // 2, y_at[d]))
        block = backs.at[source, columns[j]]
        fore_copies.append(go(block, block, fore_s, j * 4 + d, sibling))
    complete(3)
    upper[...] = product(feed[...], whole(2, 1))
    activated[...] = low(gate[...] * jax.nn.sigmoid(gate[...]) * upper[...])
    complete(4)
    total = SumOverMp(me, go, sum_two, two_s)
    total.begin(lambda rows: last_with_last(activated[rows], whole(3, 0)))
    for copy in back_relays:
        copy.wait_recv()
    for j in (0, 1):
        block = backs.at[me.along_y(2), columns[j]]
        fore_copies.append(go(block, block, fore_s, j * 4 + 2, sibling))
    total.end()
    block_out[...] = middle[...] + wide(sum_two[4][...])
    scale_three = root_scale(block_out[...])
    for i in range(10):
        span = slice(i * 128, (i + 1) * 128)
        merged_wide[i] = block_out[:, span] * scale_three * merge_gain[span][None]
        for j in range(4):
            there = pl.ds(j * 1280 + i * 128, 128)
            merged[:, there] = low(merged_wide[i, pl.ds(j, 64, stride=4), :])
    for copy in fore_copies:
        copy.wait_recv()
    for copy in keeps:
        copy.wait()
    for copy in pending:
        copy.wait_send()


def block_forward(block_input, windows, gains, merge_gain, cell_rows, cotangent, shards):
    rows, width = block_input.shape
    units = shards[2].shape[2]

    def shape(kind, *dims):
        return jax.ShapeDtypeStruct(dims, kind)

    low_, wide_ = jnp.bfloat16, jnp.float32
    outs = [shape(low_, s.shape[0], 4, *s.shape[1:]) for s in shards] + [
        shape(low_, rows, width),
        shape(low_, 3, rows, 320),
        shape(low_, rows, 320),
        shape(wide_, rows, width),
        shape(low_, rows, width),
        shape(wide_, rows, units),
        shape(wide_, rows, units),
        shape(low_, rows, units),
        shape(wide_, rows, width),
        shape(low_, rows // 4, 4 * width),
        shape(low_, 4, 4, 64, cotangent.shape[1]),
    ]
    spill = pltpu.VMEM((64, cotangent.shape[1]), jnp.bfloat16)
    scratch = [pltpu.VMEM(out.shape, jnp.bfloat16) for out in outs[:4]]
    scratch += [spill, spill, pltpu.VMEM((10, rows, 128), jnp.float32)]
    scratch += sum_buffers() + sum_buffers()
    scratch += [pltpu.SemaphoreType.DMA((4,)), pltpu.SemaphoreType.DMA((len(UNITS),))]
    for size in (60, 60, 15, 3 * CHUNKS, 3 * CHUNKS, 1, 9, 8):
        scratch += sem_pair(size)
    results = pl.pallas_call(
        forward_kernel,
        out_shape=outs,
        in_specs=[VMEM] * 10,
        out_specs=[ANY] * 4 + [VMEM] * (len(outs) - 4),
        scratch_shapes=scratch,
        compiler_params=pltpu.CompilerParams(
            collective_id=1, has_side_effects=True, vmem_limit_bytes=VMEM_LIMIT
        ),
        name="block_forward",
    )(
        block_input,
        windows,
        gains,
        merge_gain,
        cell_rows,
        cotangent,
        *shards,
    )
    return results[:4], results[4:14], results[14]


A_ROWS = 192
A_PART = A_ROWS // 4
B_PART = (320 - A_ROWS) // 4
E_ROWS = A_PART + B_PART
A_HALF, B_HALF = A_ROWS // 2, B_PART // 2
E_TOP = 48
TILE = 16
ORDER = (1, 3, 2)


def over_rows(planes, rows, body):
    tiles = rows // TILE

    @pl.loop(0, planes * tiles)
    def _(i):
        body(i // tiles, pl.multiple_of((i % tiles) * TILE, TILE))


class Reduction:
    def __init__(self, me, go, term, final, buffers, sems, index, y_at, z_at, side):
        self.me, self.go, self.term, self.final = me, go, term, final
        self.ya, self.fy, self.sa, self.za, self.zb, self.fz, self.sb, self.yb, self.ee, self.ex = buffers
        self.sems, self.index, self.y_at, self.z_at, self.side = sems, index, y_at, z_at, side
        self.planes = term.shape[0]
        self.relayed = index >= 2

    def stage_one(self):
        me, term, go, ya, zb = self.me, self.term, self.go, self.ya, self.zb
        top, bottom = pl.ds(0, A_HALF), pl.ds(A_HALF, A_HALF)
        at = self.index * 6

        def a_rows(k, span):
            return term.at[:, me.along_y(k), span]

        def b_rows(k, half):
            first = A_ROWS + me.along_z(k) * B_PART + half * B_HALF
            return term.at[:, :, pl.ds(pl.multiple_of(first, TILE), B_HALF)]

        up, down = self.y_at[1], self.y_at[3]
        sems = self.sems[0]
        self.far_a = [
            go(a_rows(2, top), self.fy.at[0], sems, at, up),
            go(a_rows(2, bottom), self.fy.at[1], sems, at + 1, down),
        ]
        up_z, down_z = self.z_at[1], self.z_at[3]
        sems_z = self.sems[1]
        self.far_b = [
            go(b_rows(2, 0), self.fz.at[0], sems_z, at, up_z),
            go(b_rows(2, 1), self.fz.at[1], sems_z, at + 1, down_z),
        ]
        self.first_a = [
            go(a_rows(1, bottom), ya.at[0, :, bottom], sems, at + 2, up),
            go(a_rows(3, top), ya.at[1, :, top], sems, at + 3, down),
        ]
        b_top, b_bottom = pl.ds(0, B_HALF), pl.ds(B_HALF, B_HALF)
        self.first_b = [
            go(b_rows(1, 1), zb.at[0, :, :, b_bottom], sems_z, at + 2, up_z),
            go(b_rows(3, 0), zb.at[1, :, :, b_top], sems_z, at + 3, down_z),
        ]

    def stage_half(self):
        me, term, go, fy, fz = self.me, self.term, self.go, self.fy, self.fz
        at = self.index * 6
        for copy in self.far_b + self.far_a:
            copy.wait_recv()

        def add_b(i, r):
            p, q = i // 4, i % 4
            here = pl.ds(r, TILE)
            first = pl.multiple_of(A_ROWS + me.along_z(1) * B_PART + r, TILE)
            fz[0, p, q, here] = low(wide(fz[0, p, q, here]) + wide(term[p, q, pl.ds(first, TILE)]))
            first = pl.multiple_of(A_ROWS + me.along_z(3) * B_PART + B_HALF + r, TILE)
            fz[1, p, q, here] = low(wide(fz[1, p, q, here]) + wide(term[p, q, pl.ds(first, TILE)]))

        def add_a(p, r):
            here = pl.ds(r, TILE)
            there = pl.ds(pl.multiple_of(A_HALF + r, TILE), TILE)
            fy[0, p, here] = low(wide(fy[0, p, here]) + wide(term[p, me.along_y(1), here]))
            fy[1, p, here] = low(wide(fy[1, p, here]) + wide(term[p, me.along_y(3), there]))

        over_rows(self.planes * 4, B_HALF, add_b)
        over_rows(self.planes, A_HALF, add_a)
        top, bottom = pl.ds(0, A_HALF), pl.ds(A_HALF, A_HALF)
        b_top, b_bottom = pl.ds(0, B_HALF), pl.ds(B_HALF, B_HALF)
        ya, zb = self.ya, self.zb
        self.first_b += [
            go(fz.at[0], zb.at[0, :, :, b_top], self.sems[1], at + 4, self.z_at[1]),
            go(fz.at[1], zb.at[1, :, :, b_bottom], self.sems[1], at + 5, self.z_at[3]),
        ]
        self.first_a += [
            go(fy.at[0], ya.at[0, :, top], self.sems[0], at + 4, self.y_at[1]),
            go(fy.at[1], ya.at[1, :, bottom], self.sems[0], at + 5, self.y_at[3]),
        ]

    def stage_two(self):
        me, term, ya, sa, zb, sb = self.me, self.term, self.ya, self.sa, self.zb, self.sb
        for copy in self.first_b:
            copy.wait_recv()

        def add_b(i, r):
            p, q = i // 4, i % 4
            here = pl.ds(r, TILE)
            there = pl.ds(pl.multiple_of(A_ROWS + me.z * B_PART + r, TILE), TILE)
            sb[p, q, here] = low(
                wide(term[p, q, there]) + wide(zb[0, p, q, here]) + wide(zb[1, p, q, here])
            )

        over_rows(self.planes * 4, B_PART, add_b)
        self.second = [
            self.go(
                sb.at[:, me.along_y(k)],
                self.yb.at[k - 1],
                self.sems[2],
                self.index * 3 + k - 1,
                self.y_at[k],
            )
            for k in ORDER
        ]
        for copy in self.first_a:
            copy.wait_recv()

        def add_a(p, r):
            here = pl.ds(r, TILE)
            sa[p, here] = low(
                wide(term[p, me.y, here]) + wide(ya[0, p, here]) + wide(ya[1, p, here])
            )

        over_rows(self.planes, A_ROWS, add_a)
        self.second += [
            self.go(
                sa.at[:, pl.ds(pl.multiple_of(me.along_z(k) * A_PART, TILE), A_PART)],
                self.za.at[k - 1],
                self.sems[3],
                self.index * 3 + k - 1,
                self.z_at[k],
            )
            for k in ORDER
        ]

    def stage_three(self):
        me, sa, za, sb, yb, ee = self.me, self.sa, self.za, self.sb, self.yb, self.ee
        for copy in self.second:
            copy.wait_recv()

        def add_a(p, r):
            here = pl.ds(r, TILE)
            there = pl.ds(pl.multiple_of(me.z * A_PART + r, TILE), TILE)
            ee[p, here] = low(
                wide(sa[p, there]) + wide(za[0, p, here]) + wide(za[1, p, here]) + wide(za[2, p, here])
            )

        def add_b(p, r):
            here = pl.ds(r, TILE)
            there = pl.ds(pl.multiple_of(A_PART + r, TILE), TILE)
            ee[p, there] = low(
                wide(sb[p, me.y, here])
                + wide(yb[0, p, here])
                + wide(yb[1, p, here])
                + wide(yb[2, p, here])
            )

        over_rows(self.planes, A_PART, add_a)
        over_rows(self.planes, B_PART, add_b)
        self.third = self.go(ee, self.ex, self.sems[4], self.index, self.side)

    def owned(self, source):
        return source % 2, (source // 2) * (A_ROWS // 2)

    def stage_four(self):
        me, ya, ee, ex = self.me, self.ya, self.ee, self.ex
        self.third.wait_recv()
        slot, base = self.owned(me.z)

        def add(p, r):
            there = pl.ds(pl.multiple_of(base + r, TILE), TILE)
            here = pl.ds(r, TILE)
            ya[slot, p, there] = low(wide(ee[p, here]) + wide(ex[p, here]))

        over_rows(self.planes, E_ROWS, add)
        mine = self.piece(0, 0, E_ROWS)
        at = self.index * 4
        near = (1, 3) if self.relayed else ORDER
        self.fourth = {k: self.go(mine, mine, self.sems[5], at + k - 1, self.z_at[k]) for k in near}

    def piece(self, k, start, rows):
        slot, base = self.owned(self.me.along_z(k))
        return self.ya.at[slot, :, pl.ds(pl.multiple_of(base + start, TILE), rows)]

    def relay(self):
        if not self.relayed:
            return
        at = self.index * 4
        self.fourth[1].wait_recv()
        piece = self.piece(3, 0, E_TOP)
        self.fourth[2] = self.go(piece, piece, self.sems[5], at + 1, self.z_at[1])
        self.fourth[3].wait_recv()
        piece = self.piece(1, E_TOP, E_ROWS - E_TOP)
        self.fourth[4] = self.go(piece, piece, self.sems[5], at + 3, self.z_at[3])

    def put(self, p, rows, value):
        if self.index in (2, 3):
            self.final[rows, self.index - 2] = value
        else:
            self.final[p, rows] = value

    def finish(self):
        me, ya = self.me, self.ya
        for k in (0,) + ORDER:
            if k == 2 and self.relayed:
                self.fourth[2].wait_recv()
                self.fourth[4].wait_recv()
            elif k and not self.relayed:
                self.fourth[k].wait_recv()
            source = me.along_z((4 - k) % 4)
            slot, base = self.owned(source)

            def put_a(p, r):
                there = pl.ds(pl.multiple_of(source * A_PART + r, TILE), TILE)
                here = pl.ds(pl.multiple_of(base + r, TILE), TILE)
                self.put(p, there, wide(ya[slot, p, here]))

            def put_b(p, r):
                there = pl.ds(pl.multiple_of(A_ROWS + source * B_PART + r, TILE), TILE)
                here = pl.ds(pl.multiple_of(base + A_PART + r, TILE), TILE)
                self.put(p, there, wide(ya[slot, p, here]))

            over_rows(self.planes, A_PART, put_a)
            over_rows(self.planes, B_PART, put_b)


def first_with_first(left, right):
    return lax.dot_general(
        left, right, (((0,), (0,)), ((), ())), preferred_element_type=jnp.float32
    )


def backward_kernel(*refs):
    (
        block_input,
        windows,
        gains,
        merge_gain,
        cells_back,
        triple_kept,
        output_kept,
        gate_up_kept,
        down_kept,
        attend,
        projected,
        heads_out,
        middle,
        feed,
        gate,
        upper,
        activated,
        block_out,
    ) = refs[:18]
    input_gradient = refs[18]
    outs = (refs[19], refs[20], refs[21], refs[21], refs[22])
    gain_out = refs[23]
    refs = refs[24:]
    triple, output, gate_up, down, load = refs[:5]
    refs = refs[5:]
    sum_one, sum_two = refs[:5], refs[5:10]
    terms = refs[10:15]
    buffers = [refs[15 + 10 * t : 25 + 10 * t] for t in range(5)]
    middle_back, middle_low, out_low, gate_up_back, triple_back, gain, gain_in, gain_sum = refs[65:73]
    sems = refs[73:]
    pair = [(sems[2 * i], sems[2 * i + 1]) for i in range(9)]
    loads = [
        local_copy(source, target, load.at[i])
        for i, (source, target) in enumerate(
            ((down_kept, down), (gate_up_kept, gate_up), (output_kept, output), (triple_kept, triple))
        )
    ]
    me = Place()
    y_at = {k: me.at(y=me.along_y(k)) for k in ORDER}
    z_at = {k: me.at(z=me.along_z(k)) for k in ORDER}
    side = me.at(low=1 - me.low)
    greet(
        [y_at[k] for k in ORDER]
        + [z_at[k] for k in ORDER]
        + [side, me.at(core=1 - me.core), me.at(high=1 - me.high)]
    )
    pending = []

    def go(*arguments):
        copy = send(*arguments)
        pending.append(copy)
        return copy

    reductions = [
        Reduction(me, go, terms[t], outs[t], buffers[t], pair[:6], t, y_at, z_at, side)
        for t in range(5)
    ]
    of_triple, of_output, of_gate, of_upper, of_down = reductions

    def form(t, p, left, right):
        for i in range(2):
            block = first_with_first(left[:, i * 640 : (i + 1) * 640], right)
            terms[t][p, 2 * i : 2 * i + 2] = low(block).reshape(2, 320, right.shape[1])

    def whole(weight, p):
        return weight[p].reshape(1280, -1)

    scale_three = root_scale(block_out[...])
    out_back = norm_backward(cells_back[...], block_out[...], scale_three, merge_gain[...][None])
    middle_back[...] = out_back
    out_low[...] = low(out_back)
    form(4, 0, out_low, activated[...])
    of_down.stage_one()
    for copy in loads:
        copy.wait()
    activated_back = product(out_low[...], whole(down, 0))
    slope = jax.nn.sigmoid(gate[...])
    gate_up_back[1] = low(activated_back * gate[...] * slope)
    gate_up_back[0] = low(activated_back * upper[...] * slope * (1.0 + gate[...] * (1.0 - slope)))
    total = SumOverMp(me, go, sum_one, pair[6])
    total.begin(
        lambda rows: last_with_last(gate_up_back[0, rows], whole(gate_up, 0))
        + last_with_last(gate_up_back[1, rows], whole(gate_up, 1))
    )
    form(2, 0, feed, gate_up_back[0])
    of_gate.stage_one()
    of_down.stage_half()
    total.end()
    feed_back = wide(sum_one[4][...])
    scale_two = root_scale(middle[...])
    middle_back[...] = middle_back[...] + norm_backward(
        feed_back, middle[...], scale_two, gains[1:2]
    )
    middle_low[...] = low(middle_back[...])
    gain[...] = jnp.zeros_like(gain)
    gain[1:2] = jnp.sum(feed_back * middle[...] * scale_two, axis=0, keepdims=True)
    form(3, 0, feed, gate_up_back[1])
    of_upper.stage_one()
    of_gate.stage_half()
    heads_back = low(product(middle_low[...], whole(output, 0)))
    allowed = same_image(windows[...])
    query_back = jnp.zeros((256, 320), jnp.float32)
    key_back = jnp.zeros((256, 320), jnp.float32)
    value_back = jnp.zeros((256, 320), jnp.float32)
    for head in range(4):
        mask = head_mask(head)
        shares = head_shares(projected[0], projected[1], mask, allowed)
        share_back = last_with_last(heads_back * mask, projected[2])
        centre = jnp.sum(shares * share_back, axis=-1, keepdims=True)
        score_back = low(shares * (share_back - centre) * (1.0 / math.sqrt(HEAD_DIM)))
        query_back = query_back + product(score_back, projected[1] * mask)
        key_back = key_back + first_with_first(score_back, projected[0] * mask)
        value_back = value_back + first_with_first(low(shares), heads_back * mask)
    triple_back[0] = low(query_back)
    triple_back[1] = low(key_back)
    triple_back[2] = low(value_back)
    for p in range(3):
        form(0, p, attend, triple_back[p])
    of_triple.stage_one()
    form(1, 0, middle_low, heads_out[...])
    of_output.stage_one()
    of_upper.stage_half()
    of_down.stage_two()
    total = SumOverMp(me, go, sum_two, pair[7])
    total.begin(
        lambda rows: last_with_last(triple_back[0, rows], whole(triple, 0))
        + last_with_last(triple_back[1, rows], whole(triple, 1))
        + last_with_last(triple_back[2, rows], whole(triple, 2))
    )
    of_triple.stage_half()
    of_gate.stage_two()
    total.end()
    attend_back = wide(sum_two[4][...])
    start = wide(block_input[...])
    scale_one = root_scale(start)
    input_gradient[...] = middle_back[...] + norm_backward(attend_back, start, scale_one, gains[0:1])
    gain[0:1] = jnp.sum(attend_back * start * scale_one, axis=0, keepdims=True)
    gain_copies = [go(gain, gain_in.at[k - 1], pair[8], k - 1, y_at[k]) for k in ORDER]
    of_down.stage_three()
    of_output.stage_half()
    of_upper.stage_two()
    of_gate.stage_three()
    of_down.stage_four()
    for copy in gain_copies:
        copy.wait_recv()
    gain_sum[0] = gain[...] + gain_in[0] + gain_in[1] + gain_in[2]
    gain_copies = [go(gain_sum.at[0], gain_in.at[2 + k], pair[8], 2 + k, z_at[k]) for k in ORDER]
    of_triple.stage_two()
    of_upper.stage_three()
    of_gate.stage_four()
    of_down.relay()
    of_output.stage_two()
    for copy in gain_copies:
        copy.wait_recv()
    gain_sum[1] = gain_sum[0] + gain_in[3] + gain_in[4] + gain_in[5]
    gain_copies = [go(gain_sum.at[1], gain_in.at[6], pair[8], 6, side)]
    of_triple.stage_three()
    of_upper.stage_four()
    of_gate.relay()
    of_output.stage_three()
    for copy in gain_copies:
        copy.wait_recv()
    gain_out[...] = gain_sum[1, :2] + gain_in[6, :2]
    of_triple.stage_four()
    of_upper.relay()
    of_output.stage_four()
    for reduction in (of_down, of_gate, of_upper, of_triple, of_output):
        reduction.finish()
    for copy in pending:
        copy.wait_send()


def block_backward(block_input, windows, gains, merge_gain, cells_back, wholes, saved):
    rows, width = block_input.shape
    units = saved[5].shape[1]

    def low_buffer(*shape):
        return pltpu.VMEM(shape, jnp.bfloat16)

    def wide_buffer(*shape):
        return pltpu.VMEM(shape, jnp.float32)

    sizes = ((3, 320), (1, 320), (1, units), (1, units), (1, units))
    scratch = [low_buffer(*whole.shape) for whole in wholes]
    scratch += [pltpu.SemaphoreType.DMA((4,))]
    scratch += sum_buffers() + sum_buffers()
    scratch += [low_buffer(planes, 4, 320, columns) for planes, columns in sizes]
    for planes, columns in sizes:
        scratch += [
            low_buffer(2, planes, A_ROWS, columns),
            low_buffer(2, planes, A_HALF, columns),
            low_buffer(planes, A_ROWS, columns),
            low_buffer(3, planes, A_PART, columns),
            low_buffer(2, planes, 4, B_PART, columns),
            low_buffer(2, planes, 4, B_HALF, columns),
            low_buffer(planes, 4, B_PART, columns),
            low_buffer(3, planes, B_PART, columns),
            low_buffer(planes, E_ROWS, columns),
            low_buffer(planes, E_ROWS, columns),
        ]
    scratch += [
        wide_buffer(rows, width),
        low_buffer(rows, width),
        low_buffer(rows, width),
        low_buffer(2, rows, units),
        low_buffer(3, rows, 320),
        wide_buffer(8, width),
        wide_buffer(7, 8, width),
        wide_buffer(2, 8, width),
    ]
    for size in (30, 30, 15, 15, 5, 20, 3 * CHUNKS, 3 * CHUNKS, 7):
        scratch += sem_pair(size)
    operands = [
        block_input,
        windows,
        gains,
        merge_gain,
        cells_back,
        *wholes,
        *saved,
    ]
    outs = (
        [jax.ShapeDtypeStruct((rows, width), jnp.float32)]
        + [
            jax.ShapeDtypeStruct(dims, jnp.float32)
            for dims in ((3, 320, 320), (1, 320, 320), (320, 2, units), (1, 320, units))
        ]
        + [jax.ShapeDtypeStruct((2, width), jnp.float32)]
    )
    results = pl.pallas_call(
        backward_kernel,
        out_shape=outs,
        in_specs=[VMEM] * 5 + [ANY] * 4 + [VMEM] * (len(operands) - 9),
        out_specs=[VMEM] * len(outs),
        scratch_shapes=scratch,
        compiler_params=pltpu.CompilerParams(
            collective_id=3, has_side_effects=True, vmem_limit_bytes=VMEM_LIMIT
        ),
        name="block_backward",
    )(*operands)

    return results[0], results[1:5], results[5]


def planes_of(weight):
    return jnp.transpose(weight, (1, 0, 2))


def local(
    block_input,
    windows,
    cell_rows,
    text_vectors,
    sequence_cotangent,
    norm_gains,
    merge_gain,
    triple_weight,
    output_weight,
    gate_up_weight,
    down_weight,
    merge_up,
    merge_down,
):
    patches = block_input[0]
    shards = (
        planes_of(triple_weight),
        output_weight[None],
        planes_of(gate_up_weight),
        down_weight[None],
    )
    wholes, saved, backs = block_forward(
        patches,
        windows,
        norm_gains,
        merge_gain,
        cell_rows,
        sequence_cotangent[0],
        shards,
    )
    sequence, cells_back = merger(
        cell_rows,
        text_vectors[0],
        saved[-1],
        backs,
        merge_up.T,
        merge_down,
    )
    input_gradient, gradients, gain_gradient = block_backward(
        patches,
        windows,
        norm_gains,
        merge_gain,
        cells_back,
        wholes,
        saved[:-1],
    )
    return (
        sequence[None],
        input_gradient[None],
        planes_of(gradients[0]),
        gradients[1][0],
        gradients[2],
        gradients[3][0],
        gain_gradient,
    )


def solution(mesh):
    placed = (
        P(("dp", "section"), None, None),
        P(("dp", "section"), None),
        P("section", "dp"),
        P("section", "dp", "mp"),
        P("section", "dp", "mp"),
        P(),
        P(),
        P("section", None, "mp"),
        P("section", "mp"),
        P("section", None, "mp"),
        P("section", "mp"),
        P(None, ("section", "mp")),
        P(("section", "mp"), None),
    )
    return jax.shard_map(
        local,
        mesh=mesh,
        in_specs=placed,
        out_specs=(
            P("section", "dp", "mp"),
            P(("dp", "section"), None, None),
            P("section", None, "mp"),
            P("section", "mp"),
            P("section", None, "mp"),
            P("section", "mp"),
            P(),
        ),
        check_vma=False,
    )
```

```python
import functools
import math

import jax
import jax.numpy as jnp
from jax import lax
from jax.experimental import pallas as pl
from jax.experimental.pallas import tpu as pltpu
from jax.sharding import PartitionSpec as P

HEAD_DIM = 80


epsilon = 1e-06
root_half = 0.7071067811865476
density_scale = 0.3989422804014327

MESH = pl.DeviceIdType.MESH
VMEM_LIMIT = 62 * 1024 * 1024
VMEM = pl.BlockSpec(memory_space=pltpu.VMEM)
ANY = pl.BlockSpec(memory_space=pl.ANY)


def upright(row):
    count = row.shape[1]
    across = lax.broadcasted_iota(jnp.int32, (count, count), 1)
    down = lax.broadcasted_iota(jnp.int32, (count, count), 0)
    return jnp.sum(jnp.where(across == down, row, 0), axis=1, keepdims=True)


def same_image(windows):
    across = lax.broadcasted_iota(jnp.int32, (64, 256), 1) // 4
    down = lax.broadcasted_iota(jnp.int32, (64, 256), 0)
    column = upright(windows)
    of_patch = jnp.sum(jnp.where(across == down, column, 0), axis=0, keepdims=True)
    return upright(of_patch) == of_patch


def local_copy(source, target, sem):
    copy = pltpu.make_async_copy(source, target, sem)
    copy.start()
    return copy


class Place:
    def __init__(self):
        dp, self.y, mp = lax.axis_index("dp"), lax.axis_index("section"), lax.axis_index("mp")
        self.z, self.low = dp // 2, dp % 2
        self.high, self.core = mp // 2, mp % 2

    def at(self, z=None, low=None, y=None, high=None, core=None):
        z = self.z if z is None else z
        low = self.low if low is None else low
        y = self.y if y is None else y
        high = self.high if high is None else high
        core = self.core if core is None else core
        return (z * 2 + low, y, high * 2 + core)

    def along_y(self, k):
        return (self.y + k) % 4

    def along_z(self, k):
        return (self.z + k) % 4


def greet(devices):
    barrier = pltpu.get_barrier_semaphore()
    for device in devices:
        pl.semaphore_signal(barrier, inc=1, device_id=device, device_id_type=MESH)
    pl.semaphore_wait(barrier, len(devices))


def send(source, target, sems, index, device):
    copy = pltpu.make_async_remote_copy(
        src_ref=source,
        dst_ref=target,
        send_sem=sems[0].at[index],
        recv_sem=sems[1].at[index],
        device_id=device,
        device_id_type=MESH,
    )
    copy.start()
    return copy


def sem_pair(*shape):
    return [pltpu.SemaphoreType.DMA(shape), pltpu.SemaphoreType.DMA(shape)]


def wide(values):
    return values.astype(jnp.float32)


def low(values):
    return values.astype(jnp.bfloat16)


def root_scale(values):
    return lax.rsqrt(jnp.mean(values * values, axis=-1, keepdims=True) + epsilon)


def norm_backward(cotangent, values, scale, gain):
    weighted = cotangent * gain
    return scale * weighted - values * scale**3 * jnp.mean(
        weighted * values, axis=-1, keepdims=True
    )


def gelu_value(values):
    return 0.5 * values * (1.0 + jax.scipy.special.erf(values * root_half))


def gelu_slope(values):
    return (
        0.5 * (1.0 + jax.scipy.special.erf(values * root_half))
        + values * jnp.exp(-0.5 * values * values) * density_scale
    )


def product(left, right):
    return jnp.dot(left, right, preferred_element_type=jnp.float32)


QUARTER, HALF = 48, 48
ALONE = 320 - 4 * QUARTER - 2 * HALF
UNITS = ((0, 0, 3), (1, 0, 1), (2, 0, 1), (2, 1, 1), (3, 0, 1))
SHARE_Z = ({1: (0, 16), 3: (16, 32)}, {1: (0, 32), 3: (32, 16)})
SHARE = ({1: (0, 32), 3: (32, 16)}, {1: (0, 16), 3: (16, 32)}, {1: (0, 16), 3: (16, 16)})
PAIRS = [(j, k) for k in (1, 3, 2) for j in (0, 1)] + [(1, 0)]


STEP = 512


def last_with_last(left, right):
    return lax.dot_general(
        left, right, (((1,), (1,)), ((), ())), preferred_element_type=jnp.float32
    )


def merger_kernel(
    merged,
    backs_kept,
    up_kept,
    down_kept,
    visual_terms,
    gradient,
    backs,
    up,
    down,
    cells_back,
    apart,
    cells,
    pre,
    hidden,
    pre_back,
    hidden_back,
    terms,
    terms_in,
    pieces,
    pieces_in,
    parts,
    parts_in,
    *sems,
):
    me = Place()
    load, *sems = sems
    merged_s, share_s, terms_s, pieces_s, parts_s, mp_s = [
        (sems[2 * i], sems[2 * i + 1]) for i in range(6)
    ]
    loads = [
        local_copy(source, target, load.at[i])
        for i, (source, target) in enumerate(
            ((down_kept, down), (backs_kept, backs), (up_kept, up))
        )
    ]
    sibling, partner = me.at(core=1 - me.core), me.at(high=1 - me.high)

    def peer(j, k):
        return me.at(y=me.along_y(k), high=(me.high + j) % 2)

    greet([peer(j, k) for j, k in PAIRS] + [sibling])
    pending = []

    def go(*arguments):
        copy = send(*arguments)
        pending.append(copy)
        return copy

    half = pl.ds(pl.multiple_of(me.core * 32, 32), 32)
    merged_copies = {
        k: go(merged.at[half], cells.at[me.y, half], merged_s, k, peer(0, k)) for k in (1, 3, 2)
    }
    cells[me.y] = merged[...]
    own = me.high * 2 + me.core
    hidden_back[...] = jnp.zeros_like(hidden_back)
    for copy in loads:
        copy.wait()

    @pl.loop(0, 16)
    def _(i):
        inner = pl.ds(pl.multiple_of((i % 4) * STEP, STEP), STEP)
        outer = pl.ds(pl.multiple_of(i * STEP, STEP), STEP)
        left = backs[:, i // 4, :, inner].reshape(256, STEP)
        hidden_back[...] += last_with_last(left, down[:, outer])

    share_copies = []
    for k in (1, 3, 2):
        merged_copies[k].wait_recv()
        region = cells.at[me.along_y(4 - k), half]
        share_copies.append(go(region, region, share_s, k, sibling))
    for copy in share_copies:
        copy.wait_recv()

    pre[...] = jnp.zeros_like(pre)

    @pl.loop(0, 10)
    def _(i):
        span = pl.ds(pl.multiple_of(i * STEP, STEP), STEP)
        pre[...] += last_with_last(cells[:, :, span].reshape(256, STEP), up[:, span])

    pre_back[...] = low(hidden_back[...] * gelu_slope(pre[...]))

    @pl.loop(0, 10)
    def _(i):
        span = pl.ds(pl.multiple_of(i * STEP, STEP), STEP)
        pieces[:, :, :, :, span] = low(product(pre_back[...], up[:, span])).reshape(4, 2, 2, 16, STEP)

    pieces_copy = go(pieces.at[:, :, 1 - me.core], pieces_in, pieces_s, 0, sibling)
    hidden[...] = low(gelu_value(pre[...]))
    pieces_copy.wait_recv()

    @pl.loop(0, 8)
    def _(i):
        a, b = i // 2, i % 2
        for n in range(4):
            span = pl.ds(n * 1280, 1280)
            parts[a, b, :, span] = low(
                wide(pieces[a, b, me.core, :, span]) + wide(pieces_in[a, b, :, span])
            )

    part_copies = [
        go(parts.at[me.along_y(k), (me.high + j) % 2], parts_in.at[j * 4 + k], parts_s, j * 4 + k, peer(j, k))
        for j, k in PAIRS
    ]

    def term_block(column):
        @pl.loop(0, 4)
        def _(i):
            span = pl.ds(pl.multiple_of(i * STEP, STEP), STEP)
            whole = pl.ds(pl.multiple_of(column * 2048 + i * STEP, STEP), STEP)
            terms[column, :, span] = low(product(hidden[...], down[:, whole]))

    term_copies = []
    for j in (0, 1):
        column = j * 2 + 1 - me.core
        term_block(column)
        term_copies.append(go(terms.at[column], terms_in.at[j], terms_s, j, sibling))
    for j in (0, 1):
        column = j * 2 + me.core
        term_block(column)
        term_copies[j].wait_recv()

        @pl.loop(0, 16)
        def _(i):
            here = pl.ds(pl.multiple_of(i * 16, 16), 16)
            visual_terms[j, here] = low(wide(terms[column, here]) + wide(terms_in[j, here]))

    for copy in part_copies:
        copy.wait_recv()
    mine = pl.ds(pl.multiple_of(own * 16, 16), 16)
    for n in range(4):
        span = pl.ds(n * 1280, 1280)
        total = wide(parts[me.y, me.high, :, span])
        for j, k in PAIRS:
            total = total + wide(parts_in[j * 4 + k, :, span])
        cells_back[mine, span] = low(total)
    mp_copies = [
        go(cells_back.at[mine], cells_back.at[mine], mp_s, 0, partner),
        go(cells_back.at[mine], cells_back.at[mine], mp_s, 1, sibling),
    ]
    mp_copies[0].wait_recv()
    theirs = pl.ds(pl.multiple_of(((1 - me.high) * 2 + me.core) * 16, 16), 16)
    mp_copies.append(go(cells_back.at[theirs], cells_back.at[theirs], mp_s, 2, sibling))

    mp_copies[1].wait_recv()
    mp_copies[2].wait_recv()
    for i in range(10):
        for j in range(4):
            there = pl.ds(j * 1280 + i * 128, 128)
            apart[i, pl.ds(j, 64, stride=4), :] = wide(cells_back[:, there])
        gradient[:, i * 128 : (i + 1) * 128] = apart[i]
    for copy in pending:
        copy.wait_send()


def merger(merged, backs, up, down):
    def buffer(*shape):
        return pltpu.VMEM(shape, jnp.bfloat16)

    scratch = [
        buffer(*backs.shape),
        buffer(*up.shape),
        buffer(*down.shape),
        buffer(*merged.shape),
        pltpu.VMEM((10, 256, 128), jnp.float32),
        buffer(4, 64, 5120),
        pltpu.VMEM((256, 320), jnp.float32),
        buffer(256, 320),
        buffer(256, 320),
        pltpu.VMEM((256, 320), jnp.float32),
        buffer(4, 256, 2048),
        buffer(2, 256, 2048),
        buffer(4, 2, 2, 16, 5120),
        buffer(4, 2, 16, 5120),
        buffer(4, 2, 16, 5120),
        buffer(8, 16, 5120),
    ]
    scratch += [pltpu.SemaphoreType.DMA((3,))]
    for size in (4, 4, 2, 1, 8, 3):
        scratch += sem_pair(size)
    return pl.pallas_call(
        merger_kernel,
        out_shape=[
            jax.ShapeDtypeStruct((2, 256, 2048), jnp.bfloat16),
            jax.ShapeDtypeStruct((256, 1280), jnp.float32),
        ],
        in_specs=[VMEM] + [ANY] * 3,
        out_specs=[VMEM] * 2,
        scratch_shapes=scratch,
        compiler_params=pltpu.CompilerParams(
            collective_id=4, has_side_effects=True, vmem_limit_bytes=VMEM_LIMIT
        ),
        name="merger",
    )(merged, backs, up, down)


CHUNKS = 4


class SumOverMp:
    def __init__(self, me, go, buffers, sems):
        self.me, self.go = me, go
        self.outgoing, self.got, self.half, self.other, self.total = buffers
        self.sems = sems
        self.sibling, self.partner = me.at(core=1 - me.core), me.at(high=1 - me.high)
        self.mine = pl.multiple_of(me.core * 128, 128)
        self.theirs = pl.multiple_of((1 - me.core) * 128, 128)

    def begin(self, compute):
        step = 128 // CHUNKS
        self.outgoing[...] = low(compute(pl.ds(self.theirs, 128)))
        first = []
        for k in range(CHUNKS):
            here = pl.ds(k * step, step)
            first.append(
                self.go(self.outgoing.at[here], self.got.at[here], self.sems, k, self.sibling)
            )
        self.half[...] = low(compute(pl.ds(self.mine, 128)))
        self.second = []
        for k in range(CHUNKS):
            here = pl.ds(k * step, step)
            first[k].wait_recv()
            self.half[here] = low(wide(self.half[here]) + wide(self.got[here]))
            self.second.append(
                self.go(self.half.at[here], self.other.at[here], self.sems, CHUNKS + k, self.partner)
            )

    def end(self):
        step = 128 // CHUNKS
        third = []
        for k in range(CHUNKS):
            here = pl.ds(k * step, step)
            there = pl.ds(pl.multiple_of(self.mine + k * step, step), step)
            self.second[k].wait_recv()
            self.total[there] = low(wide(self.half[here]) + wide(self.other[here]))
            third.append(
                self.go(
                    self.total.at[there], self.total.at[there], self.sems, 2 * CHUNKS + k, self.sibling
                )
            )
        for copy in third:
            copy.wait_recv()


def sum_buffers():
    half = pltpu.VMEM((128, 1280), jnp.bfloat16)
    return [half, half, half, half, pltpu.VMEM((256, 1280), jnp.bfloat16)]


def head_mask(head):
    lane = lax.broadcasted_iota(jnp.int32, (1, 320), 1)
    inside = (lane >= head * HEAD_DIM) & (lane < (head + 1) * HEAD_DIM)
    return jnp.where(inside, 1.0, 0.0).astype(jnp.bfloat16)


def head_shares(queries, keys, mask, allowed):
    scores = last_with_last(queries * mask, keys) * (1.0 / math.sqrt(HEAD_DIM))
    scores = jnp.where(allowed, scores, -1e30)
    raised = jnp.exp(scores - jnp.max(scores, axis=-1, keepdims=True))
    return raised / jnp.sum(raised, axis=-1, keepdims=True)


def forward_kernel(*refs):
    block_input, windows, gains, merge_gain, rows_across, cotangent = refs[:6]
    shards = refs[6:10]
    kept = refs[10:14]
    attend, projected, heads_out, middle, feed, gate, upper, activated, block_out, merged = refs[14:24]
    backs = refs[24]
    wholes = refs[25:29]
    spill, spill_in, merged_wide = refs[29:32]
    sum_one, sum_two = refs[32:37], refs[37:42]
    own, keep, *pairs = refs[42:]
    y_s, z_s, x_s, one_s, two_s, dp_s, back_s, fore_s = [
        (pairs[2 * i], pairs[2 * i + 1]) for i in range(8)
    ]
    me = Place()
    others = (1, 3, 2)
    y_at = {k: me.at(y=me.along_y(k)) for k in others}
    z_at = {k: me.at(z=me.along_z(k)) for k in others}
    side, sibling = me.at(low=1 - me.low), me.at(core=1 - me.core)
    after = me.at(z=(me.z + me.low) % 4, low=1 - me.low)
    far = me.at(z=(me.z + 3 + 2 * me.low) % 4, low=1 - me.low)

    greet(
        [y_at[1], y_at[3], z_at[1], z_at[3], side, far, sibling, me.at(high=1 - me.high)]
    )
    pending = []

    def go(*arguments):
        copy = send(*arguments)
        pending.append(copy)
        return copy

    starts = (me.z * QUARTER, 4 * QUARTER + me.low * HALF, 320 - ALONE)
    sizes = (QUARTER, HALF, ALONE)
    local_copies, near, far_copies, along, onwards, relays = [], {}, {}, {}, {}, {}

    def rows_of(u, source, start, size):
        t, p, n = UNITS[u]
        return wholes[t].at[pl.ds(p, n), source, pl.ds(pl.multiple_of(start, 16), size)]

    def begin(u):
        t, p, n = UNITS[u]
        for d in (1, 3):
            for part in range(3):
                span = pl.ds(pl.multiple_of(starts[part], 16), sizes[part])
                near[u, d, part] = go(
                    shards[t].at[pl.ds(p, n), span],
                    wholes[t].at[pl.ds(p, n), me.y, span],
                    y_s,
                    u * 12 + (d // 2) * 3 + part,
                    y_at[d],
                )

    def onward(u, k):
        source = me.along_y(k)
        block = rows_of(u, source, starts[0], sizes[0])
        for e in (1, 3):
            along[u, k, e] = go(block, block, z_s, u * 12 + (k - 1) * 2 + e // 2, z_at[e])
        block = rows_of(u, source, starts[1], sizes[1])
        onwards[u, k] = go(block, block, x_s, u * 3 + k - 1, side)

    def relay_y(u):
        for d in (1, 3):
            for part in range(3):
                near[u, d, part].wait_recv()
                first, size = SHARE[part][d]
                block = rows_of(u, me.along_y(4 - d), starts[part] + first, size)
                far_copies[u, d, part] = go(
                    block, block, y_s, u * 12 + 6 + (d // 2) * 3 + part, y_at[d]
                )
        onward(u, 3)
        onward(u, 1)

    def distant(u):
        for d in (1, 3):
            for part in range(3):
                far_copies[u, d, part].wait_recv()
        onward(u, 2)

    def relay_z(u):
        for k in (3, 1, 2):
            for e in (1, 3):
                along[u, k, e].wait_recv()
                first, size = SHARE_Z[k % 2][e]
                block = rows_of(u, me.along_y(k), me.along_z(4 - e) * QUARTER + first, size)
                relays[u, k, e] = go(
                    block, block, z_s, u * 12 + 6 + (k - 1) * 2 + e // 2, z_at[e]
                )

    keeps = []

    def complete(u):
        t, p, n = UNITS[u]
        for k in (3, 1, 2):
            onwards[u, k].wait_recv()
            relays[u, k, 1].wait_recv()
            relays[u, k, 3].wait_recv()
        planes = pl.ds(p, n)
        keeps.append(local_copy(wholes[t].at[planes], kept[t].at[planes], keep.at[u]))

    def whole(t, p):
        return wholes[t][p].reshape(1280, -1)

    begin(0)
    begin(1)
    for t in range(4):
        local_copies.append(local_copy(shards[t], wholes[t].at[:, me.y], own.at[t]))
    slot = lax.broadcasted_iota(jnp.int32, (128, 256), 0)
    offset = (me.z * 2 + me.low) * 64
    taken = jnp.where(rows_across[...] - offset == slot, 1.0, 0.0).astype(jnp.bfloat16)
    column = me.high * 2 + me.core
    for i in range(4):
        span = pl.ds(i * STEP, STEP)
        arrived = low(product(taken, cotangent[:, span]))
        spill[:, span] = arrived[64:]
        backs[me.y, column, :, span] = arrived[:64]
    spill_copy = go(spill, spill_in, dp_s, 0, after)
    start = wide(block_input[...])
    attend[...] = low(start * root_scale(start) * gains[0:1])
    relay_y(0)
    begin(2)
    distant(0)
    relay_y(1)
    distant(1)
    begin(3)
    relay_z(0)
    spill_copy.wait_recv()
    for i in range(4):
        span = pl.ds(i * STEP, STEP)
        backs[me.y, column, :, span] = backs[me.y, column, :, span] + spill_in[:, span]
    block = backs.at[me.y, column]
    across = go(block, block, back_s, 0, me.at(high=1 - me.high))
    relay_z(1)
    for copy in local_copies:
        copy.wait()
    complete(0)
    for p in range(3):
        projected[p] = low(product(attend[...], whole(0, p)))
    relay_y(2)
    begin(4)
    distant(2)
    allowed = same_image(windows[...])
    mixed = jnp.zeros((256, 320), jnp.float32)
    for head in range(4):
        mask = head_mask(head)
        shares = head_shares(projected[0], projected[1], mask, allowed)
        mixed = mixed + product(low(shares), projected[2] * mask)
    heads_out[...] = low(mixed)
    complete(1)
    relay_y(3)
    distant(3)
    relay_z(2)
    total = SumOverMp(me, go, sum_one, one_s)
    total.begin(lambda rows: last_with_last(heads_out[rows], whole(1, 0)))
    relay_y(4)
    across.wait_recv()
    columns = (column, (1 - me.high) * 2 + me.core)
    back_copies, back_relays, fore_copies = {}, [], []
    for j in (0, 1):
        block = backs.at[me.y, columns[j]]
        for d in (1, 3):
            back_copies[j, d] = go(block, block, back_s, 1 + j * 2 + d // 2, y_at[d])
        fore_copies.append(go(block, block, fore_s, j * 4, sibling))
    distant(4)
    total.end()
    middle[...] = wide(block_input[...]) + wide(sum_one[4][...])
    feed[...] = low(middle[...] * root_scale(middle[...]) * gains[1:2])
    relay_z(3)
    complete(2)
    gate[...] = product(feed[...], whole(2, 0))
    relay_z(4)
    for (j, d), copy in back_copies.items():
        copy.wait_recv()
        source = me.along_y(4 - d)
        block = backs.at[source, columns[j], pl.ds(16 * (d - 1), 32)]
        back_relays.append(go(block, block, back_s, 5 + j * 2 + d // 2, y_at[d]))
        block = backs.at[source, columns[j]]
        fore_copies.append(go(block, block, fore_s, j * 4 + d, sibling))
    complete(3)
    upper[...] = product(feed[...], whole(2, 1))
    activated[...] = low(gate[...] * jax.nn.sigmoid(gate[...]) * upper[...])
    complete(4)
    total = SumOverMp(me, go, sum_two, two_s)
    total.begin(lambda rows: last_with_last(activated[rows], whole(3, 0)))
    for copy in back_relays:
        copy.wait_recv()
    for j in (0, 1):
        block = backs.at[me.along_y(2), columns[j]]
        fore_copies.append(go(block, block, fore_s, j * 4 + 2, sibling))
    total.end()
    block_out[...] = middle[...] + wide(sum_two[4][...])
    scale_three = root_scale(block_out[...])
    for i in range(10):
        span = slice(i * 128, (i + 1) * 128)
        merged_wide[i] = block_out[:, span] * scale_three * merge_gain[span][None]
        for j in range(4):
            there = pl.ds(j * 1280 + i * 128, 128)
            merged[:, there] = low(merged_wide[i, pl.ds(j, 64, stride=4), :])
    for copy in fore_copies:
        copy.wait_recv()
    for copy in keeps:
        copy.wait()
    for copy in pending:
        copy.wait_send()


def block_forward(block_input, windows, gains, merge_gain, cell_rows, cotangent, shards):
    rows, width = block_input.shape
    units = shards[2].shape[2]

    def shape(kind, *dims):
        return jax.ShapeDtypeStruct(dims, kind)

    low_, wide_ = jnp.bfloat16, jnp.float32
    outs = [shape(low_, s.shape[0], 4, *s.shape[1:]) for s in shards] + [
        shape(low_, rows, width),
        shape(low_, 3, rows, 320),
        shape(low_, rows, 320),
        shape(wide_, rows, width),
        shape(low_, rows, width),
        shape(wide_, rows, units),
        shape(wide_, rows, units),
        shape(low_, rows, units),
        shape(wide_, rows, width),
        shape(low_, rows // 4, 4 * width),
        shape(low_, 4, 4, 64, cotangent.shape[1]),
    ]
    spill = pltpu.VMEM((64, cotangent.shape[1]), jnp.bfloat16)
    scratch = [pltpu.VMEM(out.shape, jnp.bfloat16) for out in outs[:4]]
    scratch += [spill, spill, pltpu.VMEM((10, rows, 128), jnp.float32)]
    scratch += sum_buffers() + sum_buffers()
    scratch += [pltpu.SemaphoreType.DMA((4,)), pltpu.SemaphoreType.DMA((len(UNITS),))]
    for size in (60, 60, 15, 3 * CHUNKS, 3 * CHUNKS, 1, 9, 8):
        scratch += sem_pair(size)
    results = pl.pallas_call(
        forward_kernel,
        out_shape=outs,
        in_specs=[VMEM] * 10,
        out_specs=[ANY] * 4 + [VMEM] * (len(outs) - 4),
        scratch_shapes=scratch,
        compiler_params=pltpu.CompilerParams(
            collective_id=1, has_side_effects=True, vmem_limit_bytes=VMEM_LIMIT
        ),
        name="block_forward",
    )(
        block_input,
        windows,
        gains,
        merge_gain,
        cell_rows,
        cotangent,
        *shards,
    )
    return results[:4], results[4:14], results[14]


A_ROWS = 192
A_PART = A_ROWS // 4
B_PART = (320 - A_ROWS) // 4
E_ROWS = A_PART + B_PART
A_HALF, B_HALF = A_ROWS // 2, B_PART // 2
E_TOP = 48
TILE = 16
ORDER = (1, 3, 2)


def over_rows(planes, rows, body):
    tiles = rows // TILE

    @pl.loop(0, planes * tiles)
    def _(i):
        body(i // tiles, pl.multiple_of((i % tiles) * TILE, TILE))


class Reduction:
    def __init__(self, me, go, term, final, buffers, sems, index, y_at, z_at, side):
        self.me, self.go, self.term, self.final = me, go, term, final
        self.ya, self.fy, self.sa, self.za, self.zb, self.fz, self.sb, self.yb, self.ee, self.ex = buffers
        self.sems, self.index, self.y_at, self.z_at, self.side = sems, index, y_at, z_at, side
        self.planes = term.shape[0]
        self.relayed = index >= 2

    def stage_one(self):
        me, term, go, ya, zb = self.me, self.term, self.go, self.ya, self.zb
        top, bottom = pl.ds(0, A_HALF), pl.ds(A_HALF, A_HALF)
        at = self.index * 6

        def a_rows(k, span):
            return term.at[:, me.along_y(k), span]

        def b_rows(k, half):
            first = A_ROWS + me.along_z(k) * B_PART + half * B_HALF
            return term.at[:, :, pl.ds(pl.multiple_of(first, TILE), B_HALF)]

        up, down = self.y_at[1], self.y_at[3]
        sems = self.sems[0]
        self.far_a = [
            go(a_rows(2, top), self.fy.at[0], sems, at, up),
            go(a_rows(2, bottom), self.fy.at[1], sems, at + 1, down),
        ]
        up_z, down_z = self.z_at[1], self.z_at[3]
        sems_z = self.sems[1]
        self.far_b = [
            go(b_rows(2, 0), self.fz.at[0], sems_z, at, up_z),
            go(b_rows(2, 1), self.fz.at[1], sems_z, at + 1, down_z),
        ]
        self.first_a = [
            go(a_rows(1, bottom), ya.at[0, :, bottom], sems, at + 2, up),
            go(a_rows(3, top), ya.at[1, :, top], sems, at + 3, down),
        ]
        b_top, b_bottom = pl.ds(0, B_HALF), pl.ds(B_HALF, B_HALF)
        self.first_b = [
            go(b_rows(1, 1), zb.at[0, :, :, b_bottom], sems_z, at + 2, up_z),
            go(b_rows(3, 0), zb.at[1, :, :, b_top], sems_z, at + 3, down_z),
        ]

    def stage_half(self):
        me, term, go, fy, fz = self.me, self.term, self.go, self.fy, self.fz
        at = self.index * 6
        for copy in self.far_b + self.far_a:
            copy.wait_recv()

        def add_b(i, r):
            p, q = i // 4, i % 4
            here = pl.ds(r, TILE)
            first = pl.multiple_of(A_ROWS + me.along_z(1) * B_PART + r, TILE)
            fz[0, p, q, here] = low(wide(fz[0, p, q, here]) + wide(term[p, q, pl.ds(first, TILE)]))
            first = pl.multiple_of(A_ROWS + me.along_z(3) * B_PART + B_HALF + r, TILE)
            fz[1, p, q, here] = low(wide(fz[1, p, q, here]) + wide(term[p, q, pl.ds(first, TILE)]))

        def add_a(p, r):
            here = pl.ds(r, TILE)
            there = pl.ds(pl.multiple_of(A_HALF + r, TILE), TILE)
            fy[0, p, here] = low(wide(fy[0, p, here]) + wide(term[p, me.along_y(1), here]))
            fy[1, p, here] = low(wide(fy[1, p, here]) + wide(term[p, me.along_y(3), there]))

        over_rows(self.planes * 4, B_HALF, add_b)
        over_rows(self.planes, A_HALF, add_a)
        top, bottom = pl.ds(0, A_HALF), pl.ds(A_HALF, A_HALF)
        b_top, b_bottom = pl.ds(0, B_HALF), pl.ds(B_HALF, B_HALF)
        ya, zb = self.ya, self.zb
        self.first_b += [
            go(fz.at[0], zb.at[0, :, :, b_top], self.sems[1], at + 4, self.z_at[1]),
            go(fz.at[1], zb.at[1, :, :, b_bottom], self.sems[1], at + 5, self.z_at[3]),
        ]
        self.first_a += [
            go(fy.at[0], ya.at[0, :, top], self.sems[0], at + 4, self.y_at[1]),
            go(fy.at[1], ya.at[1, :, bottom], self.sems[0], at + 5, self.y_at[3]),
        ]

    def stage_two(self):
        me, term, ya, sa, zb, sb = self.me, self.term, self.ya, self.sa, self.zb, self.sb
        for copy in self.first_b:
            copy.wait_recv()

        def add_b(i, r):
            p, q = i // 4, i % 4
            here = pl.ds(r, TILE)
            there = pl.ds(pl.multiple_of(A_ROWS + me.z * B_PART + r, TILE), TILE)
            sb[p, q, here] = low(
                wide(term[p, q, there]) + wide(zb[0, p, q, here]) + wide(zb[1, p, q, here])
            )

        over_rows(self.planes * 4, B_PART, add_b)
        self.second = [
            self.go(
                sb.at[:, me.along_y(k)],
                self.yb.at[k - 1],
                self.sems[2],
                self.index * 3 + k - 1,
                self.y_at[k],
            )
            for k in ORDER
        ]
        for copy in self.first_a:
            copy.wait_recv()

        def add_a(p, r):
            here = pl.ds(r, TILE)
            sa[p, here] = low(
                wide(term[p, me.y, here]) + wide(ya[0, p, here]) + wide(ya[1, p, here])
            )

        over_rows(self.planes, A_ROWS, add_a)
        self.second += [
            self.go(
                sa.at[:, pl.ds(pl.multiple_of(me.along_z(k) * A_PART, TILE), A_PART)],
                self.za.at[k - 1],
                self.sems[3],
                self.index * 3 + k - 1,
                self.z_at[k],
            )
            for k in ORDER
        ]

    def stage_three(self):
        me, sa, za, sb, yb, ee = self.me, self.sa, self.za, self.sb, self.yb, self.ee
        for copy in self.second:
            copy.wait_recv()

        def add_a(p, r):
            here = pl.ds(r, TILE)
            there = pl.ds(pl.multiple_of(me.z * A_PART + r, TILE), TILE)
            ee[p, here] = low(
                wide(sa[p, there]) + wide(za[0, p, here]) + wide(za[1, p, here]) + wide(za[2, p, here])
            )

        def add_b(p, r):
            here = pl.ds(r, TILE)
            there = pl.ds(pl.multiple_of(A_PART + r, TILE), TILE)
            ee[p, there] = low(
                wide(sb[p, me.y, here])
                + wide(yb[0, p, here])
                + wide(yb[1, p, here])
                + wide(yb[2, p, here])
            )

        over_rows(self.planes, A_PART, add_a)
        over_rows(self.planes, B_PART, add_b)
        self.third = self.go(ee, self.ex, self.sems[4], self.index, self.side)

    def owned(self, source):
        return source % 2, (source // 2) * (A_ROWS // 2)

    def stage_four(self):
        me, ya, ee, ex = self.me, self.ya, self.ee, self.ex
        self.third.wait_recv()
        slot, base = self.owned(me.z)

        def add(p, r):
            there = pl.ds(pl.multiple_of(base + r, TILE), TILE)
            here = pl.ds(r, TILE)
            ya[slot, p, there] = low(wide(ee[p, here]) + wide(ex[p, here]))

        over_rows(self.planes, E_ROWS, add)
        mine = self.piece(0, 0, E_ROWS)
        at = self.index * 4
        near = (1, 3) if self.relayed else ORDER
        self.fourth = {k: self.go(mine, mine, self.sems[5], at + k - 1, self.z_at[k]) for k in near}

    def piece(self, k, start, rows):
        slot, base = self.owned(self.me.along_z(k))
        return self.ya.at[slot, :, pl.ds(pl.multiple_of(base + start, TILE), rows)]

    def relay(self):
        if not self.relayed:
            return
        at = self.index * 4
        self.fourth[1].wait_recv()
        piece = self.piece(3, 0, E_TOP)
        self.fourth[2] = self.go(piece, piece, self.sems[5], at + 1, self.z_at[1])
        self.fourth[3].wait_recv()
        piece = self.piece(1, E_TOP, E_ROWS - E_TOP)
        self.fourth[4] = self.go(piece, piece, self.sems[5], at + 3, self.z_at[3])

    def put(self, p, rows, value):
        if self.index in (2, 3):
            self.final[rows, self.index - 2] = value
        else:
            self.final[p, rows] = value

    def finish(self):
        me, ya = self.me, self.ya
        for k in (0,) + ORDER:
            if k == 2 and self.relayed:
                self.fourth[2].wait_recv()
                self.fourth[4].wait_recv()
            elif k and not self.relayed:
                self.fourth[k].wait_recv()
            source = me.along_z((4 - k) % 4)
            slot, base = self.owned(source)

            def put_a(p, r):
                there = pl.ds(pl.multiple_of(source * A_PART + r, TILE), TILE)
                here = pl.ds(pl.multiple_of(base + r, TILE), TILE)
                self.put(p, there, wide(ya[slot, p, here]))

            def put_b(p, r):
                there = pl.ds(pl.multiple_of(A_ROWS + source * B_PART + r, TILE), TILE)
                here = pl.ds(pl.multiple_of(base + A_PART + r, TILE), TILE)
                self.put(p, there, wide(ya[slot, p, here]))

            over_rows(self.planes, A_PART, put_a)
            over_rows(self.planes, B_PART, put_b)


def first_with_first(left, right):
    return lax.dot_general(
        left, right, (((0,), (0,)), ((), ())), preferred_element_type=jnp.float32
    )


def backward_kernel(*refs):
    (
        block_input,
        windows,
        gains,
        merge_gain,
        cells_back,
        triple_kept,
        output_kept,
        gate_up_kept,
        down_kept,
        attend,
        projected,
        heads_out,
        middle,
        feed,
        gate,
        upper,
        activated,
        block_out,
        rows_across,
        text,
        visual_terms,
    ) = refs[:21]
    sequence = refs[21]
    refs = refs[4:]
    input_gradient = refs[18]
    outs = (refs[19], refs[20], refs[21], refs[21], refs[22])
    gain_out = refs[23]
    refs = refs[24:]
    triple, output, gate_up, down, load = refs[:5]
    visual_in, following, text_part, part_sems = refs[5:9]
    visual = visual_in.at[0]
    refs = refs[9:]
    sum_one, sum_two = refs[:5], refs[5:10]
    terms = refs[10:15]
    buffers = [refs[15 + 10 * t : 25 + 10 * t] for t in range(5)]
    middle_back = input_gradient
    out_low, gate_up_back, triple_back, gain, gain_in, gain_sum = refs[65:71]
    middle_low = out_low
    sems = refs[71:]
    pair = [(sems[2 * i], sems[2 * i + 1]) for i in range(11)]
    loads = [
        local_copy(source, target, load.at[i])
        for i, (source, target) in enumerate(
            ((down_kept, down), (gate_up_kept, gate_up), (output_kept, output), (triple_kept, triple))
        )
    ]
    me = Place()
    y_at = {k: me.at(y=me.along_y(k)) for k in ORDER}
    z_at = {k: me.at(z=me.along_z(k)) for k in ORDER}
    side = me.at(low=1 - me.low)
    far = me.at(z=(me.z + 3 + 2 * me.low) % 4, low=1 - me.low)
    before = me.at(z=(me.z + 3 + me.low) % 4, low=1 - me.low)

    def peer(j, k):
        return me.at(y=me.along_y(k), high=(me.high + j) % 2)

    greet(
        [peer(j, k) for j, k in PAIRS]
        + [z_at[k] for k in ORDER]
        + [side, far, me.at(core=1 - me.core)]
    )
    pending = []

    def go(*arguments):
        copy = send(*arguments)
        pending.append(copy)
        return copy

    reductions = [
        Reduction(me, go, terms[t], outs[t], buffers[t], pair[:6], t, y_at, z_at, side)
        for t in range(5)
    ]
    of_triple, of_output, of_gate, of_upper, of_down = reductions

    def form(t, p, left, right):
        for i in range(2):
            block = first_with_first(left[:, i * 640 : (i + 1) * 640], right)
            terms[t][p, 2 * i : 2 * i + 2] = low(block).reshape(2, 320, right.shape[1])

    def whole(weight, p):
        return weight[p].reshape(1280, -1)

    scale_three = root_scale(block_out[...])
    out_back = norm_backward(cells_back[...], block_out[...], scale_three, merge_gain[...][None])
    middle_back[...] = out_back
    out_low[...] = low(out_back)
    form(4, 0, out_low, activated[...])
    of_down.stage_one()
    for copy in loads:
        copy.wait()
    activated_back = product(out_low[...], whole(down, 0))
    slope = jax.nn.sigmoid(gate[...])
    gate_up_back[1] = low(activated_back * gate[...] * slope)
    gate_up_back[0] = low(activated_back * upper[...] * slope * (1.0 + gate[...] * (1.0 - slope)))
    total = SumOverMp(me, go, sum_one, pair[6])
    total.begin(
        lambda rows: last_with_last(gate_up_back[0, rows], whole(gate_up, 0))
        + last_with_last(gate_up_back[1, rows], whole(gate_up, 1))
    )
    form(2, 0, feed, gate_up_back[0])
    of_gate.stage_one()
    of_down.stage_half()
    total.end()
    feed_back = wide(sum_one[4][...])
    scale_two = root_scale(middle[...])
    middle_back[...] = middle_back[...] + norm_backward(
        feed_back, middle[...], scale_two, gains[1:2]
    )
    middle_low[...] = low(middle_back[...])
    gain[...] = jnp.zeros_like(gain)
    gain[1:2] = jnp.sum(feed_back * middle[...] * scale_two, axis=0, keepdims=True)
    form(3, 0, feed, gate_up_back[1])
    of_upper.stage_one()
    of_gate.stage_half()
    heads_back = low(product(middle_low[...], whole(output, 0)))
    allowed = same_image(windows[...])
    query_back = jnp.zeros((256, 320), jnp.float32)
    key_back = jnp.zeros((256, 320), jnp.float32)
    value_back = jnp.zeros((256, 320), jnp.float32)
    for head in range(4):
        mask = head_mask(head)
        shares = head_shares(projected[0], projected[1], mask, allowed)
        share_back = last_with_last(heads_back * mask, projected[2])
        centre = jnp.sum(shares * share_back, axis=-1, keepdims=True)
        score_back = low(shares * (share_back - centre) * (1.0 / math.sqrt(HEAD_DIM)))
        query_back = query_back + product(score_back, projected[1] * mask)
        key_back = key_back + first_with_first(score_back, projected[0] * mask)
        value_back = value_back + first_with_first(low(shares), heads_back * mask)
    triple_back[0] = low(query_back)
    triple_back[1] = low(key_back)
    triple_back[2] = low(value_back)
    for p in range(3):
        form(0, p, attend, triple_back[p])
    of_triple.stage_one()
    form(1, 0, middle_low, heads_out[...])
    of_output.stage_one()
    of_upper.stage_half()
    of_down.stage_two()
    total = SumOverMp(me, go, sum_two, pair[7])
    total.begin(
        lambda rows: last_with_last(triple_back[0, rows], whole(triple, 0))
        + last_with_last(triple_back[1, rows], whole(triple, 1))
        + last_with_last(triple_back[2, rows], whole(triple, 2))
    )
    of_triple.stage_half()
    of_gate.stage_two()
    total.end()
    attend_back = wide(sum_two[4][...])
    start = wide(block_input[...])
    scale_one = root_scale(start)
    input_gradient[...] = middle_back[...] + norm_backward(attend_back, start, scale_one, gains[0:1])
    gain[0:1] = jnp.sum(attend_back * start * scale_one, axis=0, keepdims=True)
    gain_copies = [go(gain, gain_in.at[k - 1], pair[8], k - 1, y_at[k]) for k in ORDER]
    of_down.stage_three()
    of_output.stage_half()
    of_upper.stage_two()
    own_visual = local_copy(
        visual_terms.at[me.high, pl.ds(pl.multiple_of(me.y * 64, 64), 64)],
        visual_in.at[0],
        part_sems.at[0],
    )
    visual_copies = []
    for j, k in PAIRS:
        rows = pl.ds(pl.multiple_of(me.along_y(k) * 64, 64), 64)
        region = visual_terms.at[(me.high + j) % 2, rows]
        visual_copies.append(go(region, visual_in.at[j * 4 + k], pair[9], j * 4 + k, peer(j, k)))
    of_gate.stage_three()
    of_down.stage_four()
    for copy in gain_copies:
        copy.wait_recv()
    gain_sum[0] = gain[...] + gain_in[0] + gain_in[1] + gain_in[2]
    gain_copies = [go(gain_sum.at[0], gain_in.at[2 + k], pair[8], 2 + k, z_at[k]) for k in ORDER]
    of_triple.stage_two()
    of_upper.stage_three()
    of_gate.stage_four()
    of_down.relay()
    of_output.stage_two()
    for copy in gain_copies:
        copy.wait_recv()
    gain_sum[1] = gain_sum[0] + gain_in[3] + gain_in[4] + gain_in[5]
    gain_copies = [go(gain_sum.at[1], gain_in.at[6], pair[8], 6, side)]
    of_triple.stage_three()
    of_upper.stage_four()
    of_gate.relay()
    of_output.stage_three()
    own_visual.wait()
    for copy in visual_copies:
        copy.wait_recv()

    @pl.loop(0, 4)
    def _(i):
        here = pl.ds(pl.multiple_of(i * 16, 16), 16)
        total = wide(visual_in[0, here])
        for j, k in PAIRS:
            total = total + wide(visual_in[j * 4 + k, here])
        visual[here] = low(total)

    visual_copy = go(visual, following, pair[10], 0, before)
    for copy in gain_copies:
        copy.wait_recv()
    gain_out[...] = gain_sum[1, :2] + gain_in[6, :2]
    of_triple.stage_four()
    of_upper.relay()
    of_output.stage_four()
    slot = lax.broadcasted_iota(jnp.int32, (256, 64), 1)
    rows_down = upright(rows_across[...])
    offset = (me.z * 2 + me.low) * 64
    here_cells = jnp.where(rows_down - offset == slot, 1.0, 0.0).astype(jnp.bfloat16)
    next_cells = jnp.where(rows_down - offset - 64 == slot, 1.0, 0.0).astype(jnp.bfloat16)
    visual_copy.wait_recv()
    for i in range(4):
        span = pl.ds(i * STEP, STEP)
        local_copy(text.at[:, span], text_part, part_sems.at[1]).wait()
        picked = product(here_cells, visual[:, span]) + product(next_cells, following[:, span])
        text_part[...] = jnp.where(rows_down >= 0, low(picked), text_part[...])
        local_copy(text_part, sequence.at[:, span], part_sems.at[2]).wait()
    for reduction in (of_down, of_gate, of_upper, of_triple, of_output):
        reduction.finish()
    for copy in pending:
        copy.wait_send()


def block_backward(
    block_input, windows, gains, merge_gain, cells_back, wholes, saved, cell_rows, text, visual_terms
):
    rows, width = block_input.shape
    units = saved[5].shape[1]

    def low_buffer(*shape):
        return pltpu.VMEM(shape, jnp.bfloat16)

    def wide_buffer(*shape):
        return pltpu.VMEM(shape, jnp.float32)

    sizes = ((3, 320), (1, 320), (1, units), (1, units), (1, units))
    scratch = [low_buffer(*whole.shape) for whole in wholes]
    scratch += [pltpu.SemaphoreType.DMA((4,)), low_buffer(8, 64, 2048)]
    scratch += [low_buffer(64, 2048), low_buffer(rows, STEP), pltpu.SemaphoreType.DMA((3,))]
    scratch += sum_buffers() + sum_buffers()
    scratch += [low_buffer(planes, 4, 320, columns) for planes, columns in sizes]
    for planes, columns in sizes:
        scratch += [
            low_buffer(2, planes, A_ROWS, columns),
            low_buffer(2, planes, A_HALF, columns),
            low_buffer(planes, A_ROWS, columns),
            low_buffer(3, planes, A_PART, columns),
            low_buffer(2, planes, 4, B_PART, columns),
            low_buffer(2, planes, 4, B_HALF, columns),
            low_buffer(planes, 4, B_PART, columns),
            low_buffer(3, planes, B_PART, columns),
            low_buffer(planes, E_ROWS, columns),
            low_buffer(planes, E_ROWS, columns),
        ]
    scratch += [
        low_buffer(rows, width),
        low_buffer(2, rows, units),
        low_buffer(3, rows, 320),
        wide_buffer(8, width),
        wide_buffer(7, 8, width),
        wide_buffer(2, 8, width),
    ]
    for size in (30, 30, 15, 15, 5, 20, 3 * CHUNKS, 3 * CHUNKS, 7, 8, 1):
        scratch += sem_pair(size)
    operands = [
        block_input,
        windows,
        gains,
        merge_gain,
        cells_back,
        *wholes,
        *saved,
        cell_rows,
        text,
        visual_terms,
    ]
    outs = (
        [jax.ShapeDtypeStruct(text.shape, jnp.bfloat16)]
        + [jax.ShapeDtypeStruct((rows, width), jnp.float32)]
        + [
            jax.ShapeDtypeStruct(dims, jnp.float32)
            for dims in ((3, 320, 320), (1, 320, 320), (320, 2, units), (1, 320, units))
        ]
        + [jax.ShapeDtypeStruct((2, width), jnp.float32)]
    )
    results = pl.pallas_call(
        backward_kernel,
        out_shape=outs,
        in_specs=[VMEM] * 5 + [ANY] * 4 + [VMEM] * (len(operands) - 11) + [ANY] * 2,
        out_specs=[ANY] + [VMEM] * (len(outs) - 1),
        scratch_shapes=scratch,
        compiler_params=pltpu.CompilerParams(
            collective_id=3, has_side_effects=True, vmem_limit_bytes=VMEM_LIMIT
        ),
        name="block_backward",
    )(*operands)

    return results[0], results[1], results[2:6], results[6]


def planes_of(weight):
    return jnp.transpose(weight, (1, 0, 2))


def local(
    block_input,
    windows,
    cell_rows,
    text_vectors,
    sequence_cotangent,
    norm_gains,
    merge_gain,
    triple_weight,
    output_weight,
    gate_up_weight,
    down_weight,
    merge_up,
    merge_down,
):
    patches = block_input[0]
    shards = (
        planes_of(triple_weight),
        output_weight[None],
        planes_of(gate_up_weight),
        down_weight[None],
    )
    wholes, saved, backs = block_forward(
        patches,
        windows,
        norm_gains,
        merge_gain,
        cell_rows,
        sequence_cotangent[0],
        shards,
    )
    visual_terms, cells_back = merger(
        saved[-1],
        backs,
        merge_up.T,
        merge_down,
    )
    sequence, input_gradient, gradients, gain_gradient = block_backward(
        patches,
        windows,
        norm_gains,
        merge_gain,
        cells_back,
        wholes,
        saved[:-1],
        cell_rows,
        text_vectors[0],
        visual_terms,
    )
    return (
        sequence[None],
        input_gradient[None],
        planes_of(gradients[0]),
        gradients[1][0],
        gradients[2],
        gradients[3][0],
        gain_gradient,
    )


def solution(mesh):
    placed = (
        P(("dp", "section"), None, None),
        P(("dp", "section"), None),
        P("section", "dp"),
        P("section", "dp", "mp"),
        P("section", "dp", "mp"),
        P(),
        P(),
        P("section", None, "mp"),
        P("section", "mp"),
        P("section", None, "mp"),
        P("section", "mp"),
        P(None, ("section", "mp")),
        P(("section", "mp"), None),
    )
    return jax.shard_map(
        local,
        mesh=mesh,
        in_specs=placed,
        out_specs=(
            P("section", "dp", "mp"),
            P(("dp", "section"), None, None),
            P("section", None, "mp"),
            P("section", "mp"),
            P("section", None, "mp"),
            P("section", "mp"),
            P(),
        ),
        check_vma=False,
    )
```

```python
import functools
import math

import jax
import jax.numpy as jnp
from jax import lax
from jax.experimental import pallas as pl
from jax.experimental.pallas import tpu as pltpu
from jax.sharding import PartitionSpec as P

HEAD_DIM = 80


epsilon = 1e-06
root_half = 0.7071067811865476
density_scale = 0.3989422804014327

MESH = pl.DeviceIdType.MESH
VMEM_LIMIT = 62 * 1024 * 1024
VMEM = pl.BlockSpec(memory_space=pltpu.VMEM)
ANY = pl.BlockSpec(memory_space=pl.ANY)


def upright(row):
    count = row.shape[1]
    across = lax.broadcasted_iota(jnp.int32, (count, count), 1)
    down = lax.broadcasted_iota(jnp.int32, (count, count), 0)
    return jnp.sum(jnp.where(across == down, row, 0), axis=1, keepdims=True)


def same_image(windows):
    across = lax.broadcasted_iota(jnp.int32, (64, 256), 1) // 4
    down = lax.broadcasted_iota(jnp.int32, (64, 256), 0)
    column = upright(windows)
    of_patch = jnp.sum(jnp.where(across == down, column, 0), axis=0, keepdims=True)
    return upright(of_patch) == of_patch


def local_copy(source, target, sem):
    copy = pltpu.make_async_copy(source, target, sem)
    copy.start()
    return copy


class Place:
    def __init__(self):
        dp, self.y, mp = lax.axis_index("dp"), lax.axis_index("section"), lax.axis_index("mp")
        self.z, self.low = dp // 2, dp % 2
        self.high, self.core = mp // 2, mp % 2

    def at(self, z=None, low=None, y=None, high=None, core=None):
        z = self.z if z is None else z
        low = self.low if low is None else low
        y = self.y if y is None else y
        high = self.high if high is None else high
        core = self.core if core is None else core
        return (z * 2 + low, y, high * 2 + core)

    def along_y(self, k):
        return (self.y + k) % 4

    def along_z(self, k):
        return (self.z + k) % 4


def greet(devices):
    barrier = pltpu.get_barrier_semaphore()
    for device in devices:
        pl.semaphore_signal(barrier, inc=1, device_id=device, device_id_type=MESH)
    pl.semaphore_wait(barrier, len(devices))


def send(source, target, sems, index, device):
    copy = pltpu.make_async_remote_copy(
        src_ref=source,
        dst_ref=target,
        send_sem=sems[0].at[index],
        recv_sem=sems[1].at[index],
        device_id=device,
        device_id_type=MESH,
    )
    copy.start()
    return copy


def sem_pair(*shape):
    return [pltpu.SemaphoreType.DMA(shape), pltpu.SemaphoreType.DMA(shape)]


def wide(values):
    return values.astype(jnp.float32)


def low(values):
    return values.astype(jnp.bfloat16)


def root_scale(values):
    return lax.rsqrt(jnp.mean(values * values, axis=-1, keepdims=True) + epsilon)


def norm_backward(cotangent, values, scale, gain):
    weighted = cotangent * gain
    return scale * weighted - values * scale**3 * jnp.mean(
        weighted * values, axis=-1, keepdims=True
    )


def gelu_value(values):
    return 0.5 * values * (1.0 + jax.scipy.special.erf(values * root_half))


def gelu_slope(values):
    return (
        0.5 * (1.0 + jax.scipy.special.erf(values * root_half))
        + values * jnp.exp(-0.5 * values * values) * density_scale
    )


def product(left, right):
    return jnp.dot(left, right, preferred_element_type=jnp.float32)


QUARTER, HALF = 48, 48
ALONE = 320 - 4 * QUARTER - 2 * HALF
UNITS = ((0, 0, 3), (1, 0, 1), (2, 0, 1), (2, 1, 1), (3, 0, 1))
SHARE_Z = ({1: (0, 16), 3: (16, 32)}, {1: (0, 32), 3: (32, 16)})
SHARE = ({1: (0, 32), 3: (32, 16)}, {1: (0, 16), 3: (16, 32)}, {1: (0, 16), 3: (16, 16)})
PAIRS = [(j, k) for k in (1, 3, 2) for j in (0, 1)] + [(1, 0)]


STEP = 512


def last_with_last(left, right):
    return lax.dot_general(
        left, right, (((1,), (1,)), ((), ())), preferred_element_type=jnp.float32
    )


def merger_kernel(
    merged,
    backs_kept,
    up_kept,
    down_kept,
    visual_terms,
    gradient,
    backs,
    up,
    down,
    cells_back,
    apart,
    cells,
    pre,
    hidden,
    pre_back,
    hidden_back,
    terms,
    terms_in,
    pieces,
    pieces_in,
    parts,
    parts_in,
    *sems,
):
    me = Place()
    load, *sems = sems
    merged_s, share_s, terms_s, pieces_s, parts_s, mp_s = [
        (sems[2 * i], sems[2 * i + 1]) for i in range(6)
    ]
    loads = [
        local_copy(source, target, load.at[i])
        for i, (source, target) in enumerate(
            ((down_kept, down), (backs_kept, backs), (up_kept, up))
        )
    ]
    sibling, partner = me.at(core=1 - me.core), me.at(high=1 - me.high)

    def peer(j, k):
        return me.at(y=me.along_y(k), high=(me.high + j) % 2)

    greet([peer(j, k) for j, k in PAIRS] + [sibling])
    pending = []

    def go(*arguments):
        copy = send(*arguments)
        pending.append(copy)
        return copy

    half = pl.ds(pl.multiple_of(me.core * 32, 32), 32)
    merged_copies = {
        k: go(merged.at[half], cells.at[me.y, half], merged_s, k, peer(0, k)) for k in (1, 3, 2)
    }
    cells[me.y] = merged[...]
    own = me.high * 2 + me.core
    hidden_back[...] = jnp.zeros_like(hidden_back)
    for copy in loads:
        copy.wait()

    @pl.loop(0, 16)
    def _(i):
        inner = pl.ds(pl.multiple_of((i % 4) * STEP, STEP), STEP)
        outer = pl.ds(pl.multiple_of(i * STEP, STEP), STEP)
        left = backs[:, i // 4, :, inner].reshape(256, STEP)
        hidden_back[...] += last_with_last(left, down[:, outer])

    share_copies = []
    for k in (1, 3, 2):
        merged_copies[k].wait_recv()
        region = cells.at[me.along_y(4 - k), half]
        share_copies.append(go(region, region, share_s, k, sibling))
    for copy in share_copies:
        copy.wait_recv()

    pre[...] = jnp.zeros_like(pre)

    @pl.loop(0, 10)
    def _(i):
        span = pl.ds(pl.multiple_of(i * STEP, STEP), STEP)
        pre[...] += last_with_last(cells[:, :, span].reshape(256, STEP), up[:, span])

    pre_back[...] = low(hidden_back[...] * gelu_slope(pre[...]))

    @pl.loop(0, 10)
    def _(i):
        span = pl.ds(pl.multiple_of(i * STEP, STEP), STEP)
        pieces[:, :, :, :, span] = low(product(pre_back[...], up[:, span])).reshape(4, 2, 2, 16, STEP)

    pieces_copy = go(pieces.at[:, :, 1 - me.core], pieces_in, pieces_s, 0, sibling)
    hidden[...] = low(gelu_value(pre[...]))
    pieces_copy.wait_recv()

    @pl.loop(0, 8)
    def _(i):
        a, b = i // 2, i % 2
        for n in range(4):
            span = pl.ds(n * 1280, 1280)
            parts[a, b, :, span] = low(
                wide(pieces[a, b, me.core, :, span]) + wide(pieces_in[a, b, :, span])
            )

    part_copies = [
        go(parts.at[me.along_y(k), (me.high + j) % 2], parts_in.at[j * 4 + k], parts_s, j * 4 + k, peer(j, k))
        for j, k in PAIRS
    ]

    def term_block(column):
        @pl.loop(0, 4)
        def _(i):
            span = pl.ds(pl.multiple_of(i * STEP, STEP), STEP)
            whole = pl.ds(pl.multiple_of(column * 2048 + i * STEP, STEP), STEP)
            terms[column, :, span] = low(product(hidden[...], down[:, whole]))

    term_copies = []
    for j in (0, 1):
        column = j * 2 + 1 - me.core
        term_block(column)
        term_copies.append(go(terms.at[column], terms_in.at[j], terms_s, j, sibling))
    for j in (0, 1):
        column = j * 2 + me.core
        term_block(column)
        term_copies[j].wait_recv()

        @pl.loop(0, 16)
        def _(i):
            here = pl.ds(pl.multiple_of(i * 16, 16), 16)
            visual_terms[j, here] = low(wide(terms[column, here]) + wide(terms_in[j, here]))

    for copy in part_copies:
        copy.wait_recv()
    mine = pl.ds(pl.multiple_of(own * 16, 16), 16)
    for n in range(4):
        span = pl.ds(n * 1280, 1280)
        total = wide(parts[me.y, me.high, :, span])
        for j, k in PAIRS:
            total = total + wide(parts_in[j * 4 + k, :, span])
        cells_back[mine, span] = low(total)
    mp_copies = [
        go(cells_back.at[mine], cells_back.at[mine], mp_s, 0, partner),
        go(cells_back.at[mine], cells_back.at[mine], mp_s, 1, sibling),
    ]
    mp_copies[0].wait_recv()
    theirs = pl.ds(pl.multiple_of(((1 - me.high) * 2 + me.core) * 16, 16), 16)
    mp_copies.append(go(cells_back.at[theirs], cells_back.at[theirs], mp_s, 2, sibling))

    mp_copies[1].wait_recv()
    mp_copies[2].wait_recv()
    for i in range(10):
        for j in range(4):
            there = pl.ds(j * 1280 + i * 128, 128)
            apart[i, pl.ds(j, 64, stride=4), :] = wide(cells_back[:, there])
        gradient[:, i * 128 : (i + 1) * 128] = apart[i]
    for copy in pending:
        copy.wait_send()


def merger(merged, backs, up, down):
    def buffer(*shape):
        return pltpu.VMEM(shape, jnp.bfloat16)

    scratch = [
        buffer(*backs.shape),
        buffer(*up.shape),
        buffer(*down.shape),
        buffer(*merged.shape),
        pltpu.VMEM((10, 256, 128), jnp.float32),
        buffer(4, 64, 5120),
        pltpu.VMEM((256, 320), jnp.float32),
        buffer(256, 320),
        buffer(256, 320),
        pltpu.VMEM((256, 320), jnp.float32),
        buffer(4, 256, 2048),
        buffer(2, 256, 2048),
        buffer(4, 2, 2, 16, 5120),
        buffer(4, 2, 16, 5120),
        buffer(4, 2, 16, 5120),
        buffer(8, 16, 5120),
    ]
    scratch += [pltpu.SemaphoreType.DMA((3,))]
    for size in (4, 4, 2, 1, 8, 3):
        scratch += sem_pair(size)
    return pl.pallas_call(
        merger_kernel,
        out_shape=[
            jax.ShapeDtypeStruct((2, 256, 2048), jnp.bfloat16),
            jax.ShapeDtypeStruct((256, 1280), jnp.float32),
        ],
        in_specs=[VMEM] + [ANY] * 3,
        out_specs=[VMEM] * 2,
        scratch_shapes=scratch,
        compiler_params=pltpu.CompilerParams(
            collective_id=4, has_side_effects=True, vmem_limit_bytes=VMEM_LIMIT
        ),
        name="merger",
    )(merged, backs, up, down)


CHUNKS = 2


class SumOverMp:
    def __init__(self, me, go, buffers, sems):
        self.me, self.go = me, go
        self.outgoing, self.got, self.half, self.other, self.total = buffers
        self.sems = sems
        self.sibling, self.partner = me.at(core=1 - me.core), me.at(high=1 - me.high)
        self.mine = pl.multiple_of(me.core * 128, 128)
        self.theirs = pl.multiple_of((1 - me.core) * 128, 128)

    def begin(self, compute):
        step = 128 // CHUNKS
        self.outgoing[...] = low(compute(pl.ds(self.theirs, 128)))
        first = []
        for k in range(CHUNKS):
            here = pl.ds(k * step, step)
            first.append(
                self.go(self.outgoing.at[here], self.got.at[here], self.sems, k, self.sibling)
            )
        self.half[...] = low(compute(pl.ds(self.mine, 128)))
        self.second = []
        for k in range(CHUNKS):
            here = pl.ds(k * step, step)
            first[k].wait_recv()
            self.half[here] = low(wide(self.half[here]) + wide(self.got[here]))
            self.second.append(
                self.go(self.half.at[here], self.other.at[here], self.sems, CHUNKS + k, self.partner)
            )

    def end(self):
        step = 128 // CHUNKS
        third = []
        for k in range(CHUNKS):
            here = pl.ds(k * step, step)
            there = pl.ds(pl.multiple_of(self.mine + k * step, step), step)
            self.second[k].wait_recv()
            self.total[there] = low(wide(self.half[here]) + wide(self.other[here]))
            third.append(
                self.go(
                    self.total.at[there], self.total.at[there], self.sems, 2 * CHUNKS + k, self.sibling
                )
            )
        for copy in third:
            copy.wait_recv()


def sum_buffers():
    half = pltpu.VMEM((128, 1280), jnp.bfloat16)
    return [half, half, half, half, pltpu.VMEM((256, 1280), jnp.bfloat16)]


def head_mask(head):
    lane = lax.broadcasted_iota(jnp.int32, (1, 320), 1)
    inside = (lane >= head * HEAD_DIM) & (lane < (head + 1) * HEAD_DIM)
    return jnp.where(inside, 1.0, 0.0).astype(jnp.bfloat16)


def head_shares(queries, keys, mask, allowed):
    scores = last_with_last(queries * mask, keys) * (1.0 / math.sqrt(HEAD_DIM))
    scores = jnp.where(allowed, scores, -1e30)
    raised = jnp.exp(scores - jnp.max(scores, axis=-1, keepdims=True))
    return raised / jnp.sum(raised, axis=-1, keepdims=True)


def forward_kernel(*refs):
    block_input, windows, gains, merge_gain, rows_across, cotangent = refs[:6]
    shards = refs[6:10]
    kept = refs[10:14]
    attend, projected, heads_out, middle, feed, gate, upper, activated, block_out, merged = refs[14:24]
    backs_kept = refs[24]
    wholes, backs = refs[25:29], refs[29]
    spill, spill_in, merged_wide = refs[30:33]
    sum_one, sum_two = refs[33:38], refs[38:43]
    own, keep, *pairs = refs[43:]
    y_s, z_s, x_s, one_s, two_s, dp_s, back_s, fore_s = [
        (pairs[2 * i], pairs[2 * i + 1]) for i in range(8)
    ]
    me = Place()
    others = (1, 3, 2)
    y_at = {k: me.at(y=me.along_y(k)) for k in others}
    z_at = {k: me.at(z=me.along_z(k)) for k in others}
    side, sibling = me.at(low=1 - me.low), me.at(core=1 - me.core)
    after = me.at(z=(me.z + me.low) % 4, low=1 - me.low)
    far = me.at(z=(me.z + 3 + 2 * me.low) % 4, low=1 - me.low)

    greet(
        [y_at[1], y_at[3], z_at[1], z_at[3], side, far, sibling, me.at(high=1 - me.high)]
    )
    pending = []

    def go(*arguments):
        copy = send(*arguments)
        pending.append(copy)
        return copy

    starts = (me.z * QUARTER, 4 * QUARTER + me.low * HALF, 320 - ALONE)
    sizes = (QUARTER, HALF, ALONE)
    local_copies, near, far_copies, along, onwards, relays = [], {}, {}, {}, {}, {}

    def rows_of(u, source, start, size):
        t, p, n = UNITS[u]
        return wholes[t].at[pl.ds(p, n), source, pl.ds(pl.multiple_of(start, 16), size)]

    def begin(u):
        t, p, n = UNITS[u]
        for d in (1, 3):
            for part in range(3):
                span = pl.ds(pl.multiple_of(starts[part], 16), sizes[part])
                near[u, d, part] = go(
                    shards[t].at[pl.ds(p, n), span],
                    wholes[t].at[pl.ds(p, n), me.y, span],
                    y_s,
                    u * 12 + (d // 2) * 3 + part,
                    y_at[d],
                )

    def onward(u, k):
        source = me.along_y(k)
        block = rows_of(u, source, starts[0], sizes[0])
        for e in (1, 3):
            along[u, k, e] = go(block, block, z_s, u * 12 + (k - 1) * 2 + e // 2, z_at[e])
        block = rows_of(u, source, starts[1], sizes[1])
        onwards[u, k] = go(block, block, x_s, u * 3 + k - 1, side)

    def relay_y(u):
        for d in (1, 3):
            for part in range(3):
                near[u, d, part].wait_recv()
                first, size = SHARE[part][d]
                block = rows_of(u, me.along_y(4 - d), starts[part] + first, size)
                far_copies[u, d, part] = go(
                    block, block, y_s, u * 12 + 6 + (d // 2) * 3 + part, y_at[d]
                )
        onward(u, 3)
        onward(u, 1)

    def distant(u):
        for d in (1, 3):
            for part in range(3):
                far_copies[u, d, part].wait_recv()
        onward(u, 2)

    def relay_z(u):
        for k in (3, 1, 2):
            for e in (1, 3):
                along[u, k, e].wait_recv()
                first, size = SHARE_Z[k % 2][e]
                block = rows_of(u, me.along_y(k), me.along_z(4 - e) * QUARTER + first, size)
                relays[u, k, e] = go(
                    block, block, z_s, u * 12 + 6 + (k - 1) * 2 + e // 2, z_at[e]
                )

    keeps = []

    def complete(u):
        t, p, n = UNITS[u]
        for k in (3, 1, 2):
            onwards[u, k].wait_recv()
            relays[u, k, 1].wait_recv()
            relays[u, k, 3].wait_recv()
        planes = pl.ds(p, n)
        keeps.append(local_copy(wholes[t].at[planes], kept[t].at[planes], keep.at[u]))

    def whole(t, p):
        return wholes[t][p].reshape(1280, -1)

    begin(0)
    begin(1)
    for t in range(4):
        local_copies.append(local_copy(shards[t], wholes[t].at[:, me.y], own.at[t]))
    slot = lax.broadcasted_iota(jnp.int32, (128, 256), 0)
    offset = (me.z * 2 + me.low) * 64
    taken = jnp.where(rows_across[...] - offset == slot, 1.0, 0.0).astype(jnp.bfloat16)
    column = me.high * 2 + me.core
    for i in range(4):
        span = pl.ds(i * STEP, STEP)
        arrived = low(product(taken, cotangent[:, span]))
        spill[:, span] = arrived[64:]
        backs[me.y, column, :, span] = arrived[:64]
    spill_copy = go(spill, spill_in, dp_s, 0, after)
    start = wide(block_input[...])
    attend[...] = low(start * root_scale(start) * gains[0:1])
    relay_y(0)
    begin(2)
    distant(0)
    relay_y(1)
    distant(1)
    begin(3)
    relay_z(0)
    spill_copy.wait_recv()
    for i in range(4):
        span = pl.ds(i * STEP, STEP)
        backs[me.y, column, :, span] = backs[me.y, column, :, span] + spill_in[:, span]
    block = backs.at[me.y, column]
    across = go(block, block, back_s, 0, me.at(high=1 - me.high))
    relay_z(1)
    for copy in local_copies:
        copy.wait()
    complete(0)
    for p in range(3):
        projected[p] = low(product(attend[...], whole(0, p)))
    relay_y(2)
    begin(4)
    distant(2)
    allowed = same_image(windows[...])
    mixed = jnp.zeros((256, 320), jnp.float32)
    for head in range(4):
        mask = head_mask(head)
        shares = head_shares(projected[0], projected[1], mask, allowed)
        mixed = mixed + product(low(shares), projected[2] * mask)
    heads_out[...] = low(mixed)
    complete(1)
    relay_y(3)
    distant(3)
    relay_z(2)
    total = SumOverMp(me, go, sum_one, one_s)
    total.begin(lambda rows: last_with_last(heads_out[rows], whole(1, 0)))
    relay_y(4)
    across.wait_recv()
    columns = (column, (1 - me.high) * 2 + me.core)
    back_copies, back_relays, fore_copies = {}, [], []
    for j in (0, 1):
        block = backs.at[me.y, columns[j]]
        for d in (1, 3):
            back_copies[j, d] = go(block, block, back_s, 1 + j * 2 + d // 2, y_at[d])
        fore_copies.append(go(block, block, fore_s, j * 4, sibling))
    distant(4)
    total.end()
    middle[...] = wide(block_input[...]) + wide(sum_one[4][...])
    feed[...] = low(middle[...] * root_scale(middle[...]) * gains[1:2])
    relay_z(3)
    complete(2)
    gate[...] = product(feed[...], whole(2, 0))
    relay_z(4)
    for (j, d), copy in back_copies.items():
        copy.wait_recv()
        source = me.along_y(4 - d)
        block = backs.at[source, columns[j], pl.ds(16 * (d - 1), 32)]
        back_relays.append(go(block, block, back_s, 5 + j * 2 + d // 2, y_at[d]))
        block = backs.at[source, columns[j]]
        fore_copies.append(go(block, block, fore_s, j * 4 + d, sibling))
    complete(3)
    upper[...] = product(feed[...], whole(2, 1))
    activated[...] = low(gate[...] * jax.nn.sigmoid(gate[...]) * upper[...])
    complete(4)
    total = SumOverMp(me, go, sum_two, two_s)
    total.begin(lambda rows: last_with_last(activated[rows], whole(3, 0)))
    for copy in back_relays:
        copy.wait_recv()
    for j in (0, 1):
        block = backs.at[me.along_y(2), columns[j]]
        fore_copies.append(go(block, block, fore_s, j * 4 + 2, sibling))
    for copy in fore_copies:
        copy.wait_recv()
    keeps.append(local_copy(backs, backs_kept, keep.at[len(UNITS)]))
    total.end()
    block_out[...] = middle[...] + wide(sum_two[4][...])
    scale_three = root_scale(block_out[...])
    for i in range(10):
        span = slice(i * 128, (i + 1) * 128)
        merged_wide[i] = block_out[:, span] * scale_three * merge_gain[span][None]
        for j in range(4):
            there = pl.ds(j * 1280 + i * 128, 128)
            merged[:, there] = low(merged_wide[i, pl.ds(j, 64, stride=4), :])
    for copy in keeps:
        copy.wait()
    for copy in pending:
        copy.wait_send()


def block_forward(block_input, windows, gains, merge_gain, cell_rows, cotangent, shards):
    rows, width = block_input.shape
    units = shards[2].shape[2]

    def shape(kind, *dims):
        return jax.ShapeDtypeStruct(dims, kind)

    low_, wide_ = jnp.bfloat16, jnp.float32
    outs = [shape(low_, s.shape[0], 4, *s.shape[1:]) for s in shards] + [
        shape(low_, rows, width),
        shape(low_, 3, rows, 320),
        shape(low_, rows, 320),
        shape(wide_, rows, width),
        shape(low_, rows, width),
        shape(wide_, rows, units),
        shape(wide_, rows, units),
        shape(low_, rows, units),
        shape(wide_, rows, width),
        shape(low_, rows // 4, 4 * width),
        shape(low_, 4, 4, 64, cotangent.shape[1]),
    ]
    spill = pltpu.VMEM((64, cotangent.shape[1]), jnp.bfloat16)
    scratch = [pltpu.VMEM(out.shape, jnp.bfloat16) for out in outs[:4] + outs[-1:]]
    scratch += [spill, spill, pltpu.VMEM((10, rows, 128), jnp.float32)]
    scratch += sum_buffers() + sum_buffers()
    scratch += [pltpu.SemaphoreType.DMA((4,)), pltpu.SemaphoreType.DMA((len(UNITS) + 1,))]
    for size in (60, 60, 15, 3 * CHUNKS, 3 * CHUNKS, 1, 9, 8):
        scratch += sem_pair(size)
    results = pl.pallas_call(
        forward_kernel,
        out_shape=outs,
        in_specs=[VMEM] * 10,
        out_specs=[ANY] * 4 + [VMEM] * (len(outs) - 5) + [ANY],
        scratch_shapes=scratch,
        compiler_params=pltpu.CompilerParams(
            collective_id=1, has_side_effects=True, vmem_limit_bytes=VMEM_LIMIT
        ),
        name="block_forward",
    )(
        block_input,
        windows,
        gains,
        merge_gain,
        cell_rows,
        cotangent,
        *shards,
    )
    return results[:4], results[4:14], results[14]


A_ROWS = 192
A_PART = A_ROWS // 4
B_PART = (320 - A_ROWS) // 4
E_ROWS = A_PART + B_PART
A_HALF, B_HALF = A_ROWS // 2, B_PART // 2
E_TOP = 48
TILE = 16
ORDER = (1, 3, 2)


def over_rows(planes, rows, body):
    tiles = rows // TILE

    @pl.loop(0, planes * tiles)
    def _(i):
        body(i // tiles, pl.multiple_of((i % tiles) * TILE, TILE))


class Reduction:
    def __init__(self, me, go, term, final, buffers, sems, index, y_at, z_at, side):
        self.me, self.go, self.term, self.final = me, go, term, final
        self.ya, self.fy, self.sa, self.za, self.zb, self.fz, self.sb, self.yb, self.ee, self.ex = buffers
        self.sems, self.index, self.y_at, self.z_at, self.side = sems, index, y_at, z_at, side
        self.planes = term.shape[0]
        self.relayed = index >= 2

    def stage_one(self):
        me, term, go, ya, zb = self.me, self.term, self.go, self.ya, self.zb
        top, bottom = pl.ds(0, A_HALF), pl.ds(A_HALF, A_HALF)
        at = self.index * 6

        def a_rows(k, span):
            return term.at[:, me.along_y(k), span]

        def b_rows(k, half):
            first = A_ROWS + me.along_z(k) * B_PART + half * B_HALF
            return term.at[:, :, pl.ds(pl.multiple_of(first, TILE), B_HALF)]

        up, down = self.y_at[1], self.y_at[3]
        sems = self.sems[0]
        self.far_a = [
            go(a_rows(2, top), self.fy.at[0], sems, at, up),
            go(a_rows(2, bottom), self.fy.at[1], sems, at + 1, down),
        ]
        up_z, down_z = self.z_at[1], self.z_at[3]
        sems_z = self.sems[1]
        self.far_b = [
            go(b_rows(2, 0), self.fz.at[0], sems_z, at, up_z),
            go(b_rows(2, 1), self.fz.at[1], sems_z, at + 1, down_z),
        ]
        self.first_a = [
            go(a_rows(1, bottom), ya.at[0, :, bottom], sems, at + 2, up),
            go(a_rows(3, top), ya.at[1, :, top], sems, at + 3, down),
        ]
        b_top, b_bottom = pl.ds(0, B_HALF), pl.ds(B_HALF, B_HALF)
        self.first_b = [
            go(b_rows(1, 1), zb.at[0, :, :, b_bottom], sems_z, at + 2, up_z),
            go(b_rows(3, 0), zb.at[1, :, :, b_top], sems_z, at + 3, down_z),
        ]

    def stage_half(self):
        me, term, go, fy, fz = self.me, self.term, self.go, self.fy, self.fz
        at = self.index * 6
        for copy in self.far_b + self.far_a:
            copy.wait_recv()

        def add_b(i, r):
            p, q = i // 4, i % 4
            here = pl.ds(r, TILE)
            first = pl.multiple_of(A_ROWS + me.along_z(1) * B_PART + r, TILE)
            fz[0, p, q, here] = low(wide(fz[0, p, q, here]) + wide(term[p, q, pl.ds(first, TILE)]))
            first = pl.multiple_of(A_ROWS + me.along_z(3) * B_PART + B_HALF + r, TILE)
            fz[1, p, q, here] = low(wide(fz[1, p, q, here]) + wide(term[p, q, pl.ds(first, TILE)]))

        def add_a(p, r):
            here = pl.ds(r, TILE)
            there = pl.ds(pl.multiple_of(A_HALF + r, TILE), TILE)
            fy[0, p, here] = low(wide(fy[0, p, here]) + wide(term[p, me.along_y(1), here]))
            fy[1, p, here] = low(wide(fy[1, p, here]) + wide(term[p, me.along_y(3), there]))

        over_rows(self.planes * 4, B_HALF, add_b)
        over_rows(self.planes, A_HALF, add_a)
        top, bottom = pl.ds(0, A_HALF), pl.ds(A_HALF, A_HALF)
        b_top, b_bottom = pl.ds(0, B_HALF), pl.ds(B_HALF, B_HALF)
        ya, zb = self.ya, self.zb
        self.first_b += [
            go(fz.at[0], zb.at[0, :, :, b_top], self.sems[1], at + 4, self.z_at[1]),
            go(fz.at[1], zb.at[1, :, :, b_bottom], self.sems[1], at + 5, self.z_at[3]),
        ]
        self.first_a += [
            go(fy.at[0], ya.at[0, :, top], self.sems[0], at + 4, self.y_at[1]),
            go(fy.at[1], ya.at[1, :, bottom], self.sems[0], at + 5, self.y_at[3]),
        ]

    def stage_two(self):
        me, term, ya, sa, zb, sb = self.me, self.term, self.ya, self.sa, self.zb, self.sb
        for copy in self.first_b:
            copy.wait_recv()

        def add_b(i, r):
            p, q = i // 4, i % 4
            here = pl.ds(r, TILE)
            there = pl.ds(pl.multiple_of(A_ROWS + me.z * B_PART + r, TILE), TILE)
            sb[p, q, here] = low(
                wide(term[p, q, there]) + wide(zb[0, p, q, here]) + wide(zb[1, p, q, here])
            )

        over_rows(self.planes * 4, B_PART, add_b)
        self.second = [
            self.go(
                sb.at[:, me.along_y(k)],
                self.yb.at[k - 1],
                self.sems[2],
                self.index * 3 + k - 1,
                self.y_at[k],
            )
            for k in ORDER
        ]
        for copy in self.first_a:
            copy.wait_recv()

        def add_a(p, r):
            here = pl.ds(r, TILE)
            sa[p, here] = low(
                wide(term[p, me.y, here]) + wide(ya[0, p, here]) + wide(ya[1, p, here])
            )

        over_rows(self.planes, A_ROWS, add_a)
        self.second += [
            self.go(
                sa.at[:, pl.ds(pl.multiple_of(me.along_z(k) * A_PART, TILE), A_PART)],
                self.za.at[k - 1],
                self.sems[3],
                self.index * 3 + k - 1,
                self.z_at[k],
            )
            for k in ORDER
        ]

    def stage_three(self):
        me, sa, za, sb, yb, ee = self.me, self.sa, self.za, self.sb, self.yb, self.ee
        for copy in self.second:
            copy.wait_recv()

        def add_a(p, r):
            here = pl.ds(r, TILE)
            there = pl.ds(pl.multiple_of(me.z * A_PART + r, TILE), TILE)
            ee[p, here] = low(
                wide(sa[p, there]) + wide(za[0, p, here]) + wide(za[1, p, here]) + wide(za[2, p, here])
            )

        def add_b(p, r):
            here = pl.ds(r, TILE)
            there = pl.ds(pl.multiple_of(A_PART + r, TILE), TILE)
            ee[p, there] = low(
                wide(sb[p, me.y, here])
                + wide(yb[0, p, here])
                + wide(yb[1, p, here])
                + wide(yb[2, p, here])
            )

        over_rows(self.planes, A_PART, add_a)
        over_rows(self.planes, B_PART, add_b)
        self.third = self.go(ee, self.ex, self.sems[4], self.index, self.side)

    def owned(self, source):
        return source % 2, (source // 2) * (A_ROWS // 2)

    def stage_four(self):
        me, ya, ee, ex = self.me, self.ya, self.ee, self.ex
        self.third.wait_recv()
        slot, base = self.owned(me.z)

        def add(p, r):
            there = pl.ds(pl.multiple_of(base + r, TILE), TILE)
            here = pl.ds(r, TILE)
            ya[slot, p, there] = low(wide(ee[p, here]) + wide(ex[p, here]))

        over_rows(self.planes, E_ROWS, add)
        mine = self.piece(0, 0, E_ROWS)
        at = self.index * 4
        near = (1, 3) if self.relayed else ORDER
        self.fourth = {k: self.go(mine, mine, self.sems[5], at + k - 1, self.z_at[k]) for k in near}

    def piece(self, k, start, rows):
        slot, base = self.owned(self.me.along_z(k))
        return self.ya.at[slot, :, pl.ds(pl.multiple_of(base + start, TILE), rows)]

    def relay(self):
        if not self.relayed:
            return
        at = self.index * 4
        self.fourth[1].wait_recv()
        piece = self.piece(3, 0, E_TOP)
        self.fourth[2] = self.go(piece, piece, self.sems[5], at + 1, self.z_at[1])
        self.fourth[3].wait_recv()
        piece = self.piece(1, E_TOP, E_ROWS - E_TOP)
        self.fourth[4] = self.go(piece, piece, self.sems[5], at + 3, self.z_at[3])

    def put(self, p, rows, value):
        if self.index in (2, 3):
            self.final[rows, self.index - 2] = value
        else:
            self.final[p, rows] = value

    def finish(self):
        me, ya = self.me, self.ya
        for k in (0,) + ORDER:
            if k == 2 and self.relayed:
                self.fourth[2].wait_recv()
                self.fourth[4].wait_recv()
            elif k and not self.relayed:
                self.fourth[k].wait_recv()
            source = me.along_z((4 - k) % 4)
            slot, base = self.owned(source)

            def put_a(p, r):
                there = pl.ds(pl.multiple_of(source * A_PART + r, TILE), TILE)
                here = pl.ds(pl.multiple_of(base + r, TILE), TILE)
                self.put(p, there, wide(ya[slot, p, here]))

            def put_b(p, r):
                there = pl.ds(pl.multiple_of(A_ROWS + source * B_PART + r, TILE), TILE)
                here = pl.ds(pl.multiple_of(base + A_PART + r, TILE), TILE)
                self.put(p, there, wide(ya[slot, p, here]))

            over_rows(self.planes, A_PART, put_a)
            over_rows(self.planes, B_PART, put_b)


def first_with_first(left, right):
    return lax.dot_general(
        left, right, (((0,), (0,)), ((), ())), preferred_element_type=jnp.float32
    )


def backward_kernel(*refs):
    (
        block_input,
        windows,
        gains,
        merge_gain,
        cells_back,
        triple_kept,
        output_kept,
        gate_up_kept,
        down_kept,
        attend,
        projected,
        heads_out,
        middle,
        feed,
        gate,
        upper,
        activated,
        block_out,
        rows_across,
        text,
        visual_terms,
    ) = refs[:21]
    sequence = refs[21]
    refs = refs[4:]
    input_gradient = refs[18]
    outs = (refs[19], refs[20], refs[21], refs[21], refs[22])
    gain_out = refs[23]
    refs = refs[24:]
    triple, output, gate_up, down, load = refs[:5]
    visual_in, following, text_part, part_sems = refs[5:9]
    visual = visual_in.at[0]
    refs = refs[9:]
    sum_one, sum_two = refs[:5], refs[5:10]
    terms = refs[10:15]
    buffers = [refs[15 + 10 * t : 25 + 10 * t] for t in range(5)]
    middle_back = input_gradient
    out_low, gate_up_back, triple_back, gain, gain_in, gain_sum = refs[65:71]
    middle_low = out_low
    sems = refs[71:]
    pair = [(sems[2 * i], sems[2 * i + 1]) for i in range(11)]
    loads = [
        local_copy(source, target, load.at[i])
        for i, (source, target) in enumerate(
            ((down_kept, down), (gate_up_kept, gate_up), (output_kept, output), (triple_kept, triple))
        )
    ]
    me = Place()
    y_at = {k: me.at(y=me.along_y(k)) for k in ORDER}
    z_at = {k: me.at(z=me.along_z(k)) for k in ORDER}
    side = me.at(low=1 - me.low)
    far = me.at(z=(me.z + 3 + 2 * me.low) % 4, low=1 - me.low)
    before = me.at(z=(me.z + 3 + me.low) % 4, low=1 - me.low)

    def peer(j, k):
        return me.at(y=me.along_y(k), high=(me.high + j) % 2)

    greet(
        [peer(j, k) for j, k in PAIRS]
        + [z_at[k] for k in ORDER]
        + [side, far, me.at(core=1 - me.core)]
    )
    pending = []

    def go(*arguments):
        copy = send(*arguments)
        pending.append(copy)
        return copy

    reductions = [
        Reduction(me, go, terms[t], outs[t], buffers[t], pair[:6], t, y_at, z_at, side)
        for t in range(5)
    ]
    of_triple, of_output, of_gate, of_upper, of_down = reductions

    def form(t, p, left, right):
        for i in range(2):
            block = first_with_first(left[:, i * 640 : (i + 1) * 640], right)
            terms[t][p, 2 * i : 2 * i + 2] = low(block).reshape(2, 320, right.shape[1])

    def whole(weight, p):
        return weight[p].reshape(1280, -1)

    scale_three = root_scale(block_out[...])
    out_back = norm_backward(cells_back[...], block_out[...], scale_three, merge_gain[...][None])
    middle_back[...] = out_back
    out_low[...] = low(out_back)
    form(4, 0, out_low, activated[...])
    of_down.stage_one()
    for copy in loads:
        copy.wait()
    activated_back = product(out_low[...], whole(down, 0))
    slope = jax.nn.sigmoid(gate[...])
    gate_up_back[1] = low(activated_back * gate[...] * slope)
    gate_up_back[0] = low(activated_back * upper[...] * slope * (1.0 + gate[...] * (1.0 - slope)))
    total = SumOverMp(me, go, sum_one, pair[6])
    total.begin(
        lambda rows: last_with_last(gate_up_back[0, rows], whole(gate_up, 0))
        + last_with_last(gate_up_back[1, rows], whole(gate_up, 1))
    )
    form(2, 0, feed, gate_up_back[0])
    of_gate.stage_one()
    of_down.stage_half()
    total.end()
    feed_back = wide(sum_one[4][...])
    scale_two = root_scale(middle[...])
    middle_back[...] = middle_back[...] + norm_backward(
        feed_back, middle[...], scale_two, gains[1:2]
    )
    middle_low[...] = low(middle_back[...])
    gain[...] = jnp.zeros_like(gain)
    gain[1:2] = jnp.sum(feed_back * middle[...] * scale_two, axis=0, keepdims=True)
    form(3, 0, feed, gate_up_back[1])
    of_upper.stage_one()
    of_gate.stage_half()
    of_down.stage_two()
    heads_back = low(product(middle_low[...], whole(output, 0)))
    allowed = same_image(windows[...])
    query_back = jnp.zeros((256, 320), jnp.float32)
    key_back = jnp.zeros((256, 320), jnp.float32)
    value_back = jnp.zeros((256, 320), jnp.float32)
    for head in range(4):
        mask = head_mask(head)
        shares = head_shares(projected[0], projected[1], mask, allowed)
        share_back = last_with_last(heads_back * mask, projected[2])
        centre = jnp.sum(shares * share_back, axis=-1, keepdims=True)
        score_back = low(shares * (share_back - centre) * (1.0 / math.sqrt(HEAD_DIM)))
        query_back = query_back + product(score_back, projected[1] * mask)
        key_back = key_back + first_with_first(score_back, projected[0] * mask)
        value_back = value_back + first_with_first(low(shares), heads_back * mask)
    triple_back[0] = low(query_back)
    triple_back[1] = low(key_back)
    triple_back[2] = low(value_back)
    for p in range(3):
        form(0, p, attend, triple_back[p])
    of_triple.stage_one()
    form(1, 0, middle_low, heads_out[...])
    of_output.stage_one()
    of_upper.stage_half()
    total = SumOverMp(me, go, sum_two, pair[7])
    total.begin(
        lambda rows: last_with_last(triple_back[0, rows], whole(triple, 0))
        + last_with_last(triple_back[1, rows], whole(triple, 1))
        + last_with_last(triple_back[2, rows], whole(triple, 2))
    )
    of_triple.stage_half()
    of_gate.stage_two()
    total.end()
    attend_back = wide(sum_two[4][...])
    start = wide(block_input[...])
    scale_one = root_scale(start)
    input_gradient[...] = middle_back[...] + norm_backward(attend_back, start, scale_one, gains[0:1])
    gain[0:1] = jnp.sum(attend_back * start * scale_one, axis=0, keepdims=True)
    gain_copies = [go(gain, gain_in.at[k - 1], pair[8], k - 1, y_at[k]) for k in ORDER]
    of_down.stage_three()
    of_output.stage_half()
    of_upper.stage_two()
    of_gate.stage_three()
    of_down.stage_four()
    for copy in gain_copies:
        copy.wait_recv()
    gain_sum[0] = gain[...] + gain_in[0] + gain_in[1] + gain_in[2]
    gain_copies = [go(gain_sum.at[0], gain_in.at[2 + k], pair[8], 2 + k, z_at[k]) for k in ORDER]
    of_triple.stage_two()
    own_visual = local_copy(
        visual_terms.at[me.high, pl.ds(pl.multiple_of(me.y * 64, 64), 64)],
        visual_in.at[0],
        part_sems.at[0],
    )
    visual_copies = []
    for j, k in PAIRS:
        rows = pl.ds(pl.multiple_of(me.along_y(k) * 64, 64), 64)
        region = visual_terms.at[(me.high + j) % 2, rows]
        visual_copies.append(go(region, visual_in.at[j * 4 + k], pair[9], j * 4 + k, peer(j, k)))
    of_upper.stage_three()
    of_gate.stage_four()
    of_down.relay()
    of_output.stage_two()
    for copy in gain_copies:
        copy.wait_recv()
    gain_sum[1] = gain_sum[0] + gain_in[3] + gain_in[4] + gain_in[5]
    gain_copies = [go(gain_sum.at[1], gain_in.at[6], pair[8], 6, side)]
    of_triple.stage_three()
    of_upper.stage_four()
    of_gate.relay()
    of_output.stage_three()
    for copy in gain_copies:
        copy.wait_recv()
    gain_out[...] = gain_sum[1, :2] + gain_in[6, :2]
    of_triple.stage_four()
    own_visual.wait()
    for copy in visual_copies:
        copy.wait_recv()

    @pl.loop(0, 4)
    def _(i):
        here = pl.ds(pl.multiple_of(i * 16, 16), 16)
        total = wide(visual_in[0, here])
        for j, k in PAIRS:
            total = total + wide(visual_in[j * 4 + k, here])
        visual[here] = low(total)

    visual_copy = go(visual, following, pair[10], 0, before)
    of_upper.relay()
    of_output.stage_four()
    slot = lax.broadcasted_iota(jnp.int32, (256, 64), 1)
    rows_down = upright(rows_across[...])
    offset = (me.z * 2 + me.low) * 64
    here_cells = jnp.where(rows_down - offset == slot, 1.0, 0.0).astype(jnp.bfloat16)
    next_cells = jnp.where(rows_down - offset - 64 == slot, 1.0, 0.0).astype(jnp.bfloat16)
    visual_copy.wait_recv()
    for i in range(4):
        span = pl.ds(i * STEP, STEP)
        local_copy(text.at[:, span], text_part, part_sems.at[1]).wait()
        picked = product(here_cells, visual[:, span]) + product(next_cells, following[:, span])
        text_part[...] = jnp.where(rows_down >= 0, low(picked), text_part[...])
        local_copy(text_part, sequence.at[:, span], part_sems.at[2]).wait()
    for reduction in (of_down, of_gate, of_upper, of_triple, of_output):
        reduction.finish()
    for copy in pending:
        copy.wait_send()


def block_backward(
    block_input, windows, gains, merge_gain, cells_back, wholes, saved, cell_rows, text, visual_terms
):
    rows, width = block_input.shape
    units = saved[5].shape[1]

    def low_buffer(*shape):
        return pltpu.VMEM(shape, jnp.bfloat16)

    def wide_buffer(*shape):
        return pltpu.VMEM(shape, jnp.float32)

    sizes = ((3, 320), (1, 320), (1, units), (1, units), (1, units))
    scratch = [low_buffer(*whole.shape) for whole in wholes]
    scratch += [pltpu.SemaphoreType.DMA((4,)), low_buffer(8, 64, 2048)]
    scratch += [low_buffer(64, 2048), low_buffer(rows, STEP), pltpu.SemaphoreType.DMA((3,))]
    scratch += sum_buffers() + sum_buffers()
    scratch += [low_buffer(planes, 4, 320, columns) for planes, columns in sizes]
    for planes, columns in sizes:
        scratch += [
            low_buffer(2, planes, A_ROWS, columns),
            low_buffer(2, planes, A_HALF, columns),
            low_buffer(planes, A_ROWS, columns),
            low_buffer(3, planes, A_PART, columns),
            low_buffer(2, planes, 4, B_PART, columns),
            low_buffer(2, planes, 4, B_HALF, columns),
            low_buffer(planes, 4, B_PART, columns),
            low_buffer(3, planes, B_PART, columns),
            low_buffer(planes, E_ROWS, columns),
            low_buffer(planes, E_ROWS, columns),
        ]
    scratch += [
        low_buffer(rows, width),
        low_buffer(2, rows, units),
        low_buffer(3, rows, 320),
        wide_buffer(8, width),
        wide_buffer(7, 8, width),
        wide_buffer(2, 8, width),
    ]
    for size in (30, 30, 15, 15, 5, 20, 3 * CHUNKS, 3 * CHUNKS, 7, 8, 1):
        scratch += sem_pair(size)
    operands = [
        block_input,
        windows,
        gains,
        merge_gain,
        cells_back,
        *wholes,
        *saved,
        cell_rows,
        text,
        visual_terms,
    ]
    outs = (
        [jax.ShapeDtypeStruct(text.shape, jnp.bfloat16)]
        + [jax.ShapeDtypeStruct((rows, width), jnp.float32)]
        + [
            jax.ShapeDtypeStruct(dims, jnp.float32)
            for dims in ((3, 320, 320), (1, 320, 320), (320, 2, units), (1, 320, units))
        ]
        + [jax.ShapeDtypeStruct((2, width), jnp.float32)]
    )
    results = pl.pallas_call(
        backward_kernel,
        out_shape=outs,
        in_specs=[VMEM] * 5 + [ANY] * 4 + [VMEM] * (len(operands) - 11) + [ANY] * 2,
        out_specs=[ANY] + [VMEM] * (len(outs) - 1),
        scratch_shapes=scratch,
        compiler_params=pltpu.CompilerParams(
            collective_id=3, has_side_effects=True, vmem_limit_bytes=VMEM_LIMIT
        ),
        name="block_backward",
    )(*operands)

    return results[0], results[1], results[2:6], results[6]


def planes_of(weight):
    return jnp.transpose(weight, (1, 0, 2))


def local(
    block_input,
    windows,
    cell_rows,
    text_vectors,
    sequence_cotangent,
    norm_gains,
    merge_gain,
    triple_weight,
    output_weight,
    gate_up_weight,
    down_weight,
    merge_up,
    merge_down,
):
    patches = block_input[0]
    shards = (
        planes_of(triple_weight),
        output_weight[None],
        planes_of(gate_up_weight),
        down_weight[None],
    )
    wholes, saved, backs = block_forward(
        patches,
        windows,
        norm_gains,
        merge_gain,
        cell_rows,
        sequence_cotangent[0],
        shards,
    )
    visual_terms, cells_back = merger(
        saved[-1],
        backs,
        merge_up.T,
        merge_down,
    )
    sequence, input_gradient, gradients, gain_gradient = block_backward(
        patches,
        windows,
        norm_gains,
        merge_gain,
        cells_back,
        wholes,
        saved[:-1],
        cell_rows,
        text_vectors[0],
        visual_terms,
    )
    return (
        sequence[None],
        input_gradient[None],
        planes_of(gradients[0]),
        gradients[1][0],
        gradients[2],
        gradients[3][0],
        gain_gradient,
    )


def solution(mesh):
    placed = (
        P(("dp", "section"), None, None),
        P(("dp", "section"), None),
        P("section", "dp"),
        P("section", "dp", "mp"),
        P("section", "dp", "mp"),
        P(),
        P(),
        P("section", None, "mp"),
        P("section", "mp"),
        P("section", None, "mp"),
        P("section", "mp"),
        P(None, ("section", "mp")),
        P(("section", "mp"), None),
    )
    return jax.shard_map(
        local,
        mesh=mesh,
        in_specs=placed,
        out_specs=(
            P("section", "dp", "mp"),
            P(("dp", "section"), None, None),
            P("section", None, "mp"),
            P("section", "mp"),
            P("section", None, "mp"),
            P("section", "mp"),
            P(),
        ),
        check_vma=False,
    )
```
